128 devices in a mesh: grp: 2 (over y_lo), seq: 16 (over z, y_hi, core), tile: 4 (over x).
Axes of the slice: x: 4, y: 4 (y_hi: 2, y_lo: 2; y = y_hi * 2 + y_lo), z: 4, core: 2. Of those that a mesh axis runs over, the one named last changes fastest.
Arguments:
- tokens: bfloat16 [2, 64, 128, 2432], P('grp', 'seq'), may hold values from -6 to 6
- shift: float32 [2, 2432], P('grp'), may hold values from -3 to 3
- scale: float32 [2, 2432], P('grp'), may hold values from -3 to 3
- gate: float32 [2, 2432], P('grp'), may hold values from -4 to 4
- fc1: bfloat16 [2432, 5120], P(('grp', 'seq'), 'tile'), may hold values from -0.125 to 0.125
- fc2: bfloat16 [5120, 2432], P('tile', ('grp', 'seq')), may hold values from -0.078125 to 0.078125
- proj: bfloat16 [2432, 64], replicated, may hold values from -0.125 to 0.125
- lift: bfloat16 [16, 256], replicated, may hold values from -1.5 to 1.5
- conv_a: bfloat16 [3, 3, 256, 256], replicated, may hold values from -0.125 to 0.125
- conv_b: bfloat16 [3, 3, 256, 256], replicated, may hold values from -0.125 to 0.125
- target: bfloat16 [2, 256, 512, 256], P('grp', 'seq', 'tile'), may hold values from -6 to 6
Outputs:
- grad_fc1: float32 [2432, 5120], P(('grp', 'seq'), 'tile')
- grad_fc2: float32 [5120, 2432], P('tile', ('grp', 'seq'))
- latent_grad: float32 [2, 64, 128, 64], P('grp', 'seq', 'tile')
The draws below stay inside these ranges and needn't reach their ends.
All inputs are finite; a program needn't handle non-finite values.
Results may differ from the reference program's by a relative error of at most 0.02.
Values may be sent and summed in bfloat16 or wider, within the bound.
A program may use at most 128 MiB of HBM per device.

```python
import jax
import jax.numpy as jnp
from jax import lax

D = 2432
FF = 5120
CH = 256
LAT = 16
PATCH = 64
TOKEN_COLS = 128
IMAGES = 2
TOKEN_ROWS = 64
N_SEQ = 16


def shard_levels(rng, shape, pieces, low, top_value):
    def one(position, shards_of):
        draws = jax.random.uniform(jax.random.fold_in(jax.random.fold_in(rng, 6), position), (shards_of,), jnp.float32, low / len(pieces), top_value / len(pieces))
        return jnp.repeat(jnp.exp(draws), shape[position] // shards_of).reshape((-1,) + (1,) * (len(shape) - position - 1))

    factor_of = one(*pieces[0])
    for cut in pieces[1:]:
        factor_of = factor_of * one(*cut)
    return factor_of


def centred(key, dims, scale, limit, split=(), kind=jnp.bfloat16):
    result = jax.random.normal(key, dims, jnp.float32) * scale
    if len(split) > 0:
        result = shard_levels(key, dims, split, -0.22, 0.18) * result
    return jnp.clip(result, min=-limit, max=limit).astype(kind)


def setup_inputs(seed: int = 0) -> dict:
    arg_keys = jax.random.split(jax.random.key(seed), 12)
    return {
        "tokens": centred(arg_keys[0], (IMAGES, TOKEN_ROWS, TOKEN_COLS, D), 1.0, 6.0, ((0, 2), (1, 16))),
        "shift": centred(arg_keys[1], (IMAGES, D), 0.5, 3.0, ((0, 2),), jnp.float32),
        "scale": centred(arg_keys[2], (IMAGES, D), 0.5, 3.0, ((0, 2),), jnp.float32),
        "gate": centred(arg_keys[3], (IMAGES, D), 1.0, 4.0, ((0, 2),), jnp.float32),
        "fc1": centred(arg_keys[4], (D, FF), D ** -0.5, 0.125, ((0, 32), (1, 4))),
        "fc2": centred(arg_keys[5], (FF, D), FF ** -0.5, 0.078125, ((0, 4), (1, 32))),
        "proj": centred(arg_keys[6], (D, PATCH), D ** -0.5, 0.125),
        "lift": centred(arg_keys[7], (LAT, CH), LAT ** -0.5, 1.5),
        "conv_a": centred(arg_keys[8], (3, 3, CH, CH), (9 * CH) ** -0.5, 0.125),
        "conv_b": centred(arg_keys[9], (3, 3, CH, CH), (9 * CH) ** -0.5, 0.125),
        "target": centred(arg_keys[10], (IMAGES, 4 * TOKEN_ROWS, 4 * TOKEN_COLS, CH), 1.0, 6.0, ((0, 2), (1, 16), (2, 4))),
    }


def gelu_tanh(value):
    return jax.nn.gelu(value, approximate=True)

def conv_tile(padded, kernel):
    height = padded.shape[0] - 2
    width = padded.shape[1] - 2
    total = jnp.zeros((height, width, kernel.shape[3]), jnp.float32)
    for row_off in range(3):
        for col_off in range(3):
            window = padded[row_off:row_off + height, col_off:col_off + width]
            total = total + jnp.dot(window, kernel[row_off, col_off], preferred_element_type=jnp.float32)
    return total

def flipped(kernel):
    return jnp.swapaxes(kernel[::-1, ::-1], 2, 3)

def pad_image(value):
    return jnp.pad(value, ((1, 1), (1, 1), (0, 0)))

def unpatch(patch):
    rows, cols = (patch.shape[0], patch.shape[1])
    return patch.reshape(rows, cols, 2, 2, -1).transpose(0, 2, 1, 3, 4).reshape(2 * rows, 2 * cols, -1)

def repatch(latent):
    rows, cols = (latent.shape[0] // 2, latent.shape[1] // 2)
    return latent.reshape(rows, 2, cols, 2, -1).transpose(0, 2, 1, 3, 4).reshape(rows, cols, -1)

def reference(tokens, shift, scale, gate, fc1, fc2, proj, lift, conv_a, conv_b, target):
    images, tok_rows, tok_cols, width = tokens.shape
    proj_full = proj.astype(jnp.float32)
    lift_full = lift.astype(jnp.float32)
    block_rows = tok_rows // N_SEQ * tok_cols
    grad_one = jnp.zeros(fc1.shape, jnp.float32)
    grad_two = jnp.zeros(fc2.shape, jnp.float32)
    latent_list = []
    for image in range(images):
        rows_x = tokens[image].reshape(-1, width)
        xfull = rows_x.astype(jnp.float32)
        center = xfull - lax.optimization_barrier(jnp.mean(xfull, axis=1, keepdims=True))
        spread = lax.optimization_barrier(jnp.mean(center * center, axis=1, keepdims=True))
        normed = (center * lax.rsqrt(spread + 1e-06) * (1.0 + scale[image]) + shift[image]).astype(jnp.bfloat16)
        pre = jnp.dot(normed, fc1, preferred_element_type=jnp.float32)
        act = gelu_tanh(pre).astype(jnp.bfloat16)
        mlp = jnp.dot(act, fc2, preferred_element_type=jnp.float32)
        patch = jnp.dot(rows_x, proj, preferred_element_type=jnp.float32) + jnp.dot(gate[image] * mlp, proj_full, precision=lax.Precision.HIGHEST)
        latent = unpatch(patch.reshape(tok_rows, tok_cols, -1)).astype(jnp.bfloat16)
        lifted = jnp.dot(latent, lift, preferred_element_type=jnp.float32).astype(jnp.bfloat16)
        upsampled = jnp.repeat(jnp.repeat(lifted, 2, axis=0), 2, axis=1)
        first = conv_tile(pad_image(upsampled), conv_a)
        smooth = jax.nn.silu(first).astype(jnp.bfloat16)
        decoded = conv_tile(pad_image(smooth), conv_b)
        grad_decoded = (decoded - target[image].astype(jnp.float32)).astype(jnp.bfloat16)
        grad_smooth = conv_tile(pad_image(grad_decoded), flipped(conv_b))
        sigma = jax.nn.sigmoid(first)
        grad_first = (grad_smooth * sigma * (1.0 + first * (1.0 - sigma))).astype(jnp.bfloat16)
        grad_up = conv_tile(pad_image(grad_first), flipped(conv_a))
        height, breadth = (grad_up.shape[0] // 2, grad_up.shape[1] // 2)
        grad_lifted = grad_up.reshape(height, 2, breadth, 2, -1).sum(axis=(1, 3))
        grad_latent = jnp.dot(grad_lifted, lift_full.T, precision=lax.Precision.HIGHEST)
        latent_grad = repatch(grad_latent)
        latent_list.append(latent_grad)
        grad_mlp = (jnp.dot(latent_grad.reshape(-1, latent_grad.shape[-1]), proj_full.T, precision=lax.Precision.HIGHEST) * gate[image]).astype(jnp.bfloat16)
        grad_act = jnp.dot(grad_mlp, fc2.T, preferred_element_type=jnp.float32)
        grad_pre = jax.vjp(gelu_tanh, pre)[1](grad_act)[0].astype(jnp.bfloat16)
        for block in range(N_SEQ):
            lo = block * block_rows
            term_one = jnp.dot(normed[lo:lo + block_rows].T, grad_pre[lo:lo + block_rows], preferred_element_type=jnp.float32)
            term_two = jnp.dot(act[lo:lo + block_rows].T, grad_mlp[lo:lo + block_rows], preferred_element_type=jnp.float32)
            grad_one = grad_one + term_one.astype(jnp.bfloat16).astype(jnp.float32)
            grad_two = grad_two + term_two.astype(jnp.bfloat16).astype(jnp.float32)
    return (grad_one, grad_two, jnp.stack(latent_list))
```

```python
import jax
import jax.numpy as jnp
from jax import lax
from jax.experimental import pallas as pl
from jax.experimental.pallas import tpu as pltpu
from jax.sharding import PartitionSpec as P

F32 = jnp.float32
BF16 = jnp.bfloat16


def gelu_tanh(value):
    return jax.nn.gelu(value, approximate=True)


def split(value):
    high = value.astype(BF16)
    return high, (value - high.astype(F32)).astype(BF16)


MESH = pl.DeviceIdType.MESH
VMEM = pltpu.VMEM


def place():
    grp, seq, tile = lax.axis_index("grp"), lax.axis_index("seq"), lax.axis_index("tile")
    core = seq % 2
    y = (seq // 2) % 2 * 2 + grp
    z = seq // 4

    def device(y, z, core):
        return (y % 2, z * 4 + y // 2 * 2 + core, tile)

    return y, z, core, device


def oriented(y, z, core):
    a = y + core * (z - y)
    b = z + core * (y - z)

    def turn(a, b):
        return a + core * (b - a), b + core * (a - b)

    return a, b, turn


def block_of(y, z):
    return y % 2 * 8 + z * 2 + y // 2


def greet(peers):
    barrier = pltpu.get_barrier_semaphore()
    for peer in peers:
        pl.semaphore_signal(barrier, inc=1, device_id=peer, device_id_type=MESH)
    pl.semaphore_wait(barrier, len(peers))


def plane_peers(y, z, core, device):
    return (
        [device(y, z, 1 - core)]
        + [device((y + d) % 4, z, core) for d in range(1, 4)]
        + [device(y, (z + d) % 4, core) for d in range(1, 4)]
    )


def tile_peer(ds, dt):
    grp, seq, tile = lax.axis_index("grp"), lax.axis_index("seq"), lax.axis_index("tile")
    return (grp, (seq + ds) % 16, (tile + dt) % 4)


AROUND = [(0, 1), (0, 2), (0, 3)] + [(ds, dt) for ds in (-1, 1) for dt in range(4)]
NEXT = [(1, 0), (-1, 0), (0, 1), (0, -1), (1, 1), (1, -1), (-1, 1), (-1, -1)]
EDGE = 8
LEAD = 16


class Courier:
    def __init__(self, send, recv):
        self.send, self.recv, self.used, self.started = send, recv, 0, []

    def slot(self):
        self.used += 1
        return self.used - 1

    def copy(self, slot, src, dst, peer):
        return pltpu.make_async_remote_copy(
            src_ref=src,
            dst_ref=dst,
            send_sem=self.send.at[slot],
            recv_sem=self.recv.at[slot],
            device_id=peer,
            device_id_type=MESH,
        )

    def start(self, slot, src, dst, peer):
        copy = self.copy(slot, src, dst, peer)
        copy.start()
        self.started.append(copy)

    def arrived(self, slot, dst, peer):
        self.copy(slot, dst, dst, peer).wait_recv()

    def finish(self):
        for copy in self.started:
            copy.wait_send()


def forward_kernel(
    nrm, nrmt, fc1, fc2, gps, target, pre, act, part, fold, gboth, sibt, t_rows, t_cols, t_ends,
    gath, gin, wpart, wsib, wsum, wz_out, wz_in, wy_out, wy_in, wfull, send, recv,
):
    y, z, core, device = place()
    a, b, turn = oriented(y, z, core)
    grp = lax.axis_index("grp")
    other = 1 - core
    sibling = device(y, z, other)
    greet(plane_peers(y, z, core, device) + [tile_peer(ds, dt) for ds, dt in NEXT])
    mail = Courier(send, recv)
    rows, half = gath.shape[2] // 2, gath.shape[3]

    def peer(da, db):
        return device(*turn((a + da) % 4, (b + db) % 4), core)

    def block(da, db):
        return block_of(*turn((a + da) % 4, (b + db) % 4))

    own = block(0, 0)
    mine = pl.ds(pl.multiple_of(core * rows, 16), rows)
    theirs = pl.ds(pl.multiple_of(other * rows, 16), rows)
    for h in range(2):
        gath[h, own, mine, :] = fc1[:, h * half : (h + 1) * half]
    s_for, s_rest = mail.slot(), mail.slot()
    mail.start(s_for, gath.at[other, own, mine], gath.at[other, own, mine], sibling)
    mail.start(s_rest, gath.at[core, own, mine], gath.at[core, own, mine], sibling)
    s_nrm = mail.slot()
    mail.start(s_nrm, nrmt, sibt, sibling)
    partner = device(y // 2 * 2 + 1 - grp, z, core)
    s_gate = mail.slot()
    mail.start(s_gate, gps.at[1], gin, partner)

    top, bottom = pl.ds(0, rows), pl.ds(rows, rows)

    def held(da, db, where=None):
        ref = gath.at[core, block(da, db)]
        return ref if where is None else ref.at[where]

    def put(slot, da, db, to, where=None):
        mail.start(slot, held(da, db, where), held(da, db, where), peer(*to))

    def take(slot, da, db, frm, where=None):
        mail.arrived(slot, held(da, db, where), peer(*frm))

    def share(slot, da, db):
        mail.start(slot, held(da, db), held(da, db), sibling)

    def other_block(da, db):
        return gath.at[other, block(da, db)]

    def multiply(h, da, db, first=False):
        at = block(da, db)
        term = jnp.dot(nrm[at], gath[h, at], preferred_element_type=F32)
        pre[h] = term if first else pre[h] + term

    height, breadth = target.shape[0], target.shape[1]
    top_rows, end_rows = pl.ds(0, 2), pl.ds(height - 2, 2)
    lead, trail = pl.ds(0, LEAD), pl.ds(breadth - LEAD, LEAD)
    borders = {
        (1, 0): (target.at[end_rows], t_rows.at[0]),
        (-1, 0): (target.at[top_rows], t_rows.at[1]),
        (0, 1): (target.at[:, trail], t_cols.at[0]),
        (0, -1): (target.at[:, lead], t_cols.at[1]),
        (1, 1): (target.at[end_rows, trail], t_ends.at[0]),
        (1, -1): (target.at[end_rows, lead], t_ends.at[1]),
        (-1, 1): (target.at[top_rows, trail], t_ends.at[2]),
        (-1, -1): (target.at[top_rows, lead], t_ends.at[3]),
    }
    s_border = {to: mail.slot() for to in NEXT}
    for to in NEXT:
        mail.start(s_border[to], *borders[to], tile_peer(*to))

    A_UP, A_DOWN, A_UP2, A_DOWN2 = (mail.slot() for _ in range(4))
    sh = {}
    for da in range(4):
        for db in range(4):
            if (da, db) != (0, 0):
                sh[da, db] = mail.slot()
    bs = {(da, k): mail.slot() for da in range(4) for k in range(4)}

    mail.arrived(s_for, gath.at[core, own, theirs], sibling)
    put(A_UP, 0, 0, (1, 0))
    put(A_DOWN, 0, 0, (-1, 0))
    put(bs[0, 0], 0, 0, (0, 1))
    put(bs[0, 1], 0, 0, (0, -1))

    mail.arrived(s_gate, gin, partner)
    both = gps[0] + gin[...]
    gboth[...] = both
    high, low = split(both)
    wpart[...] = jnp.dot(fc2[...], high, preferred_element_type=F32) + jnp.dot(
        fc2[...], low, preferred_element_type=F32
    )
    wh = wpart.shape[0] // 2
    wq = wh // 4
    s_w = mail.slot()
    mail.start(s_w, wpart.at[pl.ds(pl.multiple_of(other * wh, 16), wh)], wsib, sibling)

    multiply(core, 0, 0, first=True)
    mail.arrived(s_rest, gath.at[other, own, theirs], sibling)
    multiply(other, 0, 0, first=True)

    take(A_UP, -1, 0, (-1, 0))
    put(A_UP2, -1, 0, (1, 0), top)
    take(A_DOWN, 1, 0, (1, 0))
    put(A_DOWN2, 1, 0, (-1, 0), bottom)
    for da in (3, 1):
        put(bs[da, 0], da, 0, (0, 1))
        put(bs[da, 1], da, 0, (0, -1))
        share(sh[da, 0], da, 0)

    mail.arrived(s_w, wsib, sibling)
    wsum[...] = wpart[pl.ds(pl.multiple_of(core * wh, 16), wh), :] + wsib[...]
    wz_out[...] = wsum[...].astype(BF16)
    s_wz = [mail.slot() for _ in range(3)]
    for d in range(1, 4):
        to = (z + d) % 4
        src = wz_out.at[pl.ds(pl.multiple_of(to * wq, 16), wq)]
        mail.start(s_wz[d - 1], src, wz_in.at[d - 1], device(y, to, core))

    multiply(core, -1, 0)
    multiply(core, 1, 0)

    def from_b(da):
        take(bs[da, 0], da, -1, (0, -1))
        put(bs[da, 2], da, -1, (0, 1), top)
        share(sh[da, 3], da, -1)
        take(bs[da, 1], da, 1, (0, 1))
        put(bs[da, 3], da, 1, (0, -1), bottom)
        share(sh[da, 1], da, 1)

    def from_b2(da):
        take(bs[da, 2], da, 2, (0, -1), top)
        take(bs[da, 3], da, 2, (0, 1), bottom)
        share(sh[da, 2], da, 2)

    def from_sibling(da, db):
        mail.arrived(sh[da, db], other_block(db, da), sibling)
        multiply(other, db, da)

    from_b(0)
    take(A_UP2, 2, 0, (-1, 0), top)
    take(A_DOWN2, 2, 0, (1, 0), bottom)
    put(bs[2, 0], 2, 0, (0, 1))
    put(bs[2, 1], 2, 0, (0, -1))
    share(sh[2, 0], 2, 0)

    for d in range(1, 4):
        mail.arrived(s_wz[d - 1], wz_in.at[d - 1], device(y, (z + 4 - d) % 4, core))
    here = pl.ds(pl.multiple_of(z * wq, 16), wq)
    total = wsum[here, :]
    for d in range(3):
        total = total + wz_in[d].astype(F32)
    wy_out[...] = total.astype(BF16)
    s_wy = [mail.slot() for _ in range(3)]
    for d in range(1, 4):
        mail.start(s_wy[d - 1], wy_out, wy_in.at[d - 1], device((y + d) % 4, z, core))

    multiply(core, 0, -1)
    multiply(core, 0, 1)
    multiply(core, 2, 0)
    from_b2(0)
    multiply(core, 0, 2)
    from_b(3)
    for d in range(1, 4):
        mail.arrived(s_wy[d - 1], wy_in.at[d - 1], device((y + 4 - d) % 4, z, core))
    for d in range(3):
        total = total + wy_in[d].astype(F32)
    where_w = pl.ds(pl.multiple_of(core * wh + z * wq, 16), wq)
    wfull[where_w, :] = total.astype(BF16)
    s_wa = [mail.slot() for _ in range(3)]
    for d in range(1, 4):
        mail.start(
            s_wa[d - 1], wfull.at[where_w], wfull.at[where_w], device(y, (z + d) % 4, core)
        )
    from_sibling(3, 0)
    from_sibling(1, 0)
    multiply(core, 3, -1)
    multiply(core, 3, 1)
    from_b2(3)
    from_b(1)
    from_sibling(0, 3)
    from_sibling(0, 1)
    from_sibling(2, 0)
    multiply(core, 3, 2)
    multiply(core, 1, -1)
    multiply(core, 1, 1)
    from_b2(1)
    for d in range(1, 4):
        frm = (z + 4 - d) % 4
        at = pl.ds(pl.multiple_of(core * wh + frm * wq, 16), wq)
        mail.arrived(s_wa[d - 1], wfull.at[at], device(y, frm, core))
    s_ws = mail.slot()
    at = pl.ds(pl.multiple_of(core * wh, 16), wh)
    mail.start(s_ws, wfull.at[at], wfull.at[at], sibling)
    from_b(2)
    from_sibling(0, 2)
    from_sibling(3, 3)
    from_sibling(3, 1)
    multiply(core, 1, 2)
    multiply(core, 2, -1)
    multiply(core, 2, 1)
    from_b2(2)
    from_sibling(3, 2)
    from_sibling(1, 3)
    from_sibling(1, 1)
    from_sibling(1, 2)
    multiply(core, 2, 2)
    from_sibling(2, 3)
    from_sibling(2, 1)
    from_sibling(2, 2)

    mail.arrived(s_ws, wfull.at[pl.ds(pl.multiple_of(other * wh, 16), wh)], sibling)
    width = part.shape[1]
    fold[...] = jnp.where(grp == 0, wfull[:, :width], wfull[:, width:])
    total = jnp.zeros(part.shape, F32)
    for h in range(2):
        a_h = gelu_tanh(pre[h]).astype(BF16)
        act[h] = a_h
        total = total + jnp.dot(
            a_h, fold[h * half : (h + 1) * half], preferred_element_type=F32
        )
    part[...] = total
    mail.arrived(s_nrm, sibt, sibling)
    for ds, dt in NEXT:
        mail.arrived(s_border[ds, dt], borders[ds, dt][1], tile_peer(-ds, -dt))
    mail.finish()


def forward(nrm, nrmt, fc1, fc2, gps, target):
    n_blk, rows, depth = nrm.shape
    hidden = fc2.shape[0]
    half = hidden // 2
    width = gps.shape[2] // 2
    vmem, hbm = pl.BlockSpec(memory_space=VMEM), pl.BlockSpec(memory_space=pl.ANY)
    shape = jax.ShapeDtypeStruct
    return pl.pallas_call(
        forward_kernel,
        out_shape=(
            shape((2, rows, half), F32),
            shape((2, rows, half), BF16),
            shape((rows, width), F32),
            shape((hidden, width), BF16),
            shape(gps.shape[1:], F32),
            shape(nrmt.shape, BF16),
            shape((2, 2) + target.shape[1:], BF16),
            shape((2, target.shape[0], LEAD, target.shape[2]), BF16),
            shape((4, 2, LEAD, target.shape[2]), BF16),
        ),
        in_specs=[vmem, hbm, vmem, vmem, vmem, hbm],
        out_specs=(vmem,) * 5 + (hbm,) * 4,
        scratch_shapes=[
            VMEM((2, n_blk, depth, half), BF16),
            VMEM(gps.shape[1:], F32),
            VMEM((hidden, 2 * width), F32),
            VMEM((half, 2 * width), F32),
            VMEM((half, 2 * width), F32),
            VMEM((half, 2 * width), BF16),
            VMEM((3, half // 4, 2 * width), BF16),
            VMEM((half // 4, 2 * width), BF16),
            VMEM((3, half // 4, 2 * width), BF16),
            VMEM((hidden, 2 * width), BF16),
            pltpu.SemaphoreType.DMA((64,)),
            pltpu.SemaphoreType.DMA((64,)),
        ],
        compiler_params=pltpu.CompilerParams(
            collective_id=1, has_side_effects=True, vmem_limit_bytes=56 * 2**20
        ),
    )(nrm, nrmt, fc1, fc2, gps, target)


def pixel_kernels(lift, conv_a):
    lifted = {
        (o, e): jnp.dot(lift, conv_a[3 * o + e], preferred_element_type=F32)
        for o in range(3)
        for e in range(3)
    }

    def reach(pixel, cell):
        return [o for o in range(3) if (pixel + o - 1) // 2 == cell]

    out = {}
    for r in range(-1, 5):
        for c in range(-1, 5):
            parts = []
            for a in range(2):
                for b in range(2):
                    total = jnp.zeros_like(lifted[0, 0])
                    for o in reach(r, a):
                        for e in reach(c, b):
                            total = total + lifted[o, e]
                    parts.append(total)
            out[r, c] = jnp.concatenate(parts, axis=0)
    return out


def middle_kernel(
    part, xproj, lift, conv_a, conv_b, conv_bt, target, t_rows, t_cols, t_ends,
    latent, lg,
    psrc, main_in, edge_in, patch, kern, f_ref, a_ref, b_ref, acc, want, gf, send, recv,
):
    seq, tile = lax.axis_index("seq"), lax.axis_index("tile")
    greet([tile_peer(ds, dt) for ds, dt in AROUND])
    mail = Courier(send, recv)
    n_rows, n_cols, width = part.shape
    span = main_in.shape[2]
    here = n_cols // 4
    pairs, ch = a_ref.shape[1], a_ref.shape[2] // 4

    psrc[...] = jnp.zeros_like(psrc)
    psrc[:, EDGE : EDGE + n_cols, :] = part[...]
    cols = pl.ds(pl.multiple_of(EDGE + tile * here, 8), here)
    psrc[:, cols, :] = psrc[:, cols, :] + xproj[...]

    def window(dt):
        return pl.ds(pl.multiple_of((tile + dt) % 4 * here, 8), span)

    slots = {}
    for ds, dt in AROUND:
        slots[ds, dt] = mail.slot()
        if ds == 0:
            src, dst = psrc.at[:, window(dt)], main_in.at[dt]
        elif ds == -1:
            src, dst = psrc.at[pl.ds(0, 1), window(dt)], edge_in.at[1, dt]
        else:
            src, dst = psrc.at[pl.ds(n_rows - 1, 1), window(dt)], edge_in.at[0, dt]
        mail.start(slots[ds, dt], src, dst, tile_peer(ds, dt))

    kernels = pixel_kernels(lift[...], conv_a)
    for r in range(-1, 5):
        for c in range(-1, 5):
            kern[6 * (r + 1) + c + 1] = kernels[r, c].astype(BF16)
    height, breadth = target.shape[0], target.shape[1]
    body, lead = slice(LEAD, LEAD + breadth), slice(0, LEAD)
    trail = slice(LEAD + breadth, 2 * LEAD + breadth)
    mid = slice(2, 2 + height)

    def want_at(rows, at, value):
        value = value.astype(F32)
        want[rows, 0, at, :] = value[:, :, :128]
        want[rows, 1, at, :] = value[:, :, 128:]

    want_at(mid, body, target[...])
    want_at(slice(0, 2), body, t_rows[0])
    want_at(slice(2 + height, 4 + height), body, t_rows[1])
    for side, at in ((0, lead), (1, trail)):
        want_at(mid, at, t_cols[side])
        want_at(slice(0, 2), at, t_ends[side])
        want_at(slice(2 + height, 4 + height), at, t_ends[2 + side])

    total = psrc[:, window(0), :]
    for dt in range(1, 4):
        mail.arrived(slots[0, dt], main_in.at[dt], tile_peer(0, -dt))
        total = total + main_in[dt]
    rows = {i + 1: total[i] for i in range(n_rows)}
    for i, ds in ((0, 1), (1, -1)):
        total = jnp.zeros(edge_in.shape[3:], F32)
        for dt in range(4):
            mail.arrived(slots[ds, dt], edge_in.at[i, dt], tile_peer(-ds, -dt))
            total = total + edge_in[i, dt, 0]
        outside = (seq == 0) if i == 0 else (seq == 15)
        rows[0 if i == 0 else n_rows + 1] = jnp.where(outside, 0.0, total)
    n_tok = n_rows + 2
    for r in range(n_tok):
        patch[0, r + 1] = pltpu.roll(rows[r], 1, 0).astype(BF16)
        patch[1, r + 1] = rows[r].astype(BF16)
        patch[2, r + 1] = pltpu.roll(rows[r], span - 1, 0).astype(BF16)
    for k in range(3):
        patch[k, 0] = jnp.zeros((span, width), BF16)
        patch[k, n_tok + 1] = jnp.zeros((span, width), BF16)

    def near(phase):
        return [(d, phase - 4 * d) for d in (-1, 0, 1) if -1 <= phase - 4 * d <= 4]

    for al in range(4):
        for ph in range(4):
            value = None
            for dr, r in near(al):
                for dc, c in near(ph):
                    lhs = patch[1 + dc, 1 + dr : 1 + dr + n_tok].reshape(n_tok * span, width)
                    term = jnp.dot(
                        lhs, kern[6 * (r + 1) + c + 1], preferred_element_type=F32
                    )
                    value = term if value is None else value + term
            value = value.reshape(n_tok, span, ch)
            for tr in range(n_tok):
                at = pl.ds(ph // 2, span, stride=2)
                f_ref[4 * tr + al, ph % 2, 0, at, :] = value[tr, :, :128]
                f_ref[4 * tr + al, ph % 2, 1, at, :] = value[tr, :, 128:]

    def inside(row, b):
        r = seq * height + row
        c = 2 * (tile * breadth // 2 + lax.broadcasted_iota(jnp.int32, (pairs, 1), 0) - EDGE) + b
        return (r >= 0) & (r < 16 * height) & (c >= 0) & (c < 4 * breadth)

    def both(ref, at, rows):
        return jnp.concatenate([ref[*at, 0, rows, :], ref[*at, 1, rows, :]], axis=1)

    def spread(ref, at, v0, v1):
        ref[at, :, 0:ch] = pltpu.roll(v1, 1, 0).astype(BF16)
        ref[at, :, ch : 2 * ch] = v0.astype(BF16)
        ref[at, :, 2 * ch : 3 * ch] = v1.astype(BF16)
        ref[at, :, 3 * ch :] = pltpu.roll(v0, pairs - 1, 0).astype(BF16)

    @pl.loop(0, height + 6)
    def _(i):
        smooth = []
        for b in range(2):
            f = both(f_ref, (i + 1, b), slice(EDGE, EDGE + pairs))
            sigma = jax.nn.sigmoid(f)
            smooth.append(jnp.where(inside(i - 3, b), f * sigma, 0.0))
            slope = sigma * (1.0 + f * (1.0 - sigma))
            f_ref[i + 1, b, 0, EDGE : EDGE + pairs, :] = slope[:, :128]
            f_ref[i + 1, b, 1, EDGE : EDGE + pairs, :] = slope[:, 128:]
        spread(a_ref, i, *smooth)

    def conv(src, weights, out_rows, chunk):
        @pl.loop(0, out_rows // chunk)
        def _(i):
            for b in range(2):
                value = None
                for o in range(3):
                    lhs = src[pl.ds(i * chunk + o, chunk), :, b * ch : (b + 3) * ch]
                    term = jnp.dot(
                        lhs.reshape(chunk * pairs, 3 * ch), weights[o],
                        preferred_element_type=F32,
                    )
                    value = term if value is None else value + term
                acc[b, pl.ds(i * chunk, chunk)] = value.reshape(chunk, pairs, ch)

    conv(a_ref, conv_b, height + 4, (height + 4) // 2)

    @pl.loop(0, height + 4)
    def _(i):
        grad = []
        for b in range(2):
            diff = acc[b, i] - both(want, (i,), pl.ds(b, pairs, stride=2))
            grad.append(jnp.where(inside(i - 2, b), diff, 0.0))
        spread(b_ref, i, *grad)

    conv(b_ref, conv_bt, height + 2, (height + 2) // 2)

    @pl.loop(0, height + 2)
    def _(i):
        for b in range(2):
            value = acc[b, i] * both(f_ref, (i + 3, b), slice(EDGE, EDGE + pairs))
            value = jnp.where(inside(i - 1, b), value, 0.0)
            gf[i, b, 0], gf[i, b, 1] = value[:, :128], value[:, 128:]

    grad = None
    for r in range(-1, 5):
        for c in range(-1, 5):
            at = pl.ds(EDGE + c // 2, here, stride=2)
            lhs = jnp.concatenate(
                [both(gf, (4 * tr + r + 1, c % 2), at).astype(BF16) for tr in range(n_rows)],
                axis=0,
            )
            term = lax.dot_general(
                lhs, kern[6 * (r + 1) + c + 1], (((1,), (1,)), ((), ())),
                preferred_element_type=F32,
            )
            grad = term if grad is None else grad + term
    grad = grad.reshape(n_rows, here, width)
    latent[...] = grad
    own = pl.ds(pl.multiple_of(tile * here, 16), here)
    lg[:, own, :] = grad.astype(BF16)
    back = [mail.slot() for _ in range(3)]
    for dt in range(1, 4):
        mail.start(back[dt - 1], lg.at[:, own], lg.at[:, own], tile_peer(0, dt))
    for dt in range(1, 4):
        frm = pl.ds(pl.multiple_of((tile + 4 - dt) % 4 * here, 16), here)
        mail.arrived(back[dt - 1], lg.at[:, frm], tile_peer(0, -dt))
    mail.finish()


def middle(part, xproj, lift, conv_a, conv_b, conv_bt, target, t_rows, t_cols, t_ends):
    n_rows, n_cols, width = part.shape
    height, breadth, ch = target.shape
    here, span = n_cols // 4, n_cols // 4 + 2 * EDGE
    pairs = breadth // 2 + 2 * EDGE
    vmem = pl.BlockSpec(memory_space=VMEM)
    shape = jax.ShapeDtypeStruct
    return pl.pallas_call(
        middle_kernel,
        out_shape=(
            shape((n_rows, here, width), F32),
            shape((n_rows, n_cols, width), BF16),
        ),
        in_specs=[vmem] * 10,
        out_specs=(vmem,) * 2,
        scratch_shapes=[
            VMEM((n_rows, n_cols + 2 * EDGE, width), F32),
            VMEM((4, n_rows, span, width), F32),
            VMEM((2, 4, 1, span, width), F32),
            VMEM((3, n_rows + 4, span, width), BF16),
            VMEM((36, width, ch), BF16),
            VMEM((height + 8, 2, 2, 2 * span, ch // 2), F32),
            VMEM((height + 6, pairs, 4 * ch), BF16),
            VMEM((height + 4, pairs, 4 * ch), BF16),
            VMEM((2, height + 4, pairs, ch), F32),
            VMEM((height + 4, 2, breadth + 2 * LEAD, ch // 2), F32),
            VMEM((height + 2, 2, 2, pairs, ch // 2), F32),
            pltpu.SemaphoreType.DMA((16,)),
            pltpu.SemaphoreType.DMA((16,)),
        ],
        compiler_params=pltpu.CompilerParams(
            collective_id=3, has_side_effects=True, vmem_limit_bytes=56 * 2**20
        ),
    )(part, xproj, lift, conv_a, conv_b, conv_bt, target, t_rows, t_cols, t_ends)


def gelu_slope(x):
    k = 0.7978845608028654
    t = jnp.tanh(k * (x + 0.044715 * x * x * x))
    return 0.5 * (1.0 + t) + 0.5 * x * (1.0 - t * t) * (k + 3 * 0.044715 * k * x * x)


def backward_kernel(
    nrmt, sibt, pre, act, fold, lg, out, sfull,
    gpre, gsib, st, ssib, ssum, sz_in, sy_out, sy_in,
    far_out, up_out, down_out, half_in, full_in, reduced, fin, send, recv,
):
    y, z, core, device = place()
    a, b, turn = oriented(y, z, core)
    grp = lax.axis_index("grp")
    other = 1 - core
    sibling = device(y, z, other)
    greet(plane_peers(y, z, core, device))
    mail = Courier(send, recv)
    depth, half = gpre.shape[1], gpre.shape[2]
    rows = nrmt.shape[1] // 2
    top, bottom = pl.ds(0, rows), pl.ds(rows, rows)

    def peer(da, db):
        return device(*turn((a + da) % 4, (b + db) % 4), core)

    def block(da, db):
        return block_of(*turn((a + da) % 4, (b + db) % 4))

    def pre_grad(h):
        weights = fold[pl.ds(pl.multiple_of(h * half, 16), half), :]
        grad_act = lax.dot_general(
            lg[...], weights, (((1,), (1,)), ((), ())), preferred_element_type=F32
        )
        gpre[h] = (grad_act * gelu_slope(pre[h])).astype(BF16)

    s_g = mail.slot()
    pre_grad(other)
    mail.start(s_g, gpre.at[other], gsib, sibling)
    pre_grad(core)
    for h in range(2):
        st[:, h * half : (h + 1) * half] = lax.dot_general(
            lg[...], act[h], (((0,), (0,)), ((), ())), preferred_element_type=F32
        )
    sr = st.shape[0] // 2
    sq = sr // 4
    s_s = mail.slot()
    mail.start(s_s, st.at[pl.ds(pl.multiple_of(other * sr, 8), sr)], ssib, sibling)

    mail.arrived(s_g, gsib, sibling)

    def term(da, db):
        at = block(da, db)
        return jnp.dot(nrmt[at], gpre[core], preferred_element_type=F32) + jnp.dot(
            sibt[at], gsib[...], preferred_element_type=F32
        )

    def far(i, value, to):
        s = [mail.slot() for _ in range(2)]
        far_out[i] = value.astype(BF16)
        mail.start(s[0], far_out.at[i, top], half_in.at[i, 0], to(1))
        mail.start(s[1], far_out.at[i, bottom], half_in.at[i, 1], to(-1))
        return s

    def near(i, up, down, to, s_far):
        s = [mail.slot() for _ in range(2)]
        mail.arrived(s_far[0], half_in.at[i, 0], to(-1))
        up_out[i, :rows] = (up[:rows] + half_in[i, 0].astype(F32)).astype(BF16)
        up_out[i, rows:] = up[rows:].astype(BF16)
        mail.start(s[0], up_out.at[i], full_in.at[i, 0], to(1))
        mail.arrived(s_far[1], half_in.at[i, 1], to(1))
        down_out[i, :rows] = down[:rows].astype(BF16)
        down_out[i, rows:] = (down[rows:] + half_in[i, 1].astype(F32)).astype(BF16)
        mail.start(s[1], down_out.at[i], full_in.at[i, 1], to(-1))
        return s

    def last(i, own, to, s_near):
        mail.arrived(s_near[0], full_in.at[i, 0], to(-1))
        mail.arrived(s_near[1], full_in.at[i, 1], to(1))
        return own + full_in[i, 0].astype(F32) + full_in[i, 1].astype(F32)

    def along_a(d):
        return peer(d, 0)

    def along_b(d):
        return peer(0, d)

    def b_far(da):
        return far(da, term(da, 2), along_b)

    def b_near(da, s):
        return near(da, term(da, 1), term(da, -1), along_b, s)

    def b_last(da, s):
        reduced[da] = last(da, term(da, 0), along_b, s)

    f2 = b_far(2)
    f3 = b_far(3)
    n2 = b_near(2, f2)

    mail.arrived(s_s, ssib, sibling)
    ssum[...] = st[pl.ds(pl.multiple_of(core * sr, 8), sr), :] + ssib[...]
    s_sz = [mail.slot() for _ in range(3)]
    for d in range(1, 4):
        to = (z + d) % 4
        src = ssum.at[pl.ds(pl.multiple_of(to * sq, 8), sq)]
        mail.start(s_sz[d - 1], src, sz_in.at[d - 1], device(y, to, core))

    f1 = b_far(1)
    n3 = b_near(3, f3)
    b_last(2, n2)
    fa = far(4, reduced[2], along_a)

    for d in range(1, 4):
        mail.arrived(s_sz[d - 1], sz_in.at[d - 1], device(y, (z + 4 - d) % 4, core))
    total = ssum[pl.ds(pl.multiple_of(z * sq, 8), sq), :] + sz_in[0] + sz_in[1] + sz_in[2]
    sy_out[...] = total
    s_sy = [mail.slot() for _ in range(3)]
    for d in range(1, 4):
        mail.start(s_sy[d - 1], sy_out, sy_in.at[d - 1], device((y + d) % 4, z, core))

    f0 = b_far(0)
    n1 = b_near(1, f1)
    b_last(3, n3)

    for d in range(1, 4):
        mail.arrived(s_sy[d - 1], sy_in.at[d - 1], device((y + 4 - d) % 4, z, core))
    s_at = pl.ds(pl.multiple_of(core * sr + z * sq, 8), sq)
    sfull[grp, s_at] = sy_out[...] + sy_in[1]
    sfull[1 - grp, s_at] = sy_in[0] + sy_in[2]
    s_sa = [mail.slot() for _ in range(3)]
    for d in range(1, 4):
        mail.start(
            s_sa[d - 1], sfull.at[:, s_at], sfull.at[:, s_at], device(y, (z + d) % 4, core)
        )

    n0 = b_near(0, f0)
    b_last(1, n1)
    na = near(4, reduced[1], reduced[3], along_a, fa)
    b_last(0, n0)

    for d in range(1, 4):
        frm = (z + 4 - d) % 4
        at = pl.ds(pl.multiple_of(core * sr + frm * sq, 8), sq)
        mail.arrived(s_sa[d - 1], sfull.at[:, at], device(y, frm, core))
    s_ss = mail.slot()
    at = pl.ds(pl.multiple_of(core * sr, 8), sr)
    mail.start(s_ss, sfull.at[:, at], sfull.at[:, at], sibling)

    fin[...] = last(4, reduced[0], along_a, na)
    s_fin = mail.slot()
    theirs = pl.ds(pl.multiple_of(other * rows, 16), rows)
    mail.start(s_fin, fin.at[theirs], out.at[core], sibling)
    out[core] = fin[pl.ds(pl.multiple_of(core * rows, 16), rows), :]
    at = pl.ds(pl.multiple_of(other * sr, 8), sr)
    mail.arrived(s_ss, sfull.at[:, at], sibling)
    mail.arrived(s_fin, out.at[other], sibling)
    mail.finish()


def backward(nrmt, sibt, pre, act, fold, lg):
    n_blk, depth, rows = nrmt.shape
    half = pre.shape[2]
    width = lg.shape[1]
    vmem = pl.BlockSpec(memory_space=VMEM)
    shape = jax.ShapeDtypeStruct
    return pl.pallas_call(
        backward_kernel,
        out_shape=(shape((2, depth // 2, half), F32), shape((2, width, 2 * half), F32)),
        in_specs=[vmem] * 6,
        out_specs=(vmem,) * 2,
        scratch_shapes=[
            VMEM((2, rows, half), BF16),
            VMEM((rows, half), BF16),
            VMEM((width, 2 * half), F32),
            VMEM((width // 2, 2 * half), F32),
            VMEM((width // 2, 2 * half), F32),
            VMEM((3, width // 8, 2 * half), F32),
            VMEM((width // 8, 2 * half), F32),
            VMEM((3, width // 8, 2 * half), F32),
            VMEM((5, depth, half), BF16),
            VMEM((5, depth, half), BF16),
            VMEM((5, depth, half), BF16),
            VMEM((5, 2, depth // 2, half), BF16),
            VMEM((5, 2, depth, half), BF16),
            VMEM((4, depth, half), F32),
            VMEM((depth, half), F32),
            pltpu.SemaphoreType.DMA((40,)),
            pltpu.SemaphoreType.DMA((40,)),
        ],
        compiler_params=pltpu.CompilerParams(
            collective_id=2, has_side_effects=True, vmem_limit_bytes=56 * 2**20
        ),
    )(nrmt, sibt, pre, act, fold, lg)


def shards(tokens, shift, scale, gate, fc1, fc2, proj, lift, conv_a, conv_b, target):
    tok_here, tok_cols, width = (tokens.shape[1], tokens.shape[2], tokens.shape[3])
    n_seq, n_tile = lax.axis_size("seq"), lax.axis_size("tile")
    seq, tile, grp = lax.axis_index("seq"), lax.axis_index("tile"), lax.axis_index("grp")
    rows_x = tokens[0].reshape(-1, width)
    proj_full = proj.astype(F32)
    patch_width = proj.shape[1]

    cols_here = fc2.shape[1]
    gps = []
    for at in (grp, 1 - grp):
        col_at = (at * n_seq + seq) * cols_here
        gate_cols = lax.dynamic_slice_in_dim(gate[0], col_at, cols_here, 0)
        proj_cols = lax.dynamic_slice_in_dim(proj_full, col_at, cols_here, 0)
        here = gate_cols[:, None] * proj_cols
        zero = jnp.zeros_like(here)
        first_image = jnp.concatenate([here, zero], axis=1)
        gps.append(jnp.where(grp == 0, first_image, jnp.roll(first_image, patch_width, axis=1)))
    gps = jnp.pad(jnp.stack(gps), ((0, 0), (0, 4), (0, 0)))

    xfull = rows_x.astype(F32)
    center = xfull - jnp.mean(xfull, axis=1, keepdims=True)
    spread = jnp.mean(center * center, axis=1, keepdims=True)
    normed = (center * lax.rsqrt(spread + 1e-06) * (1.0 + scale[0]) + shift[0]).astype(BF16)
    nrm = jnp.pad(normed.reshape(-1, 2 * n_seq, cols_here), ((0, 0), (0, 0), (0, 4)))
    nrm = nrm.reshape(-1, n_seq, 2 * (cols_here + 4)).transpose(1, 0, 2)
    nrmt = nrm.transpose(0, 2, 1)
    pre, act, partial, folded, gated, sibt, *borders = forward(
        nrm,
        nrmt,
        jnp.pad(fc1, ((0, 4), (0, 0))),
        jnp.pad(fc2, ((0, 0), (0, 4))),
        gps,
        target[0],
    )
    col_count = tok_cols // n_tile
    x_mine = lax.dynamic_slice_in_dim(tokens[0], tile * col_count, col_count, 1)
    xproj = jnp.dot(x_mine, proj, preferred_element_type=F32)
    ch = conv_a.shape[2]
    conv_bt = jnp.swapaxes(conv_b[::-1, ::-1], 2, 3).reshape(3, 3 * ch, ch)
    latent_mine, latent_rows = middle(
        partial.reshape(tok_here, tok_cols, patch_width),
        xproj,
        lift,
        conv_a.reshape(9, ch, ch),
        conv_b.reshape(3, 3 * ch, ch),
        conv_bt,
        target[0],
        *borders,
    )
    latent_rows = latent_rows.reshape(-1, patch_width)
    grad_one, outers = backward(nrmt, sibt, pre, act, folded, latent_rows)
    grad_one = grad_one.transpose(1, 0, 2).reshape(grad_one.shape[1], -1)[:cols_here]
    grad_two = lax.dot_general(
        outers.reshape(2 * patch_width, -1),
        gated[:cols_here],
        (((0,), (1,)), ((), ())),
        precision=lax.Precision.HIGHEST,
    )
    return (grad_one, grad_two, latent_mine[None])


def solution(mesh):
    in_specs = (
        P("grp", "seq", None, None),
        P("grp", None),
        P("grp", None),
        P("grp", None),
        P(("grp", "seq"), "tile"),
        P("tile", ("grp", "seq")),
        P(),
        P(),
        P(),
        P(),
        P("grp", "seq", "tile", None),
    )
    out_specs = (
        P(("grp", "seq"), "tile"),
        P("tile", ("grp", "seq")),
        P("grp", "seq", "tile", None),
    )
    return jax.shard_map(shards, mesh=mesh, in_specs=in_specs, out_specs=out_specs, check_vma=False)
```

```python
import jax
import jax.numpy as jnp
from jax import lax
from jax.experimental import pallas as pl
from jax.experimental.pallas import tpu as pltpu
from jax.sharding import PartitionSpec as P

F32 = jnp.float32
BF16 = jnp.bfloat16
MESH = pl.DeviceIdType.MESH
VMEM = pltpu.VMEM
NT = (((1,), (1,)), ((), ()))
TN = (((0,), (0,)), ((), ()))
EDGE = 8
LEAD = 16
NEXT = [(1, 0), (-1, 0), (0, 1), (0, -1), (1, 1), (1, -1), (-1, 1), (-1, -1)]
AROUND = [(0, 1), (0, 2), (0, 3)] + [(ds, dt) for ds in (-1, 1) for dt in range(4)]
STEPS = (1, 3, 2)


def gelu_tanh(value):
    return jax.nn.gelu(value, approximate=True)


def gelu_slope(x):
    k = 0.7978845608028654
    t = jnp.tanh(k * (x + 0.044715 * x * x * x))
    return 0.5 * (1.0 + t) + 0.5 * x * (1.0 - t * t) * (k + 3 * 0.044715 * k * x * x)


def split(value):
    high = value.astype(BF16)
    return high, (value - high.astype(F32)).astype(BF16)


def dot(lhs, rhs, dims=(((1,), (0,)), ((), ()))):
    return lax.dot_general(lhs, rhs, dims, preferred_element_type=F32)


def place():
    grp, seq, tile = lax.axis_index("grp"), lax.axis_index("seq"), lax.axis_index("tile")
    core = seq % 2
    y = (seq // 2) % 2 * 2 + grp
    z = seq // 4

    def device(y, z, core):
        return (y % 2, z * 4 + y // 2 * 2 + core, tile)

    return y, z, core, device


def oriented(y, z, core):
    a = y + core * (z - y)
    b = z + core * (y - z)

    def turn(a, b):
        return a + core * (b - a), b + core * (a - b)

    return a, b, turn


def block_of(y, z):
    return y % 2 * 8 + z * 2 + y // 2


def tile_peer(ds, dt):
    grp, seq, tile = lax.axis_index("grp"), lax.axis_index("seq"), lax.axis_index("tile")
    return (grp, (seq + ds) % 16, (tile + dt) % 4)


def announce(peers):
    for peer in peers:
        pl.semaphore_signal(
            pltpu.get_barrier_semaphore(), inc=1, device_id=peer, device_id_type=MESH
        )


def await_peers(peers):
    pl.semaphore_wait(pltpu.get_barrier_semaphore(), len(peers))


def greet(peers):
    announce(peers)
    await_peers(peers)


class Courier:
    def __init__(self, send, recv):
        self.send, self.recv, self.used, self.started = send, recv, 0, []

    def slot(self, count=1):
        self.used += count
        return self.used - count

    def slots(self, keys):
        return {key: self.slot() for key in keys}

    def copy(self, slot, src, dst, peer, landing=None):
        return pltpu.make_async_remote_copy(
            src_ref=src,
            dst_ref=dst,
            send_sem=self.send.at[slot],
            recv_sem=self.recv.at[slot if landing is None else landing],
            device_id=peer,
            device_id_type=MESH,
        )

    def start(self, slot, src, dst, peer, landing=None):
        copy = self.copy(slot, src, dst, peer, landing)
        copy.start()
        self.started.append(copy)

    def arrived(self, slot, dst, peer):
        self.copy(slot, dst, dst, peer).wait_recv()

    def finish(self):
        for copy in self.started:
            copy.wait_send()


def forward_kernel(
    tokens, shift, scale, proj, fc1, fc2, gps, target,
    slope_hbm, act_hbm, sums, fold, gboth, nrmt_hbm, t_rows, t_cols, t_ends,
    normed, nrm, nrmt, gath, gin, wpart, wsib, wsum, wz_out, wz_in, wy_out, wy_in, wfull, xp,
    pre, act, part, part_in, psrc, main_in, edge_in, send, recv, local,
):
    y, z, core, device = place()
    a, b, turn = oriented(y, z, core)
    grp, tile = lax.axis_index("grp"), lax.axis_index("tile")
    other = 1 - core
    sibling = device(y, z, other)
    greet(
        [sibling]
        + [device((y + d) % 4, z, k) for d in STEPS for k in range(2)]
        + [device(y, (z + d) % 4, k) for d in STEPS for k in range(2)]
        + [tile_peer(ds, dt) for ds, dt in AROUND]
    )
    mail = Courier(send, recv)
    rows, half = gath.shape[1] // 2, gath.shape[2]
    here_rows, width = tokens.shape

    def peer(da, db):
        return device(*turn((a + da) % 4, (b + db) % 4), core)

    def block(da, db):
        return block_of(*turn((a + da) % 4, (b + db) % 4))

    own = block(0, 0)
    mine = pl.ds(pl.multiple_of(core * rows, 16), rows)
    theirs = pl.ds(pl.multiple_of(other * rows, 16), rows)
    s_a = mail.slots((h, d) for h in range(2) for d in STEPS)
    r_a = {d: mail.slot(2) for d in STEPS}
    s_gate, s_own = mail.slot(), mail.slot()
    partner = device(y // 2 * 2 + 1 - grp, z, core)
    mail.start(s_gate, gps.at[1], gin, partner)
    src = fc1.at[:, pl.ds(pl.multiple_of(other * half, 128), half)]
    mail.start(s_own, src, gath.at[own, mine], sibling)
    for d in STEPS:
        for h in range(2):
            to = device((y + d) % 4, z, 0) if h == 0 else device(y, (z + d) % 4, 1)
            src = fc1.at[:, h * half : (h + 1) * half]
            mail.start(s_a[h, d], src, gath.at[own, mine], to, r_a[d] + core)
    gath[own, mine, :] = fc1[:, pl.ds(pl.multiple_of(core * half, 128), half)]

    @pl.loop(0, here_rows // 64)
    def _(i):
        at = pl.ds(pl.multiple_of(i * 64, 64), 64)
        x = tokens[at, :].astype(F32)
        center = x - jnp.mean(x, axis=1, keepdims=True)
        spread = jnp.mean(center * center, axis=1, keepdims=True)
        value = center * lax.rsqrt(spread + 1e-06) * (1.0 + scale[...]) + shift[...]
        normed[at, :] = value.astype(BF16)

    mail.arrived(s_gate, gin, partner)
    both = gps[0] + gin[...]
    gboth[...] = both
    high, low = split(both[: fc2.shape[1]])
    wpart[...] = dot(fc2[...], high) + dot(fc2[...], low)
    wq = half // 4
    s_w = mail.slot()
    mail.start(s_w, wpart.at[pl.ds(pl.multiple_of(other * half, 16), half)], wsib, sibling)

    blk_rows = pl.ds(pl.multiple_of(core * here_rows, 128), here_rows)
    cols = fc2.shape[1]

    def rechunk(i):
        first = 2 * cols * i // 128 * 128
        off = 2 * cols * i - first
        span = 256 if off + 2 * cols <= 256 else 384
        r = lax.broadcasted_iota(jnp.int32, (2 * rows, span), 0)
        k = lax.broadcasted_iota(jnp.int32, (2 * rows, span), 1)
        low_part = (k == r + off) & (r < cols)
        high_part = (k == r + (off + cols - rows)) & (r >= rows) & (r < rows + cols)
        pick = jnp.where(low_part | high_part, 1.0, 0.0).astype(BF16)
        value = normed[:, first : first + span]
        nrm[i, blk_rows, :] = dot(value, pick, NT).astype(BF16)
        nrmt[i, :, blk_rows] = dot(pick, value, NT).astype(BF16)

    s_n = mail.slots((q, k) for q in range(4) for k in range(2))

    def rechunk_four(q):
        for i in range(4 * q, 4 * q + 4):
            rechunk(i)
        four = pl.ds(4 * q, 4)
        ref = nrm.at[four, blk_rows]
        mail.start(s_n[q, 0], ref, ref, sibling)
        ref = nrmt.at[four, :, blk_rows]
        mail.start(s_n[q, 1], ref, ref, sibling)

    mail.arrived(s_w, wsib, sibling)
    wsum[...] = wpart[pl.ds(pl.multiple_of(core * half, 16), half), :] + wsib[...]
    wz_out[...] = wsum[...].astype(BF16)
    s_wz, s_wy, s_wa = mail.slots(STEPS), mail.slots(STEPS), mail.slots(STEPS)
    for d in STEPS:
        to = (z + d) % 4
        src = wz_out.at[pl.ds(pl.multiple_of(to * wq, 16), wq)]
        mail.start(s_wz[d], src, wz_in.at[d - 1], device(y, to, core))

    s_b = mail.slots((da, d) for da in range(4) for d in STEPS)

    def put_b(da):
        ref = gath.at[block(da, 0)]
        for d in STEPS:
            mail.start(s_b[da, d], ref, ref, peer(0, d))

    mail.arrived(s_own, gath.at[own, theirs], sibling)
    put_b(0)
    rechunk_four(0)

    def relay(d):
        at = block(-d, 0)
        frm = turn((a + 4 - d) % 4, b)
        for k in range(2):
            landed = gath.at[at, pl.ds(k * rows, rows)]
            mail.arrived(r_a[d] + k, landed, device(*frm, k))
        put_b((4 - d) % 4)

    def w_along_y():
        for d in STEPS:
            mail.arrived(s_wz[d], wz_in.at[d - 1], device(y, (z + 4 - d) % 4, core))
        here = pl.ds(pl.multiple_of(z * wq, 16), wq)
        total = wsum[here, :]
        for d in STEPS:
            total = total + wz_in[d - 1].astype(F32)
        wsum[here, :] = total
        wy_out[...] = total.astype(BF16)
        for d in STEPS:
            mail.start(s_wy[d], wy_out, wy_in.at[d - 1], device((y + d) % 4, z, core))

    def w_back():
        for d in STEPS:
            mail.arrived(s_wy[d], wy_in.at[d - 1], device((y + 4 - d) % 4, z, core))
        at = pl.ds(pl.multiple_of(z * wq, 16), wq)
        total = wsum[at, :]
        for d in STEPS:
            total = total + wy_in[d - 1].astype(F32)
        wfull[at, :] = total.astype(BF16)
        for d in STEPS:
            mail.start(s_wa[d], wfull.at[at], wfull.at[at], device(y, (z + d) % 4, core))

    w_along_y()
    relay(1)
    relay(3)
    w_back()
    relay(2)
    for q in range(1, 4):
        rechunk_four(q)
    height, breadth = target.shape[0], target.shape[1]
    top_rows, end_rows = pl.ds(0, 2), pl.ds(height - 2, 2)
    lead, trail = pl.ds(0, LEAD), pl.ds(breadth - LEAD, LEAD)
    borders = {
        (1, 0): (target.at[end_rows], t_rows.at[0]),
        (-1, 0): (target.at[top_rows], t_rows.at[1]),
        (0, 1): (target.at[:, trail], t_cols.at[0]),
        (0, -1): (target.at[:, lead], t_cols.at[1]),
        (1, 1): (target.at[end_rows, trail], t_ends.at[0]),
        (1, -1): (target.at[end_rows, lead], t_ends.at[1]),
        (-1, 1): (target.at[top_rows, trail], t_ends.at[2]),
        (-1, -1): (target.at[top_rows, lead], t_ends.at[3]),
    }
    s_border = mail.slots(NEXT)
    for to in NEXT:
        mail.start(s_border[to], *borders[to], tile_peer(*to))
    xp[...] = dot(tokens[...], proj[...]).reshape(xp.shape)

    sib_rows = pl.ds(pl.multiple_of(other * here_rows, 128), here_rows)
    for q in range(4):
        four = pl.ds(4 * q, 4)
        mail.arrived(s_n[q, 0], nrm.at[four, sib_rows], sibling)
        mail.arrived(s_n[q, 1], nrmt.at[four, :, sib_rows], sibling)
    keep = [pltpu.make_async_copy(nrmt, nrmt_hbm, local.at[0])]
    keep[0].start()

    def multiply(blocks, first=False):
        total = None
        for da, db in blocks:
            at = block(da, db)
            term = dot(nrm[at], gath[at])
            total = term if total is None else total + term
        pre[...] = total if first else pre[...] + total

    def take_b(da, d):
        mail.arrived(s_b[da, d], gath.at[block(da, -d)], peer(0, -d))

    multiply([(0, 0), (3, 0)], first=True)
    multiply([(1, 0), (2, 0)])
    for da in (0, 3, 1, 2):
        take_b(da, 1)
        take_b(da, 3)
        multiply([(da, 3), (da, 1)])
        take_b(da, 2)
        multiply([(da, 2)])

    a_all = gelu_tanh(pre[...]).astype(BF16)
    act[...] = a_all
    for d in STEPS:
        frm = (z + 4 - d) % 4
        at = pl.ds(pl.multiple_of(frm * wq, 16), wq)
        mail.arrived(s_wa[d], wfull.at[at], device(y, frm, core))
    n_out = fold.shape[1]
    fold[...] = jnp.where(grp == 0, wfull[:, :n_out], wfull[:, n_out:])

    n_rows, n_cols = xp.shape[0], xp.shape[1]
    for k in range(2):
        at = pl.ds(k * here_rows, here_rows)
        part[k] = dot(act[at, :], fold[...]).reshape(part.shape[1:])
    s_part = mail.slot()
    mail.start(s_part, part.at[other], part_in, sibling)
    own_cols = pl.ds(pl.multiple_of(tile * (n_cols // 4), 16), n_cols // 4)
    part[core, :, own_cols, :] = part[core, :, own_cols, :] + xp[:, own_cols, :]
    keep.append(pltpu.make_async_copy(act, act_hbm, local.at[1]))
    keep[1].start()
    mail.arrived(s_part, part_in, sibling)
    total = part[core] + part_in[...]

    edge = jnp.zeros((n_rows // 2, EDGE, 2 * n_out), F32)
    psrc[:, :EDGE, :] = edge
    psrc[:, EDGE + n_cols :, :] = edge
    psrc[:, EDGE : EDGE + n_cols, :] = jnp.concatenate(
        [total[: n_rows // 2], total[n_rows // 2 :]], axis=2
    )
    span = main_in.shape[2]

    def window(dt):
        return pl.ds(pl.multiple_of((tile + dt) % 4 * (n_cols // 4), 8), span)

    s_around = mail.slots(AROUND)
    for ds, dt in AROUND:
        if ds == 0:
            src, dst = psrc.at[:, window(dt)], main_in.at[dt]
        elif ds == -1:
            src, dst = psrc.at[pl.ds(0, 1), window(dt)], edge_in.at[1, dt]
        else:
            src, dst = psrc.at[pl.ds(n_rows // 2 - 1, 1), window(dt)], edge_in.at[0, dt]
        mail.start(s_around[ds, dt], src, dst, tile_peer(ds, dt))
    pre[...] = gelu_slope(pre[...])
    keep.append(pltpu.make_async_copy(pre, slope_hbm, local.at[2]))
    keep[2].start()

    total = psrc[:, window(0), :]
    for dt in range(1, 4):
        mail.arrived(s_around[0, dt], main_in.at[dt], tile_peer(0, -dt))
        total = total + main_in[dt]
    sums[1 : 1 + n_rows // 2] = total[:, :, :n_out]
    sums[1 + n_rows // 2 : 1 + n_rows] = total[:, :, n_out:]
    seq = lax.axis_index("seq")
    for i, ds in ((0, 1), (1, -1)):
        total = jnp.zeros(edge_in.shape[3:], F32)
        for dt in range(4):
            mail.arrived(s_around[ds, dt], edge_in.at[i, dt], tile_peer(-ds, -dt))
            total = total + edge_in[i, dt, 0]
        outside = (seq == 0) if i == 0 else (seq == 15)
        total = total[:, n_out:] if i == 0 else total[:, :n_out]
        sums[(n_rows + 1) * i] = jnp.where(outside, 0.0, total)

    for ds, dt in NEXT:
        mail.arrived(s_border[ds, dt], borders[ds, dt][1], tile_peer(-ds, -dt))
    for copy in keep:
        copy.wait()
    mail.finish()


def forward(tokens, shift, scale, proj, fc1, fc2, gps, target):
    rows, width = tokens.shape
    depth, hidden = fc1.shape
    half = hidden // 2
    n_out = proj.shape[1]
    n_blk = 16
    height, breadth, ch = target.shape
    token_rows, n_cols = 4 * rows // 512, 128
    span = n_cols // 4 + 2 * EDGE
    vmem, hbm = pl.BlockSpec(memory_space=VMEM), pl.BlockSpec(memory_space=pl.ANY)
    shape = jax.ShapeDtypeStruct
    return pl.pallas_call(
        forward_kernel,
        out_shape=(
            shape((2 * rows, half), F32),
            shape((2 * rows, half), BF16),
            shape((token_rows + 2, span, n_out), F32),
            shape((half, n_out), BF16),
            shape(gps.shape[1:], F32),
            shape((n_blk, 2 * depth, 2 * rows), BF16),
            shape((2, 2, breadth, ch), BF16),
            shape((2, height, LEAD, ch), BF16),
            shape((4, 2, LEAD, ch), BF16),
        ),
        in_specs=[vmem] * 7 + [hbm],
        out_specs=(hbm, hbm, vmem, vmem, vmem, hbm, hbm, hbm, hbm),
        scratch_shapes=[
            VMEM((rows, width), BF16),
            VMEM((n_blk, 2 * rows, 2 * depth), BF16),
            VMEM((n_blk, 2 * depth, 2 * rows), BF16),
            VMEM((n_blk, 2 * depth, half), BF16),
            VMEM(gps.shape[1:], F32),
            VMEM((hidden, 2 * n_out), F32),
            VMEM((half, 2 * n_out), F32),
            VMEM((half, 2 * n_out), F32),
            VMEM((half, 2 * n_out), BF16),
            VMEM((3, half // 4, 2 * n_out), BF16),
            VMEM((half // 4, 2 * n_out), BF16),
            VMEM((3, half // 4, 2 * n_out), BF16),
            VMEM((half, 2 * n_out), BF16),
            VMEM((token_rows, n_cols, n_out), F32),
            VMEM((2 * rows, half), F32),
            VMEM((2 * rows, half), BF16),
            VMEM((2, token_rows, n_cols, n_out), F32),
            VMEM((token_rows, n_cols, n_out), F32),
            VMEM((token_rows // 2, n_cols + 2 * EDGE, 2 * n_out), F32),
            VMEM((4, token_rows // 2, span, 2 * n_out), F32),
            VMEM((2, 4, 1, span, 2 * n_out), F32),
            pltpu.SemaphoreType.DMA((72,)),
            pltpu.SemaphoreType.DMA((72,)),
            pltpu.SemaphoreType.DMA((3,)),
        ],
        compiler_params=pltpu.CompilerParams(
            collective_id=1, has_side_effects=True, vmem_limit_bytes=58 * 2**20
        ),
    )(tokens, shift, scale, proj, fc1, fc2, gps, target)


def pixel_kernels(lift, conv_a):
    lifted = {
        (o, e): dot(lift, conv_a[3 * o + e])
        for o in range(3)
        for e in range(3)
    }

    def reach(pixel, cell):
        return [o for o in range(3) if (pixel + o - 1) // 2 == cell]

    out = {}
    for r in range(-1, 5):
        for c in range(-1, 5):
            parts = []
            for a in range(2):
                for b in range(2):
                    total = jnp.zeros_like(lifted[0, 0])
                    for o in reach(r, a):
                        for e in reach(c, b):
                            total = total + lifted[o, e]
                    parts.append(total)
            out[r, c] = jnp.concatenate(parts, axis=0)
    return out


def middle_kernel(
    sums, lift, conv_a, conv_b, conv_bt, target, t_rows, t_cols, t_ends,
    latent, lg,
    patch, kern, f_ref, a_ref, b_ref, acc, want, gf, send, recv,
):
    grp, seq, tile = lax.axis_index("grp"), lax.axis_index("seq"), lax.axis_index("tile")
    core = seq % 2

    def cores(k, dt):
        return (grp, seq - core + (core + k) % 2, (tile + dt) % 4)

    around = [(k, dt) for k in range(2) for dt in range(4) if (k, dt) != (0, 0)]
    announce([cores(k, dt) for k, dt in around])
    mail = Courier(send, recv)
    n_tok, span, width = sums.shape
    n_rows, here = n_tok - 2, span - 2 * EDGE
    pairs, ch = a_ref.shape[1], a_ref.shape[2] // 4

    kernels = pixel_kernels(lift[...], conv_a)
    for r in range(-1, 5):
        for c in range(-1, 5):
            kern[6 * (r + 1) + c + 1] = kernels[r, c].astype(BF16)
    height, breadth = target.shape[0], target.shape[1]
    body, lead = slice(LEAD, LEAD + breadth), slice(0, LEAD)
    trail = slice(LEAD + breadth, 2 * LEAD + breadth)
    mid = slice(2, 2 + height)

    def want_at(rows, at, value):
        value = value.astype(F32)
        want[rows, 0, at, :] = value[:, :, :128]
        want[rows, 1, at, :] = value[:, :, 128:]

    want_at(mid, body, target[...])
    want_at(slice(0, 2), body, t_rows[0])
    want_at(slice(2 + height, 4 + height), body, t_rows[1])
    for side, at in ((0, lead), (1, trail)):
        want_at(mid, at, t_cols[side])
        want_at(slice(0, 2), at, t_ends[side])
        want_at(slice(2 + height, 4 + height), at, t_ends[2 + side])

    rows = {r: sums[r] for r in range(n_tok)}
    for r in range(n_tok):
        patch[0, r + 1] = pltpu.roll(rows[r], 1, 0).astype(BF16)
        patch[1, r + 1] = rows[r].astype(BF16)
        patch[2, r + 1] = pltpu.roll(rows[r], span - 1, 0).astype(BF16)
    for k in range(3):
        patch[k, 0] = jnp.zeros((span, width), BF16)
        patch[k, n_tok + 1] = jnp.zeros((span, width), BF16)

    def near(phase):
        return [(d, phase - 4 * d) for d in (-1, 0, 1) if -1 <= phase - 4 * d <= 4]

    for al in range(4):
        for ph in range(4):
            value = None
            for dr, r in near(al):
                for dc, c in near(ph):
                    lhs = patch[1 + dc, 1 + dr : 1 + dr + n_tok].reshape(n_tok * span, width)
                    term = dot(lhs, kern[6 * (r + 1) + c + 1])
                    value = term if value is None else value + term
            value = value.reshape(n_tok, span, ch)
            for tr in range(n_tok):
                at = pl.ds(ph // 2, span, stride=2)
                f_ref[4 * tr + al, ph % 2, 0, at, :] = value[tr, :, :128]
                f_ref[4 * tr + al, ph % 2, 1, at, :] = value[tr, :, 128:]

    def inside(row, b):
        r = seq * height + row
        c = 2 * (tile * breadth // 2 + lax.broadcasted_iota(jnp.int32, (pairs, 1), 0) - EDGE) + b
        return (r >= 0) & (r < 16 * height) & (c >= 0) & (c < 4 * breadth)

    def both(ref, at, rows):
        return jnp.concatenate([ref[*at, 0, rows, :], ref[*at, 1, rows, :]], axis=1)

    def spread(ref, at, v0, v1):
        ref[at, :, 0:ch] = pltpu.roll(v1, 1, 0).astype(BF16)
        ref[at, :, ch : 2 * ch] = v0.astype(BF16)
        ref[at, :, 2 * ch : 3 * ch] = v1.astype(BF16)
        ref[at, :, 3 * ch :] = pltpu.roll(v0, pairs - 1, 0).astype(BF16)

    @pl.loop(0, height + 6)
    def _(i):
        smooth = []
        for b in range(2):
            f = both(f_ref, (i + 1, b), slice(EDGE, EDGE + pairs))
            sigma = jax.nn.sigmoid(f)
            smooth.append(jnp.where(inside(i - 3, b), f * sigma, 0.0))
            slope = sigma * (1.0 + f * (1.0 - sigma))
            f_ref[i + 1, b, 0, EDGE : EDGE + pairs, :] = slope[:, :128]
            f_ref[i + 1, b, 1, EDGE : EDGE + pairs, :] = slope[:, 128:]
        spread(a_ref, i, *smooth)

    def conv(src, weights, out_rows, chunk):
        @pl.loop(0, out_rows // chunk)
        def _(i):
            for b in range(2):
                value = None
                for o in range(3):
                    lhs = src[pl.ds(i * chunk + o, chunk), :, b * ch : (b + 3) * ch]
                    term = dot(lhs.reshape(chunk * pairs, 3 * ch), weights[o])
                    value = term if value is None else value + term
                acc[b, pl.ds(i * chunk, chunk)] = value.reshape(chunk, pairs, ch)

    conv(a_ref, conv_b, height + 4, (height + 4) // 2)

    @pl.loop(0, height + 4)
    def _(i):
        grad = []
        for b in range(2):
            diff = acc[b, i] - both(want, (i,), pl.ds(b, pairs, stride=2))
            grad.append(jnp.where(inside(i - 2, b), diff, 0.0))
        spread(b_ref, i, *grad)

    conv(b_ref, conv_bt, height + 2, (height + 2) // 2)

    @pl.loop(0, height + 2)
    def _(i):
        for b in range(2):
            value = acc[b, i] * both(f_ref, (i + 3, b), slice(EDGE, EDGE + pairs))
            value = jnp.where(inside(i - 1, b), value, 0.0)
            gf[i, b, 0], gf[i, b, 1] = value[:, :128], value[:, 128:]

    grad = None
    for r in range(-1, 5):
        for c in range(-1, 5):
            at = pl.ds(EDGE + c // 2, here, stride=2)
            lhs = jnp.concatenate(
                [both(gf, (4 * tr + r + 1, c % 2), at).astype(BF16) for tr in range(n_rows)],
                axis=0,
            )
            term = dot(lhs, kern[6 * (r + 1) + c + 1], NT)
            grad = term if grad is None else grad + term
    grad = grad.reshape(n_rows, here, width)
    latent[...] = grad
    def part_of(k, dt):
        cols = pl.ds(pl.multiple_of((tile + dt) % 4 * here, 16), here)
        return lg.at[pl.ds((core + k) % 2 * n_rows, n_rows), cols]

    cols = pl.ds(pl.multiple_of(tile * here, 16), here)
    lg[pl.ds(core * n_rows, n_rows), cols, :] = grad.astype(BF16)
    await_peers(around)
    s_back = mail.slots(around)
    for k, dt in around:
        mail.start(s_back[k, dt], part_of(0, 0), part_of(0, 0), cores(k, dt))
    for k, dt in around:
        mail.arrived(s_back[k, dt], part_of(k, -dt), cores(k, -dt))
    mail.finish()


def middle(sums, lift, conv_a, conv_b, conv_bt, target, t_rows, t_cols, t_ends):
    n_tok, span, width = sums.shape
    n_rows, here = n_tok - 2, span - 2 * EDGE
    height, breadth, ch = target.shape
    pairs = breadth // 2 + 2 * EDGE
    vmem = pl.BlockSpec(memory_space=VMEM)
    shape = jax.ShapeDtypeStruct
    return pl.pallas_call(
        middle_kernel,
        out_shape=(
            shape((n_rows, here, width), F32),
            shape((2 * n_rows, 4 * here, width), BF16),
        ),
        in_specs=[vmem] * 9,
        out_specs=(vmem,) * 2,
        scratch_shapes=[
            VMEM((3, n_rows + 4, span, width), BF16),
            VMEM((36, width, ch), BF16),
            VMEM((height + 8, 2, 2, 2 * span, ch // 2), F32),
            VMEM((height + 6, pairs, 4 * ch), BF16),
            VMEM((height + 4, pairs, 4 * ch), BF16),
            VMEM((2, height + 4, pairs, ch), F32),
            VMEM((height + 4, 2, breadth + 2 * LEAD, ch // 2), F32),
            VMEM((height + 2, 2, 2, pairs, ch // 2), F32),
            pltpu.SemaphoreType.DMA((40,)),
            pltpu.SemaphoreType.DMA((40,)),
        ],
        compiler_params=pltpu.CompilerParams(
            collective_id=3, has_side_effects=True, vmem_limit_bytes=58 * 2**20
        ),
    )(sums, lift, conv_a, conv_b, conv_bt, target, t_rows, t_cols, t_ends)
def backward_kernel(
    nrmt_hbm, slope_hbm, act_hbm, fold, lg, gboth, out, two,
    nrmt, slope, act, gpre, st, sz_in, sy_out, sy_in, sfull, b_out, b_in, a_out, a_in, fin, fin_in,
    send, recv, local,
):
    y, z, core, device = place()
    a, b, turn = oriented(y, z, core)
    grp = lax.axis_index("grp")
    other = 1 - core
    sibling = device(y, z, other)
    peers = (
        [sibling]
        + [device((y + d) % 4, z, core) for d in STEPS]
        + [device(y, (z + d) % 4, core) for d in STEPS]
    )
    announce(peers)
    loads = [
        pltpu.make_async_copy(src, dst, local.at[i])
        for i, (src, dst) in enumerate(
            ((act_hbm, act), (slope_hbm, slope), (nrmt_hbm, nrmt))
        )
    ]
    for load in loads:
        load.start()
    mail = Courier(send, recv)
    half = gpre.shape[1]
    rows = nrmt.shape[1] // 2

    def peer(da, db):
        return device(*turn((a + da) % 4, (b + db) % 4), core)

    def block(da, db):
        return block_of(*turn((a + da) % 4, (b + db) % 4))

    def term(da, db):
        return dot(nrmt[block(da, db)], gpre[...])

    s_b = mail.slots((da, d) for da in range(4) for d in STEPS)
    s_a = mail.slots(STEPS)

    def send_b(da):
        for d in (2, 1, 3):
            b_out[da, d - 1] = term(da, d).astype(BF16)
            mail.start(s_b[da, d], b_out.at[da, d - 1], b_in.at[da, d - 1], peer(0, d))

    def sum_b(da):
        total = term(da, 0)
        for d in STEPS:
            mail.arrived(s_b[da, d], b_in.at[da, d - 1], peer(0, -d))
            total = total + b_in[da, d - 1].astype(F32)
        return total

    def send_a(d):
        a_out[d - 1] = sum_b(d).astype(BF16)
        mail.start(s_a[d], a_out.at[d - 1], a_in.at[d - 1], peer(d, 0))

    loads[0].wait()
    st[...] = dot(lg[...], act[...], TN)
    sq = st.shape[0] // 4
    s_sz, s_sy, s_sa = mail.slots(STEPS), mail.slots(STEPS), mail.slots(STEPS)
    await_peers(peers)
    for d in STEPS:
        to = (z + d) % 4
        src = st.at[pl.ds(pl.multiple_of(to * sq, 8), sq)]
        mail.start(s_sz[d], src, sz_in.at[d - 1], device(y, to, core))

    loads[1].wait()
    gpre[...] = (dot(lg[...], fold[...], NT) * slope[...]).astype(BF16)
    loads[2].wait()
    send_b(2)

    for d in STEPS:
        mail.arrived(s_sz[d], sz_in.at[d - 1], device(y, (z + 4 - d) % 4, core))
    s_at = pl.ds(pl.multiple_of(z * sq, 8), sq)
    sy_out[...] = st[s_at, :] + sz_in[0] + sz_in[1] + sz_in[2]
    for d in STEPS:
        mail.start(s_sy[d], sy_out, sy_in.at[d - 1], device((y + d) % 4, z, core))

    send_b(1)
    for d in STEPS:
        mail.arrived(s_sy[d], sy_in.at[d - 1], device((y + 4 - d) % 4, z, core))
    sfull[core, grp, s_at] = sy_out[...] + sy_in[1]
    sfull[core, 1 - grp, s_at] = sy_in[0] + sy_in[2]
    for d in STEPS:
        ref = sfull.at[core, :, s_at]
        mail.start(s_sa[d], ref, ref, device(y, (z + d) % 4, core))
    send_b(3)
    send_b(0)

    send_a(2)
    for d in STEPS:
        frm = (z + 4 - d) % 4
        at = pl.ds(pl.multiple_of(frm * sq, 8), sq)
        mail.arrived(s_sa[d], sfull.at[core, :, at], device(y, frm, core))
    s_ss = mail.slot()
    mail.start(s_ss, sfull.at[core], sfull.at[core], sibling)
    send_a(1)
    send_a(3)

    mail.arrived(s_ss, sfull.at[other], sibling)
    g_high, g_low = split(gboth[...])
    for h in range(2):
        s_high, s_low = split(sfull[h].reshape(-1, half).T)
        value = dot(s_high, g_high, NT) + dot(s_high, g_low, NT) + dot(s_low, g_high, NT)
        two[h * half : (h + 1) * half, :] = value[:, : two.shape[1]]

    total = sum_b(0)
    for d in STEPS:
        mail.arrived(s_a[d], a_in.at[d - 1], peer(-d, 0))
        total = total + a_in[d - 1].astype(F32)
    fin[...] = total
    s_fin = mail.slot()
    theirs = pl.ds(pl.multiple_of(other * rows, 16), rows)
    mail.start(s_fin, fin.at[theirs], fin_in, sibling)
    here = out.shape[0]
    mine = fin[pl.ds(pl.multiple_of(core * rows, 16), rows), :]
    out[:, pl.ds(pl.multiple_of(core * half, 128), half)] = mine[:here]
    mail.arrived(s_fin, fin_in, sibling)
    out[:, pl.ds(pl.multiple_of(other * half, 128), half)] = fin_in[:here, :]
    mail.finish()


def backward(nrmt, slope, act, fold, lg, gboth, here):
    n_blk, depth, rows = nrmt.shape
    half = slope.shape[1]
    width = lg.shape[1]
    vmem, hbm = pl.BlockSpec(memory_space=VMEM), pl.BlockSpec(memory_space=pl.ANY)
    shape = jax.ShapeDtypeStruct
    return pl.pallas_call(
        backward_kernel,
        out_shape=(shape((here, 2 * half), F32), shape((2 * half, here), F32)),
        in_specs=[hbm] * 3 + [vmem] * 3,
        out_specs=(vmem,) * 2,
        scratch_shapes=[
            VMEM(nrmt.shape, BF16),
            VMEM(slope.shape, F32),
            VMEM(act.shape, BF16),
            VMEM((rows, half), BF16),
            VMEM((width, half), F32),
            VMEM((3, width // 4, half), F32),
            VMEM((width // 4, half), F32),
            VMEM((3, width // 4, half), F32),
            VMEM((2, 2, width, half), F32),
            VMEM((4, 3, depth, half), BF16),
            VMEM((4, 3, depth, half), BF16),
            VMEM((3, depth, half), BF16),
            VMEM((3, depth, half), BF16),
            VMEM((depth, half), F32),
            VMEM((depth // 2, half), F32),
            pltpu.SemaphoreType.DMA((32,)),
            pltpu.SemaphoreType.DMA((32,)),
            pltpu.SemaphoreType.DMA((3,)),
        ],
        compiler_params=pltpu.CompilerParams(
            collective_id=2, has_side_effects=True, vmem_limit_bytes=58 * 2**20
        ),
    )(nrmt, slope, act, fold, lg, gboth)


def shards(tokens, shift, scale, gate, fc1, fc2, proj, lift, conv_a, conv_b, target):
    width = tokens.shape[3]
    n_seq = lax.axis_size("seq")
    seq, grp = lax.axis_index("seq"), lax.axis_index("grp")
    patch_width = proj.shape[1]

    cols_here = fc2.shape[1]
    gps = []
    for at in (grp, 1 - grp):
        col_at = (at * n_seq + seq) * cols_here
        gate_cols = lax.dynamic_slice_in_dim(gate[0], col_at, cols_here, 0)
        proj_cols = lax.dynamic_slice_in_dim(proj, col_at, cols_here, 0)
        here = gate_cols[:, None] * proj_cols.astype(F32)
        zero = jnp.zeros_like(here)
        pair = [jnp.where(grp == i, here, zero) for i in range(2)]
        gps.append(jnp.concatenate(pair, axis=1))
    gps = jnp.pad(jnp.stack(gps), ((0, 0), (0, 4), (0, 0)))

    slope, act, sums, fold, gboth, nrmt, *borders = forward(
        tokens[0].reshape(-1, width),
        shift,
        scale,
        proj,
        jnp.pad(fc1, ((0, 4), (0, 0))),
        fc2,
        gps,
        target[0],
    )
    ch = conv_a.shape[2]
    conv_bt = jnp.swapaxes(conv_b[::-1, ::-1], 2, 3).reshape(3, 3 * ch, ch)
    latent_mine, latent_rows = middle(
        sums,
        lift,
        conv_a.reshape(9, ch, ch),
        conv_b.reshape(3, 3 * ch, ch),
        conv_bt,
        target[0],
        *borders,
    )
    latent_rows = latent_rows.reshape(-1, patch_width)
    grad_one, grad_two = backward(nrmt, slope, act, fold, latent_rows, gboth, cols_here)
    return (grad_one, grad_two, latent_mine[None])


def solution(mesh):
    in_specs = (
        P("grp", "seq", None, None),
        P("grp", None),
        P("grp", None),
        P("grp", None),
        P(("grp", "seq"), "tile"),
        P("tile", ("grp", "seq")),
        P(),
        P(),
        P(),
        P(),
        P("grp", "seq", "tile", None),
    )
    out_specs = (
        P(("grp", "seq"), "tile"),
        P("tile", ("grp", "seq")),
        P("grp", "seq", "tile", None),
    )
    return jax.shard_map(shards, mesh=mesh, in_specs=in_specs, out_specs=out_specs, check_vma=False)
```

```python
import jax
import jax.numpy as jnp
from jax import lax
from jax.experimental import pallas as pl
from jax.experimental.pallas import tpu as pltpu
from jax.sharding import PartitionSpec as P

F32 = jnp.float32
BF16 = jnp.bfloat16
MESH = pl.DeviceIdType.MESH
VMEM = pltpu.VMEM
NT = (((1,), (1,)), ((), ()))
TN = (((0,), (0,)), ((), ()))
EDGE = 8
LEAD = 16
NEXT = [(1, 0), (-1, 0), (0, 1), (0, -1), (1, 1), (1, -1), (-1, 1), (-1, -1)]
AROUND = [(0, 1), (0, 2), (0, 3)] + [(ds, dt) for ds in (-1, 1) for dt in range(4)]
STEPS = (1, 3, 2)


def gelu_tanh(value):
    return jax.nn.gelu(value, approximate=True)


def gelu_slope(x):
    k = 0.7978845608028654
    t = jnp.tanh(k * (x + 0.044715 * x * x * x))
    return 0.5 * (1.0 + t) + 0.5 * x * (1.0 - t * t) * (k + 3 * 0.044715 * k * x * x)


def split(value):
    high = value.astype(BF16)
    return high, (value - high.astype(F32)).astype(BF16)


def dot(lhs, rhs, dims=(((1,), (0,)), ((), ()))):
    return lax.dot_general(lhs, rhs, dims, preferred_element_type=F32)


def place():
    grp, seq, tile = lax.axis_index("grp"), lax.axis_index("seq"), lax.axis_index("tile")
    core = seq % 2
    y = (seq // 2) % 2 * 2 + grp
    z = seq // 4

    def device(y, z, core):
        return (y % 2, z * 4 + y // 2 * 2 + core, tile)

    return y, z, core, device


def oriented(y, z, core):
    a = y + core * (z - y)
    b = z + core * (y - z)

    def turn(a, b):
        return a + core * (b - a), b + core * (a - b)

    return a, b, turn


def block_of(y, z):
    return y % 2 * 8 + z * 2 + y // 2


def tile_peer(ds, dt):
    grp, seq, tile = lax.axis_index("grp"), lax.axis_index("seq"), lax.axis_index("tile")
    return (grp, (seq + ds) % 16, (tile + dt) % 4)


def announce(peers):
    for peer in peers:
        pl.semaphore_signal(
            pltpu.get_barrier_semaphore(), inc=1, device_id=peer, device_id_type=MESH
        )


def await_peers(peers):
    pl.semaphore_wait(pltpu.get_barrier_semaphore(), len(peers))


def greet(peers):
    announce(peers)
    await_peers(peers)


class Courier:
    def __init__(self, send, recv):
        self.send, self.recv, self.used, self.started = send, recv, 0, []

    def slot(self, count=1):
        self.used += count
        return self.used - count

    def slots(self, keys):
        return {key: self.slot() for key in keys}

    def copy(self, slot, src, dst, peer, landing=None):
        return pltpu.make_async_remote_copy(
            src_ref=src,
            dst_ref=dst,
            send_sem=self.send.at[slot],
            recv_sem=self.recv.at[slot if landing is None else landing],
            device_id=peer,
            device_id_type=MESH,
        )

    def start(self, slot, src, dst, peer, landing=None):
        copy = self.copy(slot, src, dst, peer, landing)
        copy.start()
        self.started.append(copy)

    def arrived(self, slot, dst, peer):
        self.copy(slot, dst, dst, peer).wait_recv()

    def finish(self):
        for copy in self.started:
            copy.wait_send()


def pixel_kernels(lift, conv_a):
    lifted = {
        (o, e): dot(lift, conv_a[3 * o + e])
        for o in range(3)
        for e in range(3)
    }

    def reach(pixel, cell):
        return [o for o in range(3) if (pixel + o - 1) // 2 == cell]

    out = {}
    for r in range(-1, 5):
        for c in range(-1, 5):
            parts = []
            for a in range(2):
                for b in range(2):
                    total = jnp.zeros_like(lifted[0, 0])
                    for o in reach(r, a):
                        for e in reach(c, b):
                            total = total + lifted[o, e]
                    parts.append(total)
            out[r, c] = jnp.concatenate(parts, axis=0)
    return out


def forward_kernel(
    tokens_hbm, shift, scale, gate, projt, fc1_own, fc2t, lift, conv_a_hbm, conv_b_hbm, target,
    slope_hbm, act_hbm, sums, fold, gboth, nrmt_hbm, kern_hbm, conv_bt_hbm,
    t_rows, t_cols, t_ends,
    fc1, gps, tokens, conv_a, conv_b, kern, conv_bt, normed, nrm, nrmt, gath, gin, wpart, wsib, wsum, wz_out, wz_in, wy_out, wy_in, wfull, xp,
    pre, act, part, part_in, psrc, main_in, edge_in, send, recv, local,
):
    y, z, core, device = place()
    a, b, turn = oriented(y, z, core)
    grp, tile = lax.axis_index("grp"), lax.axis_index("tile")
    other = 1 - core
    sibling = device(y, z, other)
    peers = (
        [sibling]
        + [device((y + d) % 4, z, k) for d in STEPS for k in range(2)]
        + [device(y, (z + d) % 4, k) for d in STEPS for k in range(2)]
        + [tile_peer(ds, dt) for ds, dt in AROUND]
    )
    announce(peers)
    loads = [
        pltpu.make_async_copy(src, dst, local.at[i])
        for i, (src, dst) in enumerate(
            ((tokens_hbm, tokens), (conv_a_hbm, conv_a), (conv_b_hbm, conv_b))
        )
    ]
    for load in loads:
        load.start()
    mail = Courier(send, recv)
    rows, half = gath.shape[1] // 2, gath.shape[2]
    here_rows, width = tokens.shape
    cols = fc2t.shape[0]
    last = cols // 16 * 16
    fc1[:last] = fc1_own[:last]
    tail = jnp.concatenate(
        [fc1_own[last:].astype(F32), jnp.zeros((rows - cols, 2 * half), F32)], axis=0
    )
    fc1[last:] = tail.astype(BF16)

    n_out = projt.shape[0]
    seq = lax.axis_index("seq")
    for i, g in enumerate((grp, 1 - grp)):
        start = (g * 16 + seq) * cols
        first = jnp.minimum(start // 128 * 128, width - 256)
        at = pl.ds(pl.multiple_of(first, 128), 256)
        high, low = split(gate[:, at] * projt[:, at].astype(F32))
        r = lax.broadcasted_iota(jnp.int32, (rows, 256), 0)
        k = lax.broadcasted_iota(jnp.int32, (rows, 256), 1)
        pick = jnp.where((k == r + (start - first)) & (r < cols), 1.0, 0.0).astype(BF16)
        value = dot(pick, high, NT) + dot(pick, low, NT)
        zero = jnp.zeros_like(value)
        gps[i] = jnp.concatenate(
            [jnp.where(grp == 0, value, zero), jnp.where(grp == 1, value, zero)], axis=1
        )
    await_peers(peers)

    def peer(da, db):
        return device(*turn((a + da) % 4, (b + db) % 4), core)

    def block(da, db):
        return block_of(*turn((a + da) % 4, (b + db) % 4))

    own = block(0, 0)
    mine = pl.ds(pl.multiple_of(core * rows, 16), rows)
    theirs = pl.ds(pl.multiple_of(other * rows, 16), rows)
    s_a = mail.slots((h, d) for h in range(2) for d in STEPS)
    r_a = {d: mail.slot(2) for d in STEPS}
    s_gate, s_own = mail.slot(), mail.slot()
    partner = device(y // 2 * 2 + 1 - grp, z, core)
    mail.start(s_gate, gps.at[1], gin, partner)
    src = fc1.at[:, pl.ds(pl.multiple_of(other * half, 128), half)]
    mail.start(s_own, src, gath.at[own, mine], sibling)
    for d in STEPS:
        for h in range(2):
            to = device((y + d) % 4, z, 0) if h == 0 else device(y, (z + d) % 4, 1)
            src = fc1.at[:, h * half : (h + 1) * half]
            mail.start(s_a[h, d], src, gath.at[own, mine], to, r_a[d] + core)
    gath[own, mine, :] = fc1[:, pl.ds(pl.multiple_of(core * half, 128), half)]

    loads[0].wait()

    @pl.loop(0, here_rows // 64)
    def _(i):
        x = tokens[pl.ds(pl.multiple_of(i * 64, 64), 64), :].astype(F32)
        center = x - jnp.mean(x, axis=1, keepdims=True)
        spread = jnp.mean(center * center, axis=1, keepdims=True)
        value = center * lax.rsqrt(spread + 1e-06) * (1.0 + scale[...]) + shift[...]
        at = pl.ds(pl.multiple_of(core * here_rows + i * 64, 64), 64)
        normed[at, :] = value.astype(BF16)

    blk_rows = pl.ds(pl.multiple_of(core * here_rows, 128), here_rows)
    s_n = mail.slot()
    mail.start(s_n, normed.at[blk_rows], normed.at[blk_rows], sibling)

    mail.arrived(s_gate, gin, partner)
    both = gps[0] + gin[...]
    gboth[...] = both
    high, low = split(both[:cols])
    wpart[...] = dot(fc2t[...], high, TN) + dot(fc2t[...], low, TN)
    wq = half // 4
    s_w = mail.slot()
    mail.start(s_w, wpart.at[pl.ds(pl.multiple_of(other * half, 16), half)], wsib, sibling)

    def rechunk(i):
        first = 2 * cols * i // 128 * 128
        off = 2 * cols * i - first
        span = 256 if off + 2 * cols <= 256 else 384
        r = lax.broadcasted_iota(jnp.int32, (2 * rows, span), 0)
        k = lax.broadcasted_iota(jnp.int32, (2 * rows, span), 1)
        low_part = (k == r + off) & (r < cols)
        high_part = (k == r + (off + cols - rows)) & (r >= rows) & (r < rows + cols)
        pick = jnp.where(low_part | high_part, 1.0, 0.0).astype(BF16)
        value = normed[:, first : first + span]
        nrm[i] = dot(value, pick, NT).astype(BF16)
        nrmt[i] = dot(pick, value, NT).astype(BF16)

    mail.arrived(s_w, wsib, sibling)
    wsum[...] = wpart[pl.ds(pl.multiple_of(core * half, 16), half), :] + wsib[...]
    wz_out[...] = wsum[...].astype(BF16)
    s_wz, s_wy, s_wa = mail.slots(STEPS), mail.slots(STEPS), mail.slots(STEPS)
    for d in STEPS:
        to = (z + d) % 4
        src = wz_out.at[pl.ds(pl.multiple_of(to * wq, 16), wq)]
        mail.start(s_wz[d], src, wz_in.at[d - 1], device(y, to, core))

    s_b = mail.slots((da, d) for da in range(4) for d in STEPS)

    def put_b(da):
        ref = gath.at[block(da, 0)]
        for d in STEPS:
            mail.start(s_b[da, d], ref, ref, peer(0, d))

    mail.arrived(s_own, gath.at[own, theirs], sibling)
    put_b(0)

    keep = [
        pltpu.make_async_copy(src, dst, local.at[3 + i])
        for i, (src, dst) in enumerate(
            (
                (nrmt, nrmt_hbm),
                (act, act_hbm),
                (pre, slope_hbm),
                (kern, kern_hbm),
                (conv_bt, conv_bt_hbm),
            )
        )
    ]
    loads[1].wait()
    kernels = pixel_kernels(lift[...], conv_a)
    for i, value in enumerate(kernels.values()):
        kern[i] = value.astype(BF16)
    keep[3].start()
    loads[2].wait()
    ch = conv_b.shape[2]
    for o in range(3):
        for e in range(3):
            conv_bt[o, e * ch : (e + 1) * ch, :] = conv_b[8 - 3 * o - e].T
    keep[4].start()
    xp[...] = dot(tokens[...], projt[...], NT).reshape(xp.shape)

    def relay(d):
        at = block(-d, 0)
        frm = turn((a + 4 - d) % 4, b)
        for k in range(2):
            landed = gath.at[at, pl.ds(k * rows, rows)]
            mail.arrived(r_a[d] + k, landed, device(*frm, k))
        put_b((4 - d) % 4)

    def w_along_y():
        for d in STEPS:
            mail.arrived(s_wz[d], wz_in.at[d - 1], device(y, (z + 4 - d) % 4, core))
        here = pl.ds(pl.multiple_of(z * wq, 16), wq)
        total = wsum[here, :]
        for d in STEPS:
            total = total + wz_in[d - 1].astype(F32)
        wsum[here, :] = total
        wy_out[...] = total.astype(BF16)
        for d in STEPS:
            mail.start(s_wy[d], wy_out, wy_in.at[d - 1], device((y + d) % 4, z, core))

    def w_back():
        for d in STEPS:
            mail.arrived(s_wy[d], wy_in.at[d - 1], device((y + 4 - d) % 4, z, core))
        at = pl.ds(pl.multiple_of(z * wq, 16), wq)
        total = wsum[at, :]
        for d in STEPS:
            total = total + wy_in[d - 1].astype(F32)
        wfull[at, :] = total.astype(BF16)
        for d in STEPS:
            mail.start(s_wa[d], wfull.at[at], wfull.at[at], device(y, (z + d) % 4, core))

    w_along_y()
    relay(1)
    relay(3)
    w_back()
    relay(2)
    mail.arrived(s_n, normed.at[pl.ds(pl.multiple_of(other * here_rows, 128), here_rows)], sibling)
    for i in range(gath.shape[0]):
        rechunk(i)
    keep[0].start()
    height, breadth = target.shape[0], target.shape[1]
    top_rows, end_rows = pl.ds(0, 2), pl.ds(height - 2, 2)
    lead, trail = pl.ds(0, LEAD), pl.ds(breadth - LEAD, LEAD)
    borders = {
        (1, 0): (target.at[end_rows], t_rows.at[0]),
        (-1, 0): (target.at[top_rows], t_rows.at[1]),
        (0, 1): (target.at[:, trail], t_cols.at[0]),
        (0, -1): (target.at[:, lead], t_cols.at[1]),
        (1, 1): (target.at[end_rows, trail], t_ends.at[0]),
        (1, -1): (target.at[end_rows, lead], t_ends.at[1]),
        (-1, 1): (target.at[top_rows, trail], t_ends.at[2]),
        (-1, -1): (target.at[top_rows, lead], t_ends.at[3]),
    }
    s_border = mail.slots(NEXT)
    for to in NEXT:
        mail.start(s_border[to], *borders[to], tile_peer(*to))

    def multiply(blocks, first=False):
        total = None
        for da, db in blocks:
            at = block(da, db)
            term = dot(nrm[at], gath[at])
            total = term if total is None else total + term
        pre[...] = total if first else pre[...] + total

    def take_b(da, d):
        mail.arrived(s_b[da, d], gath.at[block(da, -d)], peer(0, -d))

    multiply([(0, 0), (3, 0)], first=True)
    multiply([(1, 0), (2, 0)])
    for da in (0, 3, 1, 2):
        take_b(da, 1)
        take_b(da, 3)
        multiply([(da, 3), (da, 1)])
        take_b(da, 2)
        multiply([(da, 2)])

    for d in STEPS:
        frm = (z + 4 - d) % 4
        at = pl.ds(pl.multiple_of(frm * wq, 16), wq)
        mail.arrived(s_wa[d], wfull.at[at], device(y, frm, core))
    fold[...] = jnp.where(grp == 0, wfull[:, :n_out], wfull[:, n_out:])

    n_rows, n_cols = xp.shape[0], xp.shape[1]
    s_part = mail.slot()
    for k in (other, core):
        at = pl.ds(pl.multiple_of(k * here_rows, 128), here_rows)
        value = gelu_tanh(pre[at, :]).astype(BF16)
        act[at, :] = value
        part[k] = dot(value, fold[...]).reshape(part.shape[1:])
        if k is other:
            mail.start(s_part, part.at[other], part_in, sibling)
    own_cols = pl.ds(pl.multiple_of(tile * (n_cols // 4), 16), n_cols // 4)
    part[core, :, own_cols, :] = part[core, :, own_cols, :] + xp[:, own_cols, :]
    keep[1].start()
    mail.arrived(s_part, part_in, sibling)
    total = part[core] + part_in[...]

    edge = jnp.zeros((n_rows // 2, EDGE, 2 * n_out), F32)
    psrc[:, :EDGE, :] = edge
    psrc[:, EDGE + n_cols :, :] = edge
    psrc[:, EDGE : EDGE + n_cols, :] = jnp.concatenate(
        [total[: n_rows // 2], total[n_rows // 2 :]], axis=2
    )
    span = main_in.shape[2]

    def window(dt):
        return pl.ds(pl.multiple_of((tile + dt) % 4 * (n_cols // 4), 8), span)

    s_around = mail.slots(AROUND)
    for ds, dt in AROUND:
        if ds == 0:
            src, dst = psrc.at[:, window(dt)], main_in.at[dt]
        elif ds == -1:
            src, dst = psrc.at[pl.ds(0, 1), window(dt)], edge_in.at[1, dt]
        else:
            src, dst = psrc.at[pl.ds(n_rows // 2 - 1, 1), window(dt)], edge_in.at[0, dt]
        mail.start(s_around[ds, dt], src, dst, tile_peer(ds, dt))
    pre[...] = gelu_slope(pre[...])
    keep[2].start()

    total = psrc[:, window(0), :]
    for dt in range(1, 4):
        mail.arrived(s_around[0, dt], main_in.at[dt], tile_peer(0, -dt))
        total = total + main_in[dt]
    sums[1 : 1 + n_rows // 2] = total[:, :, :n_out]
    sums[1 + n_rows // 2 : 1 + n_rows] = total[:, :, n_out:]
    for i, ds in ((0, 1), (1, -1)):
        total = jnp.zeros(edge_in.shape[3:], F32)
        for dt in range(4):
            mail.arrived(s_around[ds, dt], edge_in.at[i, dt], tile_peer(-ds, -dt))
            total = total + edge_in[i, dt, 0]
        outside = (seq == 0) if i == 0 else (seq == 15)
        total = total[:, n_out:] if i == 0 else total[:, :n_out]
        sums[(n_rows + 1) * i] = jnp.where(outside, 0.0, total)

    for ds, dt in NEXT:
        mail.arrived(s_border[ds, dt], borders[ds, dt][1], tile_peer(-ds, -dt))
    for copy in keep:
        copy.wait()
    mail.finish()


def forward(tokens, shift, scale, gate, projt, fc1, fc2t, lift, conv_a, conv_b, target):
    rows, width = tokens.shape
    hidden = fc1.shape[1]
    depth = (fc1.shape[0] + 15) // 16 * 16
    half = hidden // 2
    n_out = projt.shape[0]
    wide = (depth, 2 * n_out)
    n_blk = 16
    height, breadth, ch = target.shape
    token_rows, n_cols = 4 * rows // 512, 128
    span = n_cols // 4 + 2 * EDGE
    vmem, hbm = pl.BlockSpec(memory_space=VMEM), pl.BlockSpec(memory_space=pl.ANY)
    shape = jax.ShapeDtypeStruct
    return pl.pallas_call(
        forward_kernel,
        out_shape=(
            shape((2 * rows, half), F32),
            shape((2 * rows, half), BF16),
            shape((token_rows + 2, span, n_out), F32),
            shape((half, n_out), BF16),
            shape(wide, F32),
            shape((n_blk, 2 * depth, 2 * rows), BF16),
            shape((36, n_out, ch), BF16),
            shape((3, 3 * ch, ch), BF16),
            shape((2, 2, breadth, ch), BF16),
            shape((2, height, LEAD, ch), BF16),
            shape((4, 2, LEAD, ch), BF16),
        ),
        in_specs=[hbm] + [vmem] * 7 + [hbm] * 3,
        out_specs=(hbm, hbm, vmem, vmem, vmem) + (hbm,) * 6,
        scratch_shapes=[
            VMEM((depth, hidden), BF16),
            VMEM((2,) + wide, F32),
            VMEM((rows, width), BF16),
            VMEM((9, ch, ch), BF16),
            VMEM((9, ch, ch), BF16),
            VMEM((36, n_out, ch), BF16),
            VMEM((3, 3 * ch, ch), BF16),
            VMEM((2 * rows, width), BF16),
            VMEM((n_blk, 2 * rows, 2 * depth), BF16),
            VMEM((n_blk, 2 * depth, 2 * rows), BF16),
            VMEM((n_blk, 2 * depth, half), BF16),
            VMEM(wide, F32),
            VMEM((hidden, 2 * n_out), F32),
            VMEM((half, 2 * n_out), F32),
            VMEM((half, 2 * n_out), F32),
            VMEM((half, 2 * n_out), BF16),
            VMEM((3, half // 4, 2 * n_out), BF16),
            VMEM((half // 4, 2 * n_out), BF16),
            VMEM((3, half // 4, 2 * n_out), BF16),
            VMEM((half, 2 * n_out), BF16),
            VMEM((token_rows, n_cols, n_out), F32),
            VMEM((2 * rows, half), F32),
            VMEM((2 * rows, half), BF16),
            VMEM((2, token_rows, n_cols, n_out), F32),
            VMEM((token_rows, n_cols, n_out), F32),
            VMEM((token_rows // 2, n_cols + 2 * EDGE, 2 * n_out), F32),
            VMEM((4, token_rows // 2, span, 2 * n_out), F32),
            VMEM((2, 4, 1, span, 2 * n_out), F32),
            pltpu.SemaphoreType.DMA((72,)),
            pltpu.SemaphoreType.DMA((72,)),
            pltpu.SemaphoreType.DMA((8,)),
        ],
        compiler_params=pltpu.CompilerParams(
            collective_id=1, has_side_effects=True, vmem_limit_bytes=60 * 2**20
        ),
    )(tokens, shift, scale, gate, projt, fc1, fc2t, lift, conv_a, conv_b, target)


def middle_kernel(
    sums, *refs,
):
    hbm, (latent, lg), refs = refs[:7], refs[7:9], refs[9:]
    kern, target, t_rows, t_cols, t_ends, conv_b, conv_bt = refs[:7]
    patch, f_ref, a_ref, b_ref, acc, want, gf, send, recv, local = refs[7:]
    loads = [
        pltpu.make_async_copy(src, dst, local.at[i])
        for i, (src, dst) in enumerate(zip(hbm, refs))
    ]
    for load in loads:
        load.start()
    grp, seq, tile = lax.axis_index("grp"), lax.axis_index("seq"), lax.axis_index("tile")
    core = seq % 2

    def cores(k, dt):
        return (grp, seq - core + (core + k) % 2, (tile + dt) % 4)

    around = [(k, dt) for k in range(2) for dt in range(4) if (k, dt) != (0, 0)]
    announce([cores(k, dt) for k, dt in around])
    mail = Courier(send, recv)
    n_tok, span, width = sums.shape
    n_rows, here = n_tok - 2, span - 2 * EDGE
    pairs, ch = a_ref.shape[1], a_ref.shape[2] // 4

    height, breadth = target.shape[0], target.shape[1]
    body, lead = slice(LEAD, LEAD + breadth), slice(0, LEAD)
    trail = slice(LEAD + breadth, 2 * LEAD + breadth)
    mid = slice(2, 2 + height)

    def want_at(rows, at, value):
        value = value.astype(F32)
        want[rows, 0, at, :] = value[:, :, :128]
        want[rows, 1, at, :] = value[:, :, 128:]

    for load in loads[1:5]:
        load.wait()
    want_at(mid, body, target[...])
    want_at(slice(0, 2), body, t_rows[0])
    want_at(slice(2 + height, 4 + height), body, t_rows[1])
    for side, at in ((0, lead), (1, trail)):
        want_at(mid, at, t_cols[side])
        want_at(slice(0, 2), at, t_ends[side])
        want_at(slice(2 + height, 4 + height), at, t_ends[2 + side])

    rows = {r: sums[r] for r in range(n_tok)}
    for r in range(n_tok):
        patch[0, r + 1] = pltpu.roll(rows[r], 1, 0).astype(BF16)
        patch[1, r + 1] = rows[r].astype(BF16)
        patch[2, r + 1] = pltpu.roll(rows[r], span - 1, 0).astype(BF16)
    for k in range(3):
        patch[k, 0] = jnp.zeros((span, width), BF16)
        patch[k, n_tok + 1] = jnp.zeros((span, width), BF16)

    loads[0].wait()

    def near(phase):
        return [(d, phase - 4 * d) for d in (-1, 0, 1) if -1 <= phase - 4 * d <= 4]

    for al in range(4):
        for ph in range(4):
            value = None
            for dr, r in near(al):
                for dc, c in near(ph):
                    lhs = patch[1 + dc, 1 + dr : 1 + dr + n_tok].reshape(n_tok * span, width)
                    term = dot(lhs, kern[6 * (r + 1) + c + 1])
                    value = term if value is None else value + term
            value = value.reshape(n_tok, span, ch)
            for tr in range(n_tok):
                at = pl.ds(ph // 2, span, stride=2)
                f_ref[4 * tr + al, ph % 2, 0, at, :] = value[tr, :, :128]
                f_ref[4 * tr + al, ph % 2, 1, at, :] = value[tr, :, 128:]

    def inside(row, b):
        r = seq * height + row
        c = 2 * (tile * breadth // 2 + lax.broadcasted_iota(jnp.int32, (pairs, 1), 0) - EDGE) + b
        return (r >= 0) & (r < 16 * height) & (c >= 0) & (c < 4 * breadth)

    def both(ref, at, rows):
        return jnp.concatenate([ref[*at, 0, rows, :], ref[*at, 1, rows, :]], axis=1)

    def spread(ref, at, v0, v1):
        ref[at, :, 0:ch] = pltpu.roll(v1, 1, 0).astype(BF16)
        ref[at, :, ch : 2 * ch] = v0.astype(BF16)
        ref[at, :, 2 * ch : 3 * ch] = v1.astype(BF16)
        ref[at, :, 3 * ch :] = pltpu.roll(v0, pairs - 1, 0).astype(BF16)

    @pl.loop(0, height + 6)
    def _(i):
        smooth = []
        for b in range(2):
            f = both(f_ref, (i + 1, b), slice(EDGE, EDGE + pairs))
            sigma = jax.nn.sigmoid(f)
            smooth.append(jnp.where(inside(i - 3, b), f * sigma, 0.0))
            slope = sigma * (1.0 + f * (1.0 - sigma))
            f_ref[i + 1, b, 0, EDGE : EDGE + pairs, :] = slope[:, :128]
            f_ref[i + 1, b, 1, EDGE : EDGE + pairs, :] = slope[:, 128:]
        spread(a_ref, i, *smooth)

    def conv(src, weights, out_rows, chunk):
        @pl.loop(0, out_rows // chunk)
        def _(i):
            for b in range(2):
                value = None
                for o in range(3):
                    lhs = src[pl.ds(i * chunk + o, chunk), :, b * ch : (b + 3) * ch]
                    term = dot(lhs.reshape(chunk * pairs, 3 * ch), weights[o])
                    value = term if value is None else value + term
                acc[b, pl.ds(i * chunk, chunk)] = value.reshape(chunk, pairs, ch)

    loads[5].wait()
    conv(a_ref, conv_b, height + 4, (height + 4) // 2)

    @pl.loop(0, height + 4)
    def _(i):
        grad = []
        for b in range(2):
            diff = acc[b, i] - both(want, (i,), pl.ds(b, pairs, stride=2))
            grad.append(jnp.where(inside(i - 2, b), diff, 0.0))
        spread(b_ref, i, *grad)

    loads[6].wait()
    conv(b_ref, conv_bt, height + 2, (height + 2) // 2)

    @pl.loop(0, height + 2)
    def _(i):
        for b in range(2):
            value = acc[b, i] * both(f_ref, (i + 3, b), slice(EDGE, EDGE + pairs))
            value = jnp.where(inside(i - 1, b), value, 0.0)
            gf[i, b, 0], gf[i, b, 1] = value[:, :128], value[:, 128:]

    grad = None
    for r in range(-1, 5):
        for c in range(-1, 5):
            at = pl.ds(EDGE + c // 2, here, stride=2)
            lhs = jnp.concatenate(
                [both(gf, (4 * tr + r + 1, c % 2), at).astype(BF16) for tr in range(n_rows)],
                axis=0,
            )
            term = dot(lhs, kern[6 * (r + 1) + c + 1], NT)
            grad = term if grad is None else grad + term
    grad = grad.reshape(n_rows, here, width)
    latent[...] = grad
    def part_of(k, dt):
        cols = pl.ds(pl.multiple_of((tile + dt) % 4 * here, 16), here)
        return lg.at[pl.ds((core + k) % 2 * n_rows, n_rows), cols]

    cols = pl.ds(pl.multiple_of(tile * here, 16), here)
    lg[pl.ds(core * n_rows, n_rows), cols, :] = grad.astype(BF16)
    await_peers(around)
    s_back = mail.slots(around)
    for k, dt in around:
        mail.start(s_back[k, dt], part_of(0, 0), part_of(0, 0), cores(k, dt))
    for k, dt in around:
        mail.arrived(s_back[k, dt], part_of(k, -dt), cores(k, -dt))
    mail.finish()


def middle(sums, kern, target, t_rows, t_cols, t_ends, conv_b, conv_bt):
    n_tok, span, width = sums.shape
    n_rows, here = n_tok - 2, span - 2 * EDGE
    height, breadth, ch = target.shape
    pairs = breadth // 2 + 2 * EDGE
    vmem, hbm = pl.BlockSpec(memory_space=VMEM), pl.BlockSpec(memory_space=pl.ANY)
    shape = jax.ShapeDtypeStruct
    loaded = (kern, target, t_rows, t_cols, t_ends, conv_b, conv_bt)
    return pl.pallas_call(
        middle_kernel,
        out_shape=(
            shape((n_rows, here, width), F32),
            shape((2 * n_rows, 4 * here, width), BF16),
        ),
        in_specs=[vmem] + [hbm] * len(loaded),
        out_specs=(vmem,) * 2,
        scratch_shapes=[VMEM(x.shape, x.dtype) for x in loaded]
        + [
            VMEM((3, n_rows + 4, span, width), BF16),
            VMEM((height + 8, 2, 2, 2 * span, ch // 2), F32),
            VMEM((height + 6, pairs, 4 * ch), BF16),
            VMEM((height + 4, pairs, 4 * ch), BF16),
            VMEM((2, height + 4, pairs, ch), F32),
            VMEM((height + 4, 2, breadth + 2 * LEAD, ch // 2), F32),
            VMEM((height + 2, 2, 2, pairs, ch // 2), F32),
            pltpu.SemaphoreType.DMA((16,)),
            pltpu.SemaphoreType.DMA((16,)),
            pltpu.SemaphoreType.DMA((len(loaded),)),
        ],
        compiler_params=pltpu.CompilerParams(
            collective_id=3, has_side_effects=True, vmem_limit_bytes=58 * 2**20
        ),
    )(sums, *loaded)


def backward_kernel(
    nrmt_hbm, slope_hbm, act_hbm, fold, lg, gboth, out, two,
    nrmt, slope, act, gpre, st, sz_in, sy_out, sy_in, sfull, b_out, b_in, a_out, a_in, fin, fin_in,
    send, recv, local,
):
    y, z, core, device = place()
    a, b, turn = oriented(y, z, core)
    grp = lax.axis_index("grp")
    other = 1 - core
    sibling = device(y, z, other)
    peers = (
        [sibling]
        + [device((y + d) % 4, z, core) for d in STEPS]
        + [device(y, (z + d) % 4, core) for d in STEPS]
    )
    announce(peers)
    loads = [
        pltpu.make_async_copy(src, dst, local.at[i])
        for i, (src, dst) in enumerate(
            ((act_hbm, act), (slope_hbm, slope), (nrmt_hbm, nrmt))
        )
    ]
    for load in loads:
        load.start()
    mail = Courier(send, recv)
    half = gpre.shape[1]
    rows = nrmt.shape[1] // 2

    def peer(da, db):
        return device(*turn((a + da) % 4, (b + db) % 4), core)

    def block(da, db):
        return block_of(*turn((a + da) % 4, (b + db) % 4))

    def term(da, db):
        return dot(nrmt[block(da, db)], gpre[...])

    s_b = mail.slots((da, d) for da in range(4) for d in STEPS)
    s_a = mail.slots(STEPS)

    def send_b(da):
        for d in (2, 1, 3):
            b_out[da, d - 1] = term(da, d).astype(BF16)
            mail.start(s_b[da, d], b_out.at[da, d - 1], b_in.at[da, d - 1], peer(0, d))

    def sum_b(da):
        total = term(da, 0)
        for d in STEPS:
            mail.arrived(s_b[da, d], b_in.at[da, d - 1], peer(0, -d))
            total = total + b_in[da, d - 1].astype(F32)
        return total

    def send_a(d):
        a_out[d - 1] = sum_b(d).astype(BF16)
        mail.start(s_a[d], a_out.at[d - 1], a_in.at[d - 1], peer(d, 0))

    loads[0].wait()
    st[...] = dot(lg[...], act[...], TN)
    sq = st.shape[0] // 4
    s_sz, s_sy, s_sa = mail.slots(STEPS), mail.slots(STEPS), mail.slots(STEPS)
    await_peers(peers)
    for d in STEPS:
        to = (z + d) % 4
        src = st.at[pl.ds(pl.multiple_of(to * sq, 8), sq)]
        mail.start(s_sz[d], src, sz_in.at[d - 1], device(y, to, core))

    loads[1].wait()
    gpre[...] = (dot(lg[...], fold[...], NT) * slope[...]).astype(BF16)
    loads[2].wait()
    send_b(2)

    for d in STEPS:
        mail.arrived(s_sz[d], sz_in.at[d - 1], device(y, (z + 4 - d) % 4, core))
    s_at = pl.ds(pl.multiple_of(z * sq, 8), sq)
    sy_out[...] = st[s_at, :] + sz_in[0] + sz_in[1] + sz_in[2]
    for d in STEPS:
        mail.start(s_sy[d], sy_out, sy_in.at[d - 1], device((y + d) % 4, z, core))

    send_b(1)
    for d in STEPS:
        mail.arrived(s_sy[d], sy_in.at[d - 1], device((y + 4 - d) % 4, z, core))
    sfull[core, grp, s_at] = sy_out[...] + sy_in[1]
    sfull[core, 1 - grp, s_at] = sy_in[0] + sy_in[2]
    for d in STEPS:
        ref = sfull.at[core, :, s_at]
        mail.start(s_sa[d], ref, ref, device(y, (z + d) % 4, core))
    send_b(3)
    send_b(0)

    send_a(2)
    for d in STEPS:
        frm = (z + 4 - d) % 4
        at = pl.ds(pl.multiple_of(frm * sq, 8), sq)
        mail.arrived(s_sa[d], sfull.at[core, :, at], device(y, frm, core))
    s_ss = mail.slot()
    mail.start(s_ss, sfull.at[core], sfull.at[core], sibling)
    send_a(1)
    send_a(3)

    mail.arrived(s_ss, sfull.at[other], sibling)
    g_high, g_low = split(gboth[...])
    for h in range(2):
        s_high, s_low = split(sfull[h].reshape(-1, half))
        value = dot(g_high, s_high) + dot(g_low, s_high) + dot(g_high, s_low)
        two[:, h * half : (h + 1) * half] = value[: two.shape[0]]

    total = sum_b(0)
    for d in STEPS:
        mail.arrived(s_a[d], a_in.at[d - 1], peer(-d, 0))
        total = total + a_in[d - 1].astype(F32)
    fin[...] = total
    s_fin = mail.slot()
    theirs = pl.ds(pl.multiple_of(other * rows, 16), rows)
    mail.start(s_fin, fin.at[theirs], fin_in, sibling)
    here = out.shape[0]
    mine = fin[pl.ds(pl.multiple_of(core * rows, 16), rows), :]
    out[:, pl.ds(pl.multiple_of(core * half, 128), half)] = mine[:here]
    mail.arrived(s_fin, fin_in, sibling)
    out[:, pl.ds(pl.multiple_of(other * half, 128), half)] = fin_in[:here, :]
    mail.finish()


def backward(nrmt, slope, act, fold, lg, gboth, here):
    n_blk, depth, rows = nrmt.shape
    half = slope.shape[1]
    width = lg.shape[1]
    vmem, hbm = pl.BlockSpec(memory_space=VMEM), pl.BlockSpec(memory_space=pl.ANY)
    shape = jax.ShapeDtypeStruct
    return pl.pallas_call(
        backward_kernel,
        out_shape=(shape((here, 2 * half), F32), shape((here, 2 * half), F32)),
        in_specs=[hbm] * 3 + [vmem] * 3,
        out_specs=(vmem,) * 2,
        scratch_shapes=[
            VMEM(nrmt.shape, BF16),
            VMEM(slope.shape, F32),
            VMEM(act.shape, BF16),
            VMEM((rows, half), BF16),
            VMEM((width, half), F32),
            VMEM((3, width // 4, half), F32),
            VMEM((width // 4, half), F32),
            VMEM((3, width // 4, half), F32),
            VMEM((2, 2, width, half), F32),
            VMEM((4, 3, depth, half), BF16),
            VMEM((4, 3, depth, half), BF16),
            VMEM((3, depth, half), BF16),
            VMEM((3, depth, half), BF16),
            VMEM((depth, half), F32),
            VMEM((depth // 2, half), F32),
            pltpu.SemaphoreType.DMA((32,)),
            pltpu.SemaphoreType.DMA((32,)),
            pltpu.SemaphoreType.DMA((3,)),
        ],
        compiler_params=pltpu.CompilerParams(
            collective_id=2, has_side_effects=True, vmem_limit_bytes=58 * 2**20
        ),
    )(nrmt, slope, act, fold, lg, gboth)


def leave_kernel(*refs):
    for src, dst in zip(refs[:3], refs[3:]):
        dst[...] = src[...]


def leave(*values):
    vmem = pl.BlockSpec(memory_space=VMEM)
    return pl.pallas_call(
        leave_kernel,
        out_shape=tuple(jax.ShapeDtypeStruct(v.shape, v.dtype) for v in values),
        in_specs=[vmem] * 3,
        out_specs=(vmem,) * 3,
    )(*values)


def shards(tokens, shift, scale, gate, fc1, fc2, proj, lift, conv_a, conv_b, target):
    width = tokens.shape[3]
    patch_width = proj.shape[1]

    cols_here = fc2.shape[1]
    ch = conv_a.shape[2]
    slope, act, sums, fold, gboth, nrmt, kern, conv_bt, *borders = forward(
        tokens[0].reshape(-1, width),
        shift,
        scale,
        gate,
        proj.T,
        fc1,
        fc2.T,
        lift,
        conv_a.reshape(9, ch, ch),
        conv_b.reshape(9, ch, ch),
        target[0],
    )
    latent_mine, latent_rows = middle(
        sums, kern, target[0], *borders, conv_b.reshape(3, 3 * ch, ch), conv_bt
    )
    latent_rows = latent_rows.reshape(-1, patch_width)
    grad_one, grad_two = backward(nrmt, slope, act, fold, latent_rows, gboth, cols_here)
    grad_one, grad_two, latent_mine = leave(grad_one, grad_two, latent_mine)
    return (grad_one, grad_two.T, latent_mine[None])


def solution(mesh):
    in_specs = (
        P("grp", "seq", None, None),
        P("grp", None),
        P("grp", None),
        P("grp", None),
        P(("grp", "seq"), "tile"),
        P("tile", ("grp", "seq")),
        P(),
        P(),
        P(),
        P(),
        P("grp", "seq", "tile", None),
    )
    out_specs = (
        P(("grp", "seq"), "tile"),
        P("tile", ("grp", "seq")),
        P("grp", "seq", "tile", None),
    )
    return jax.shard_map(shards, mesh=mesh, in_specs=in_specs, out_specs=out_specs, check_vma=False)
```

```python
import jax
import jax.numpy as jnp
from jax import lax
from jax.experimental import pallas as pl
from jax.experimental.pallas import tpu as pltpu
from jax.sharding import PartitionSpec as P

F32 = jnp.float32
BF16 = jnp.bfloat16
MESH = pl.DeviceIdType.MESH
VMEM = pltpu.VMEM
NT = (((1,), (1,)), ((), ()))
TN = (((0,), (0,)), ((), ()))
EDGE = 8
LEAD = 16
NEXT = [(1, 0), (-1, 0), (0, 1), (0, -1), (1, 1), (1, -1), (-1, 1), (-1, -1)]
AROUND = [(0, 1), (0, 2), (0, 3)] + [(ds, dt) for ds in (-1, 1) for dt in range(4)]
STEPS = (1, 3, 2)


def gelu_tanh(value):
    return jax.nn.gelu(value, approximate=True)


def gelu_slope(x):
    k = 0.7978845608028654
    t = jnp.tanh(k * (x + 0.044715 * x * x * x))
    return 0.5 * (1.0 + t) + 0.5 * x * (1.0 - t * t) * (k + 3 * 0.044715 * k * x * x)


def split(value):
    high = value.astype(BF16)
    return high, (value - high.astype(F32)).astype(BF16)


def dot(lhs, rhs, dims=(((1,), (0,)), ((), ()))):
    return lax.dot_general(lhs, rhs, dims, preferred_element_type=F32)


def place():
    grp, seq, tile = lax.axis_index("grp"), lax.axis_index("seq"), lax.axis_index("tile")
    core = seq % 2
    y = (seq // 2) % 2 * 2 + grp
    z = seq // 4

    def device(y, z, core):
        return (y % 2, z * 4 + y // 2 * 2 + core, tile)

    return y, z, core, device


def oriented(y, z, core):
    a = y + core * (z - y)
    b = z + core * (y - z)

    def turn(a, b):
        return a + core * (b - a), b + core * (a - b)

    return a, b, turn


def block_of(y, z):
    return y % 2 * 8 + z * 2 + y // 2


def tile_peer(ds, dt):
    grp, seq, tile = lax.axis_index("grp"), lax.axis_index("seq"), lax.axis_index("tile")
    return (grp, (seq + ds) % 16, (tile + dt) % 4)


def announce(peers):
    for peer in peers:
        pl.semaphore_signal(
            pltpu.get_barrier_semaphore(), inc=1, device_id=peer, device_id_type=MESH
        )


def await_peers(peers):
    pl.semaphore_wait(pltpu.get_barrier_semaphore(), len(peers))


def greet(peers):
    announce(peers)
    await_peers(peers)


class Courier:
    def __init__(self, send, recv):
        self.send, self.recv, self.used, self.started = send, recv, 0, []

    def slot(self, count=1):
        self.used += count
        return self.used - count

    def slots(self, keys):
        return {key: self.slot() for key in keys}

    def copy(self, slot, src, dst, peer, landing=None):
        return pltpu.make_async_remote_copy(
            src_ref=src,
            dst_ref=dst,
            send_sem=self.send.at[slot],
            recv_sem=self.recv.at[slot if landing is None else landing],
            device_id=peer,
            device_id_type=MESH,
        )

    def start(self, slot, src, dst, peer, landing=None):
        copy = self.copy(slot, src, dst, peer, landing)
        copy.start()
        self.started.append(copy)

    def arrived(self, slot, dst, peer):
        self.copy(slot, dst, dst, peer).wait_recv()

    def finish(self):
        for copy in self.started:
            copy.wait_send()


def pixel_kernels(lift, conv_a):
    lifted = {
        (o, e): dot(lift, conv_a[3 * o + e])
        for o in range(3)
        for e in range(3)
    }

    def reach(pixel, cell):
        return [o for o in range(3) if (pixel + o - 1) // 2 == cell]

    out = {}
    for r in range(-1, 5):
        for c in range(-1, 5):
            parts = []
            for a in range(2):
                for b in range(2):
                    total = jnp.zeros_like(lifted[0, 0])
                    for o in reach(r, a):
                        for e in reach(c, b):
                            total = total + lifted[o, e]
                    parts.append(total)
            out[r, c] = jnp.concatenate(parts, axis=0)
    return out


def forward_kernel(
    tokens_hbm, shift, scale, gate, projt, fc1_own, fc2t, lift, conv_a_hbm, conv_b_hbm, target_hbm,
    slope_hbm, act_hbm, sums, fold, gboth, nrmt_hbm, kern_hbm, conv_bt_hbm,
    want_hbm,
    t_rows, t_cols, t_ends, want, target, fc1, gps, tokens, conv_a, conv_b, kern, conv_bt, normed, nrm, nrmt, gath, gin, wpart, wsib, wsum, wz_out, wz_in, wy_out, wy_in, wfull, xp,
    pre, act, part, part_in, psrc, main_in, edge_in, send, recv, local,
):
    y, z, core, device = place()
    a, b, turn = oriented(y, z, core)
    grp, tile = lax.axis_index("grp"), lax.axis_index("tile")
    other = 1 - core
    sibling = device(y, z, other)
    peers = (
        [sibling]
        + [device((y + d) % 4, z, k) for d in STEPS for k in range(2)]
        + [device(y, (z + d) % 4, k) for d in STEPS for k in range(2)]
        + [tile_peer(ds, dt) for ds, dt in AROUND]
    )
    announce(peers)
    loads = [
        pltpu.make_async_copy(src, dst, local.at[i])
        for i, (src, dst) in enumerate(
            (
                (tokens_hbm, tokens),
                (conv_a_hbm, conv_a),
                (conv_b_hbm, conv_b),
                (target_hbm, target),
            )
        )
    ]
    for load in loads:
        load.start()
    mail = Courier(send, recv)
    rows, half = gath.shape[1] // 2, gath.shape[2]
    here_rows, width = tokens.shape
    cols = fc2t.shape[0]
    last = cols // 16 * 16
    fc1[:last] = fc1_own[:last]
    tail = jnp.concatenate(
        [fc1_own[last:].astype(F32), jnp.zeros((rows - cols, 2 * half), F32)], axis=0
    )
    fc1[last:] = tail.astype(BF16)

    n_out = projt.shape[0]
    seq = lax.axis_index("seq")
    for i, g in enumerate((grp, 1 - grp)):
        start = (g * 16 + seq) * cols
        first = jnp.minimum(start // 128 * 128, width - 256)
        at = pl.ds(pl.multiple_of(first, 128), 256)
        high, low = split(gate[:, at] * projt[:, at].astype(F32))
        r = lax.broadcasted_iota(jnp.int32, (rows, 256), 0)
        k = lax.broadcasted_iota(jnp.int32, (rows, 256), 1)
        pick = jnp.where((k == r + (start - first)) & (r < cols), 1.0, 0.0).astype(BF16)
        value = dot(pick, high, NT) + dot(pick, low, NT)
        zero = jnp.zeros_like(value)
        gps[i] = jnp.concatenate(
            [jnp.where(grp == 0, value, zero), jnp.where(grp == 1, value, zero)], axis=1
        )
    await_peers(peers)

    def peer(da, db):
        return device(*turn((a + da) % 4, (b + db) % 4), core)

    def block(da, db):
        return block_of(*turn((a + da) % 4, (b + db) % 4))

    own = block(0, 0)
    mine = pl.ds(pl.multiple_of(core * rows, 16), rows)
    theirs = pl.ds(pl.multiple_of(other * rows, 16), rows)
    s_a = mail.slots((h, d) for h in range(2) for d in STEPS)
    r_a = {d: mail.slot(2) for d in STEPS}
    s_gate, s_own = mail.slot(), mail.slot()
    partner = device(y // 2 * 2 + 1 - grp, z, core)
    mail.start(s_gate, gps.at[1], gin, partner)
    src = fc1.at[:, pl.ds(pl.multiple_of(other * half, 128), half)]
    mail.start(s_own, src, gath.at[own, mine], sibling)
    for d in STEPS:
        for h in range(2):
            to = device((y + d) % 4, z, 0) if h == 0 else device(y, (z + d) % 4, 1)
            src = fc1.at[:, h * half : (h + 1) * half]
            mail.start(s_a[h, d], src, gath.at[own, mine], to, r_a[d] + core)
    gath[own, mine, :] = fc1[:, pl.ds(pl.multiple_of(core * half, 128), half)]

    loads[0].wait()

    def normalise(i):
        x = tokens[pl.ds(pl.multiple_of(i * 64, 64), 64), :].astype(F32)
        center = x - jnp.mean(x, axis=1, keepdims=True)
        spread = jnp.mean(center * center, axis=1, keepdims=True)
        value = center * lax.rsqrt(spread + 1e-06) * (1.0 + scale[...]) + shift[...]
        at = pl.ds(pl.multiple_of(core * here_rows + i * 64, 64), 64)
        normed[at, :] = value.astype(BF16)

    s_b = mail.slots((da, d) for da in range(4) for d in STEPS)

    def put_b(da):
        ref = gath.at[block(da, 0)]
        for d in STEPS:
            mail.start(s_b[da, d], ref, ref, peer(0, d))

    n_steps = here_rows // 64
    pl.loop(0, n_steps // 2)(normalise)
    mail.arrived(s_own, gath.at[own, theirs], sibling)
    put_b(0)
    pl.loop(n_steps // 2, n_steps)(normalise)
    blk_rows = pl.ds(pl.multiple_of(core * here_rows, 128), here_rows)
    s_n = mail.slot()
    mail.start(s_n, normed.at[blk_rows], normed.at[blk_rows], sibling)

    mail.arrived(s_gate, gin, partner)
    both = gps[0] + gin[...]
    gboth[...] = both
    high, low = split(both[:cols])
    wpart[...] = dot(fc2t[...], high, TN) + dot(fc2t[...], low, TN)
    wq = half // 4
    s_w = mail.slot()
    mail.start(s_w, wpart.at[pl.ds(pl.multiple_of(other * half, 16), half)], wsib, sibling)

    def window_of(i):
        first = 2 * cols * i // 128 * 128
        off = 2 * cols * i - first
        span = 256 if off + 2 * cols <= 256 else 384
        r = lax.broadcasted_iota(jnp.int32, (2 * rows, span), 0)
        k = lax.broadcasted_iota(jnp.int32, (2 * rows, span), 1)
        low_part = (k == r + off) & (r < cols)
        high_part = (k == r + (off + cols - rows)) & (r >= rows) & (r < rows + cols)
        pick = jnp.where(low_part | high_part, 1.0, 0.0).astype(BF16)
        return normed[:, first : first + span], pick

    def rechunk(i):
        value, pick = window_of(i)
        nrm[i] = dot(value, pick, NT).astype(BF16)

    def rechunk_turned(indices):
        for i in indices:
            value, pick = window_of(i)
            nrmt[i] = dot(pick, value, NT).astype(BF16)

    mail.arrived(s_w, wsib, sibling)
    wsum[...] = wpart[pl.ds(pl.multiple_of(core * half, 16), half), :] + wsib[...]
    wz_out[...] = wsum[...].astype(BF16)
    s_wz, s_wy, s_wa = mail.slots(STEPS), mail.slots(STEPS), mail.slots(STEPS)
    for d in STEPS:
        to = (z + d) % 4
        src = wz_out.at[pl.ds(pl.multiple_of(to * wq, 16), wq)]
        mail.start(s_wz[d], src, wz_in.at[d - 1], device(y, to, core))

    keep = [
        pltpu.make_async_copy(src, dst, local.at[4 + i])
        for i, (src, dst) in enumerate(
            (
                (nrmt, nrmt_hbm),
                (act, act_hbm),
                (pre, slope_hbm),
                (kern, kern_hbm),
                (conv_bt, conv_bt_hbm),
                (want, want_hbm),
            )
        )
    ]
    loads[1].wait()
    kernels = pixel_kernels(lift[...], conv_a)
    for i, value in enumerate(kernels.values()):
        kern[i] = value.astype(BF16)
    keep[3].start()

    def relay(d):
        at = block(-d, 0)
        frm = turn((a + 4 - d) % 4, b)
        for k in range(2):
            landed = gath.at[at, pl.ds(k * rows, rows)]
            mail.arrived(r_a[d] + k, landed, device(*frm, k))
        put_b((4 - d) % 4)

    def w_along_y():
        for d in STEPS:
            mail.arrived(s_wz[d], wz_in.at[d - 1], device(y, (z + 4 - d) % 4, core))
        here = pl.ds(pl.multiple_of(z * wq, 16), wq)
        total = wsum[here, :]
        for d in STEPS:
            total = total + wz_in[d - 1].astype(F32)
        wsum[here, :] = total
        wy_out[...] = total.astype(BF16)
        for d in STEPS:
            mail.start(s_wy[d], wy_out, wy_in.at[d - 1], device((y + d) % 4, z, core))

    def w_back():
        for d in STEPS:
            mail.arrived(s_wy[d], wy_in.at[d - 1], device((y + 4 - d) % 4, z, core))
        at = pl.ds(pl.multiple_of(z * wq, 16), wq)
        total = wsum[at, :]
        for d in STEPS:
            total = total + wy_in[d - 1].astype(F32)
        wfull[at, :] = total.astype(BF16)
        for d in STEPS:
            mail.start(s_wa[d], wfull.at[at], wfull.at[at], device(y, (z + d) % 4, core))

    relay(1)
    relay(3)
    w_along_y()
    mail.arrived(s_n, normed.at[pl.ds(pl.multiple_of(other * here_rows, 128), here_rows)], sibling)
    for i in range(gath.shape[0]):
        rechunk(i)
    relay(2)
    loads[3].wait()
    height, breadth = target.shape[0], target.shape[1]
    top_rows, end_rows = pl.ds(0, 2), pl.ds(height - 2, 2)
    lead, trail = pl.ds(0, LEAD), pl.ds(breadth - LEAD, LEAD)
    borders = {
        (1, 0): (target.at[end_rows], t_rows.at[0]),
        (-1, 0): (target.at[top_rows], t_rows.at[1]),
        (0, 1): (target.at[:, trail], t_cols.at[0]),
        (0, -1): (target.at[:, lead], t_cols.at[1]),
        (1, 1): (target.at[end_rows, trail], t_ends.at[0]),
        (1, -1): (target.at[end_rows, lead], t_ends.at[1]),
        (-1, 1): (target.at[top_rows, trail], t_ends.at[2]),
        (-1, -1): (target.at[top_rows, lead], t_ends.at[3]),
    }
    s_border = mail.slots(NEXT)
    for to in NEXT:
        mail.start(s_border[to], *borders[to], tile_peer(*to))

    def multiply(blocks, first=False):
        total = None
        for da, db in blocks:
            at = block(da, db)
            term = dot(nrm[at], gath[at])
            total = term if total is None else total + term
        pre[...] = total if first else pre[...] + total

    def take_b(da, d):
        mail.arrived(s_b[da, d], gath.at[block(da, -d)], peer(0, -d))

    multiply([(0, 0), (3, 0)], first=True)
    multiply([(1, 0), (2, 0)])
    for da in (0, 3, 1, 2):
        take_b(da, 1)
        take_b(da, 3)
        multiply([(da, 3), (da, 1)])
        take_b(da, 2)
        multiply([(da, 2)])
        if da == 0:
            rechunk_turned(range(0, 5))
            w_back()
        elif da == 3:
            rechunk_turned(range(5, 8))
            loads[2].wait()
            ch = conv_b.shape[2]
            for o in range(3):
                for e in range(3):
                    conv_bt[o, e * ch : (e + 1) * ch, :] = conv_b[8 - 3 * o - e].T
            keep[4].start()
            xp[...] = dot(tokens[...], projt[...], NT).reshape(xp.shape)

    for d in STEPS:
        frm = (z + 4 - d) % 4
        at = pl.ds(pl.multiple_of(frm * wq, 16), wq)
        mail.arrived(s_wa[d], wfull.at[at], device(y, frm, core))
    fold[...] = jnp.where(grp == 0, wfull[:, :n_out], wfull[:, n_out:])

    n_rows, n_cols = xp.shape[0], xp.shape[1]
    s_part = mail.slot()
    for k in (other, core):
        at = pl.ds(pl.multiple_of(k * here_rows, 128), here_rows)
        value = gelu_tanh(pre[at, :]).astype(BF16)
        act[at, :] = value
        part[k] = dot(value, fold[...]).reshape(part.shape[1:])
        if k is other:
            mail.start(s_part, part.at[other], part_in, sibling)
    own_cols = pl.ds(pl.multiple_of(tile * (n_cols // 4), 16), n_cols // 4)
    part[core, :, own_cols, :] = part[core, :, own_cols, :] + xp[:, own_cols, :]
    keep[1].start()
    mail.arrived(s_part, part_in, sibling)
    total = part[core] + part_in[...]

    edge = jnp.zeros((n_rows // 2, EDGE, 2 * n_out), F32)
    psrc[:, :EDGE, :] = edge
    psrc[:, EDGE + n_cols :, :] = edge
    psrc[:, EDGE : EDGE + n_cols, :] = jnp.concatenate(
        [total[: n_rows // 2], total[n_rows // 2 :]], axis=2
    )
    span = main_in.shape[2]

    def window(dt):
        return pl.ds(pl.multiple_of((tile + dt) % 4 * (n_cols // 4), 8), span)

    s_around = mail.slots(AROUND)
    for ds, dt in AROUND:
        if ds == 0:
            src, dst = psrc.at[:, window(dt)], main_in.at[dt]
        elif ds == -1:
            src, dst = psrc.at[pl.ds(0, 1), window(dt)], edge_in.at[1, dt]
        else:
            src, dst = psrc.at[pl.ds(n_rows // 2 - 1, 1), window(dt)], edge_in.at[0, dt]
        mail.start(s_around[ds, dt], src, dst, tile_peer(ds, dt))
    pre[...] = gelu_slope(pre[...])
    keep[2].start()
    rechunk_turned(range(8, 16))
    keep[0].start()

    for ds, dt in NEXT:
        mail.arrived(s_border[ds, dt], borders[ds, dt][1], tile_peer(-ds, -dt))
    body, first_cols = slice(LEAD, LEAD + breadth), slice(0, LEAD)
    last_cols = slice(LEAD + breadth, 2 * LEAD + breadth)
    inner, under = slice(2, 2 + height), slice(2 + height, 4 + height)

    def want_at(rows, at, value):
        value = value.astype(F32)
        want[rows, 0, at, :] = value[:, :, :128]
        want[rows, 1, at, :] = value[:, :, 128:]

    want_at(inner, body, target[...])
    want_at(slice(0, 2), body, t_rows[0])
    want_at(under, body, t_rows[1])
    for side, at in ((0, first_cols), (1, last_cols)):
        want_at(inner, at, t_cols[side])
        want_at(slice(0, 2), at, t_ends[side])
        want_at(under, at, t_ends[2 + side])
    keep[5].start()

    total = psrc[:, window(0), :]
    for dt in range(1, 4):
        mail.arrived(s_around[0, dt], main_in.at[dt], tile_peer(0, -dt))
        total = total + main_in[dt]
    sums[1 : 1 + n_rows // 2] = total[:, :, :n_out]
    sums[1 + n_rows // 2 : 1 + n_rows] = total[:, :, n_out:]
    for i, ds in ((0, 1), (1, -1)):
        total = jnp.zeros(edge_in.shape[3:], F32)
        for dt in range(4):
            mail.arrived(s_around[ds, dt], edge_in.at[i, dt], tile_peer(-ds, -dt))
            total = total + edge_in[i, dt, 0]
        outside = (seq == 0) if i == 0 else (seq == 15)
        total = total[:, n_out:] if i == 0 else total[:, :n_out]
        sums[(n_rows + 1) * i] = jnp.where(outside, 0.0, total)

    for copy in keep:
        copy.wait()
    mail.finish()


def forward(tokens, shift, scale, gate, projt, fc1, fc2t, lift, conv_a, conv_b, target):
    rows, width = tokens.shape
    hidden = fc1.shape[1]
    depth = (fc1.shape[0] + 15) // 16 * 16
    half = hidden // 2
    n_out = projt.shape[0]
    wide = (depth, 2 * n_out)
    n_blk = 16
    height, breadth, ch = target.shape
    token_rows, n_cols = 4 * rows // 512, 128
    span = n_cols // 4 + 2 * EDGE
    vmem, hbm = pl.BlockSpec(memory_space=VMEM), pl.BlockSpec(memory_space=pl.ANY)
    shape = jax.ShapeDtypeStruct
    return pl.pallas_call(
        forward_kernel,
        out_shape=(
            shape((2 * rows, half), F32),
            shape((2 * rows, half), BF16),
            shape((token_rows + 2, span, n_out), F32),
            shape((half, n_out), BF16),
            shape(wide, F32),
            shape((n_blk, 2 * depth, 2 * rows), BF16),
            shape((36, n_out, ch), BF16),
            shape((3, 3 * ch, ch), BF16),
            shape((height + 4, 2, breadth + 2 * LEAD, ch // 2), F32),
        ),
        in_specs=[hbm] + [vmem] * 7 + [hbm] * 3,
        out_specs=(hbm, hbm, vmem, vmem, vmem) + (hbm,) * 4,
        scratch_shapes=[
            VMEM((2, 2, breadth, ch), BF16),
            VMEM((2, height, LEAD, ch), BF16),
            VMEM((4, 2, LEAD, ch), BF16),
            VMEM((height + 4, 2, breadth + 2 * LEAD, ch // 2), F32),
            VMEM((height, breadth, ch), BF16),
            VMEM((depth, hidden), BF16),
            VMEM((2,) + wide, F32),
            VMEM((rows, width), BF16),
            VMEM((9, ch, ch), BF16),
            VMEM((9, ch, ch), BF16),
            VMEM((36, n_out, ch), BF16),
            VMEM((3, 3 * ch, ch), BF16),
            VMEM((2 * rows, width), BF16),
            VMEM((n_blk, 2 * rows, 2 * depth), BF16),
            VMEM((n_blk, 2 * depth, 2 * rows), BF16),
            VMEM((n_blk, 2 * depth, half), BF16),
            VMEM(wide, F32),
            VMEM((hidden, 2 * n_out), F32),
            VMEM((half, 2 * n_out), F32),
            VMEM((half, 2 * n_out), F32),
            VMEM((half, 2 * n_out), BF16),
            VMEM((3, half // 4, 2 * n_out), BF16),
            VMEM((half // 4, 2 * n_out), BF16),
            VMEM((3, half // 4, 2 * n_out), BF16),
            VMEM((half, 2 * n_out), BF16),
            VMEM((token_rows, n_cols, n_out), F32),
            VMEM((2 * rows, half), F32),
            VMEM((2 * rows, half), BF16),
            VMEM((2, token_rows, n_cols, n_out), F32),
            VMEM((token_rows, n_cols, n_out), F32),
            VMEM((token_rows // 2, n_cols + 2 * EDGE, 2 * n_out), F32),
            VMEM((4, token_rows // 2, span, 2 * n_out), F32),
            VMEM((2, 4, 1, span, 2 * n_out), F32),
            pltpu.SemaphoreType.DMA((72,)),
            pltpu.SemaphoreType.DMA((72,)),
            pltpu.SemaphoreType.DMA((10,)),
        ],
        compiler_params=pltpu.CompilerParams(
            collective_id=1, has_side_effects=True, vmem_limit_bytes=60 * 2**20
        ),
    )(tokens, shift, scale, gate, projt, fc1, fc2t, lift, conv_a, conv_b, target)


def middle_kernel(
    sums, *refs,
):
    hbm, (latent, lg), refs = refs[:4], refs[4:6], refs[6:]
    kern, want, conv_b, conv_bt = refs[:4]
    patch, f_ref, a_ref, b_ref, acc, gf, send, recv, local = refs[4:]
    loads = [
        pltpu.make_async_copy(src, dst, local.at[i])
        for i, (src, dst) in enumerate(zip(hbm, refs))
    ]
    for load in loads:
        load.start()
    grp, seq, tile = lax.axis_index("grp"), lax.axis_index("seq"), lax.axis_index("tile")
    core = seq % 2

    def cores(k, dt):
        return (grp, seq - core + (core + k) % 2, (tile + dt) % 4)

    around = [(k, dt) for k in range(2) for dt in range(4) if (k, dt) != (0, 0)]
    announce([cores(k, dt) for k, dt in around])
    mail = Courier(send, recv)
    n_tok, span, width = sums.shape
    n_rows, here = n_tok - 2, span - 2 * EDGE
    pairs, ch = a_ref.shape[1], a_ref.shape[2] // 4

    rows = {r: sums[r] for r in range(n_tok)}
    height, breadth = f_ref.shape[0] - 8, 4 * here
    for r in range(n_tok):
        patch[0, r + 1] = pltpu.roll(rows[r], 1, 0).astype(BF16)
        patch[1, r + 1] = rows[r].astype(BF16)
        patch[2, r + 1] = pltpu.roll(rows[r], span - 1, 0).astype(BF16)
    for k in range(3):
        patch[k, 0] = jnp.zeros((span, width), BF16)
        patch[k, n_tok + 1] = jnp.zeros((span, width), BF16)

    loads[0].wait()

    def near(phase):
        return [(d, phase - 4 * d) for d in (-1, 0, 1) if -1 <= phase - 4 * d <= 4]

    for al in range(4):
        for ph in range(4):
            value = None
            for dr, r in near(al):
                for dc, c in near(ph):
                    lhs = patch[1 + dc, 1 + dr : 1 + dr + n_tok].reshape(n_tok * span, width)
                    term = dot(lhs, kern[6 * (r + 1) + c + 1])
                    value = term if value is None else value + term
            value = value.reshape(n_tok, span, ch)
            for tr in range(n_tok):
                at = pl.ds(ph // 2, span, stride=2)
                f_ref[4 * tr + al, ph % 2, 0, at, :] = value[tr, :, :128]
                f_ref[4 * tr + al, ph % 2, 1, at, :] = value[tr, :, 128:]

    def inside(row, b):
        r = seq * height + row
        c = 2 * (tile * breadth // 2 + lax.broadcasted_iota(jnp.int32, (pairs, 1), 0) - EDGE) + b
        return (r >= 0) & (r < 16 * height) & (c >= 0) & (c < 4 * breadth)

    def both(ref, at, rows):
        return jnp.concatenate([ref[*at, 0, rows, :], ref[*at, 1, rows, :]], axis=1)

    def spread(ref, at, v0, v1):
        ref[at, :, 0:ch] = pltpu.roll(v1, 1, 0).astype(BF16)
        ref[at, :, ch : 2 * ch] = v0.astype(BF16)
        ref[at, :, 2 * ch : 3 * ch] = v1.astype(BF16)
        ref[at, :, 3 * ch :] = pltpu.roll(v0, pairs - 1, 0).astype(BF16)

    @pl.loop(0, height + 6)
    def _(i):
        smooth = []
        for b in range(2):
            f = both(f_ref, (i + 1, b), slice(EDGE, EDGE + pairs))
            sigma = jax.nn.sigmoid(f)
            smooth.append(jnp.where(inside(i - 3, b), f * sigma, 0.0))
            slope = sigma * (1.0 + f * (1.0 - sigma))
            f_ref[i + 1, b, 0, EDGE : EDGE + pairs, :] = slope[:, :128]
            f_ref[i + 1, b, 1, EDGE : EDGE + pairs, :] = slope[:, 128:]
        spread(a_ref, i, *smooth)

    def conv(src, weights, out_rows, chunk):
        @pl.loop(0, out_rows // chunk)
        def _(i):
            for b in range(2):
                value = None
                for o in range(3):
                    lhs = src[pl.ds(i * chunk + o, chunk), :, b * ch : (b + 3) * ch]
                    term = dot(lhs.reshape(chunk * pairs, 3 * ch), weights[o])
                    value = term if value is None else value + term
                acc[b, pl.ds(i * chunk, chunk)] = value.reshape(chunk, pairs, ch)

    loads[2].wait()
    conv(a_ref, conv_b, height + 4, (height + 4) // 2)
    loads[1].wait()

    @pl.loop(0, height + 4)
    def _(i):
        grad = []
        for b in range(2):
            diff = acc[b, i] - both(want, (i,), pl.ds(b, pairs, stride=2))
            grad.append(jnp.where(inside(i - 2, b), diff, 0.0))
        spread(b_ref, i, *grad)

    loads[3].wait()
    conv(b_ref, conv_bt, height + 2, (height + 2) // 2)

    @pl.loop(0, height + 2)
    def _(i):
        for b in range(2):
            value = acc[b, i] * both(f_ref, (i + 3, b), slice(EDGE, EDGE + pairs))
            value = jnp.where(inside(i - 1, b), value, 0.0)
            gf[i, b, 0], gf[i, b, 1] = value[:, :128], value[:, 128:]

    grad = None
    for r in range(-1, 5):
        for c in range(-1, 5):
            at = pl.ds(EDGE + c // 2, here, stride=2)
            lhs = jnp.concatenate(
                [both(gf, (4 * tr + r + 1, c % 2), at).astype(BF16) for tr in range(n_rows)],
                axis=0,
            )
            term = dot(lhs, kern[6 * (r + 1) + c + 1], NT)
            grad = term if grad is None else grad + term
    grad = grad.reshape(n_rows, here, width)
    latent[...] = grad
    def part_of(k, dt):
        cols = pl.ds(pl.multiple_of((tile + dt) % 4 * here, 16), here)
        return lg.at[pl.ds((core + k) % 2 * n_rows, n_rows), cols]

    cols = pl.ds(pl.multiple_of(tile * here, 16), here)
    lg[pl.ds(core * n_rows, n_rows), cols, :] = grad.astype(BF16)
    await_peers(around)
    s_back = mail.slots(around)
    for k, dt in around:
        mail.start(s_back[k, dt], part_of(0, 0), part_of(0, 0), cores(k, dt))
    for k, dt in around:
        mail.arrived(s_back[k, dt], part_of(k, -dt), cores(k, -dt))
    mail.finish()


def middle(sums, kern, want, conv_b, conv_bt):
    n_tok, span, width = sums.shape
    n_rows, here = n_tok - 2, span - 2 * EDGE
    height, breadth, ch = want.shape[0] - 4, 4 * here, conv_bt.shape[2]
    pairs = breadth // 2 + 2 * EDGE
    vmem, hbm = pl.BlockSpec(memory_space=VMEM), pl.BlockSpec(memory_space=pl.ANY)
    shape = jax.ShapeDtypeStruct
    loaded = (kern, want, conv_b, conv_bt)
    return pl.pallas_call(
        middle_kernel,
        out_shape=(
            shape((n_rows, here, width), F32),
            shape((2 * n_rows, 4 * here, width), BF16),
        ),
        in_specs=[vmem] + [hbm] * len(loaded),
        out_specs=(vmem,) * 2,
        scratch_shapes=[VMEM(x.shape, x.dtype) for x in loaded]
        + [
            VMEM((3, n_rows + 4, span, width), BF16),
            VMEM((height + 8, 2, 2, 2 * span, ch // 2), F32),
            VMEM((height + 6, pairs, 4 * ch), BF16),
            VMEM((height + 4, pairs, 4 * ch), BF16),
            VMEM((2, height + 4, pairs, ch), F32),
            VMEM((height + 2, 2, 2, pairs, ch // 2), F32),
            pltpu.SemaphoreType.DMA((16,)),
            pltpu.SemaphoreType.DMA((16,)),
            pltpu.SemaphoreType.DMA((len(loaded),)),
        ],
        compiler_params=pltpu.CompilerParams(
            collective_id=3, has_side_effects=True, vmem_limit_bytes=58 * 2**20
        ),
    )(sums, *loaded)


def backward_kernel(
    nrmt_hbm, slope_hbm, act_hbm, fold, lg, gboth, out, two,
    nrmt, slope, act, gpre, st, sz_in, sy_out, sy_in, sfull, b_out, b_in, a_out, a_in, fin, fin_in,
    send, recv, local,
):
    y, z, core, device = place()
    a, b, turn = oriented(y, z, core)
    grp = lax.axis_index("grp")
    other = 1 - core
    sibling = device(y, z, other)
    peers = (
        [sibling]
        + [device((y + d) % 4, z, core) for d in STEPS]
        + [device(y, (z + d) % 4, core) for d in STEPS]
    )
    announce(peers)
    loads = [
        pltpu.make_async_copy(src, dst, local.at[i])
        for i, (src, dst) in enumerate(
            ((act_hbm, act), (slope_hbm, slope), (nrmt_hbm, nrmt))
        )
    ]
    for load in loads:
        load.start()
    mail = Courier(send, recv)
    half = gpre.shape[1]
    rows = nrmt.shape[1] // 2

    def peer(da, db):
        return device(*turn((a + da) % 4, (b + db) % 4), core)

    def block(da, db):
        return block_of(*turn((a + da) % 4, (b + db) % 4))

    def term(da, db):
        return dot(nrmt[block(da, db)], gpre[...])

    s_b = mail.slots((da, d) for da in range(4) for d in STEPS)
    s_a = mail.slots(STEPS)

    def send_b(da):
        for d in (2, 1, 3):
            b_out[da, d - 1] = term(da, d).astype(BF16)
            mail.start(s_b[da, d], b_out.at[da, d - 1], b_in.at[da, d - 1], peer(0, d))

    def sum_b(da):
        total = term(da, 0)
        for d in STEPS:
            mail.arrived(s_b[da, d], b_in.at[da, d - 1], peer(0, -d))
            total = total + b_in[da, d - 1].astype(F32)
        return total

    def send_a(d):
        a_out[d - 1] = sum_b(d).astype(BF16)
        mail.start(s_a[d], a_out.at[d - 1], a_in.at[d - 1], peer(d, 0))

    loads[0].wait()
    st[...] = dot(lg[...], act[...], TN).astype(BF16)
    sq = st.shape[0] // 4
    s_sz, s_sy, s_sa = mail.slots(STEPS), mail.slots(STEPS), mail.slots(STEPS)
    await_peers(peers)
    for d in STEPS:
        to = (z + d) % 4
        src = st.at[pl.ds(pl.multiple_of(to * sq, 16), sq)]
        mail.start(s_sz[d], src, sz_in.at[d - 1], device(y, to, core))

    loads[1].wait()
    gpre[...] = (dot(lg[...], fold[...], NT) * slope[...]).astype(BF16)
    loads[2].wait()
    send_b(2)

    for d in STEPS:
        mail.arrived(s_sz[d], sz_in.at[d - 1], device(y, (z + 4 - d) % 4, core))
    s_at = pl.ds(pl.multiple_of(z * sq, 16), sq)
    total = st[s_at, :].astype(F32)
    for d in STEPS:
        total = total + sz_in[d - 1].astype(F32)
    sy_out[...] = total.astype(BF16)
    for d in STEPS:
        mail.start(s_sy[d], sy_out, sy_in.at[d - 1], device((y + d) % 4, z, core))

    send_b(1)
    for d in STEPS:
        mail.arrived(s_sy[d], sy_in.at[d - 1], device((y + 4 - d) % 4, z, core))
    sfull[core, grp, s_at] = (total + sy_in[1].astype(F32)).astype(BF16)
    sfull[core, 1 - grp, s_at] = (sy_in[0].astype(F32) + sy_in[2].astype(F32)).astype(BF16)
    for d in STEPS:
        ref = sfull.at[core, :, s_at]
        mail.start(s_sa[d], ref, ref, device(y, (z + d) % 4, core))
    send_b(3)
    send_b(0)

    send_a(2)
    for d in STEPS:
        frm = (z + 4 - d) % 4
        at = pl.ds(pl.multiple_of(frm * sq, 16), sq)
        mail.arrived(s_sa[d], sfull.at[core, :, at], device(y, frm, core))
    s_ss = mail.slot()
    mail.start(s_ss, sfull.at[core], sfull.at[core], sibling)
    send_a(1)
    send_a(3)

    mail.arrived(s_ss, sfull.at[other], sibling)
    g_high, g_low = split(gboth[...])
    for h in range(2):
        sums = sfull[h].reshape(-1, half)
        value = dot(g_high, sums) + dot(g_low, sums)
        two[:, h * half : (h + 1) * half] = value[: two.shape[0]]

    total = sum_b(0)
    for d in STEPS:
        mail.arrived(s_a[d], a_in.at[d - 1], peer(-d, 0))
        total = total + a_in[d - 1].astype(F32)
    fin[...] = total
    s_fin = mail.slot()
    theirs = pl.ds(pl.multiple_of(other * rows, 16), rows)
    mail.start(s_fin, fin.at[theirs], fin_in, sibling)
    here = out.shape[0]
    mine = fin[pl.ds(pl.multiple_of(core * rows, 16), rows), :]
    out[:, pl.ds(pl.multiple_of(core * half, 128), half)] = mine[:here]
    mail.arrived(s_fin, fin_in, sibling)
    out[:, pl.ds(pl.multiple_of(other * half, 128), half)] = fin_in[:here, :]
    mail.finish()


def backward(nrmt, slope, act, fold, lg, gboth, here):
    n_blk, depth, rows = nrmt.shape
    half = slope.shape[1]
    width = lg.shape[1]
    vmem, hbm = pl.BlockSpec(memory_space=VMEM), pl.BlockSpec(memory_space=pl.ANY)
    shape = jax.ShapeDtypeStruct
    return pl.pallas_call(
        backward_kernel,
        out_shape=(shape((here, 2 * half), F32), shape((here, 2 * half), F32)),
        in_specs=[hbm] * 3 + [vmem] * 3,
        out_specs=(vmem,) * 2,
        scratch_shapes=[
            VMEM(nrmt.shape, BF16),
            VMEM(slope.shape, F32),
            VMEM(act.shape, BF16),
            VMEM((rows, half), BF16),
            VMEM((width, half), BF16),
            VMEM((3, width // 4, half), BF16),
            VMEM((width // 4, half), BF16),
            VMEM((3, width // 4, half), BF16),
            VMEM((2, 2, width, half), BF16),
            VMEM((4, 3, depth, half), BF16),
            VMEM((4, 3, depth, half), BF16),
            VMEM((3, depth, half), BF16),
            VMEM((3, depth, half), BF16),
            VMEM((depth, half), F32),
            VMEM((depth // 2, half), F32),
            pltpu.SemaphoreType.DMA((32,)),
            pltpu.SemaphoreType.DMA((32,)),
            pltpu.SemaphoreType.DMA((3,)),
        ],
        compiler_params=pltpu.CompilerParams(
            collective_id=2, has_side_effects=True, vmem_limit_bytes=58 * 2**20
        ),
    )(nrmt, slope, act, fold, lg, gboth)


def leave_kernel(*refs):
    for src, dst in zip(refs[:3], refs[3:]):
        dst[...] = src[...]


def leave(*values):
    vmem = pl.BlockSpec(memory_space=VMEM)
    return pl.pallas_call(
        leave_kernel,
        out_shape=tuple(jax.ShapeDtypeStruct(v.shape, v.dtype) for v in values),
        in_specs=[vmem] * 3,
        out_specs=(vmem,) * 3,
    )(*values)


def shards(tokens, shift, scale, gate, fc1, fc2, proj, lift, conv_a, conv_b, target):
    width = tokens.shape[3]
    patch_width = proj.shape[1]

    cols_here = fc2.shape[1]
    ch = conv_a.shape[2]
    slope, act, sums, fold, gboth, nrmt, kern, conv_bt, want = forward(
        tokens[0].reshape(-1, width),
        shift,
        scale,
        gate,
        proj.T,
        fc1,
        fc2.T,
        lift,
        conv_a.reshape(9, ch, ch),
        conv_b.reshape(9, ch, ch),
        target[0],
    )
    latent_mine, latent_rows = middle(
        sums, kern, want, conv_b.reshape(3, 3 * ch, ch), conv_bt
    )
    latent_rows = latent_rows.reshape(-1, patch_width)
    grad_one, grad_two = backward(nrmt, slope, act, fold, latent_rows, gboth, cols_here)
    grad_one, grad_two, latent_mine = leave(grad_one, grad_two, latent_mine)
    return (grad_one, grad_two.T, latent_mine[None])


def solution(mesh):
    in_specs = (
        P("grp", "seq", None, None),
        P("grp", None),
        P("grp", None),
        P("grp", None),
        P(("grp", "seq"), "tile"),
        P("tile", ("grp", "seq")),
        P(),
        P(),
        P(),
        P(),
        P("grp", "seq", "tile", None),
    )
    out_specs = (
        P(("grp", "seq"), "tile"),
        P("tile", ("grp", "seq")),
        P("grp", "seq", "tile", None),
    )
    return jax.shard_map(shards, mesh=mesh, in_specs=in_specs, out_specs=out_specs, check_vma=False)
```

```python
import jax
import jax.numpy as jnp
from jax import lax
from jax.experimental import pallas as pl
from jax.experimental.pallas import tpu as pltpu
from jax.sharding import PartitionSpec as P

F32 = jnp.float32
BF16 = jnp.bfloat16
MESH = pl.DeviceIdType.MESH
VMEM = pltpu.VMEM
NT = (((1,), (1,)), ((), ()))
TN = (((0,), (0,)), ((), ()))
EDGE = 8
PAIR_EDGE = 4
LEAD = 16
NEXT = [(1, 0), (-1, 0), (0, 1), (0, -1), (1, 1), (1, -1), (-1, 1), (-1, -1)]
AROUND = [(0, 1), (0, 2), (0, 3)] + [(ds, dt) for ds in (-1, 1) for dt in range(4)]
STEPS = (1, 3, 2)


def gelu_tanh(value):
    return jax.nn.gelu(value, approximate=True)


def gelu_slope(x):
    k = 0.7978845608028654
    t = jnp.tanh(k * (x + 0.044715 * x * x * x))
    return 0.5 * (1.0 + t) + 0.5 * x * (1.0 - t * t) * (k + 3 * 0.044715 * k * x * x)


def split(value):
    high = value.astype(BF16)
    return high, (value - high.astype(F32)).astype(BF16)


def dot(lhs, rhs, dims=(((1,), (0,)), ((), ()))):
    return lax.dot_general(lhs, rhs, dims, preferred_element_type=F32)


def place():
    grp, seq, tile = lax.axis_index("grp"), lax.axis_index("seq"), lax.axis_index("tile")
    core = seq % 2
    y = (seq // 2) % 2 * 2 + grp
    z = seq // 4

    def device(y, z, core):
        return (y % 2, z * 4 + y // 2 * 2 + core, tile)

    return y, z, core, device


def oriented(y, z, core):
    a = y + core * (z - y)
    b = z + core * (y - z)

    def turn(a, b):
        return a + core * (b - a), b + core * (a - b)

    return a, b, turn


def block_of(y, z):
    return y % 2 * 8 + z * 2 + y // 2


def tile_peer(ds, dt):
    grp, seq, tile = lax.axis_index("grp"), lax.axis_index("seq"), lax.axis_index("tile")
    return (grp, (seq + ds) % 16, (tile + dt) % 4)


def announce(peers):
    for peer in peers:
        pl.semaphore_signal(
            pltpu.get_barrier_semaphore(), inc=1, device_id=peer, device_id_type=MESH
        )


def await_peers(peers):
    pl.semaphore_wait(pltpu.get_barrier_semaphore(), len(peers))


def greet(peers):
    announce(peers)
    await_peers(peers)


class Courier:
    def __init__(self, send, recv):
        self.send, self.recv, self.used, self.started = send, recv, 0, []

    def slot(self, count=1):
        self.used += count
        return self.used - count

    def slots(self, keys):
        return {key: self.slot() for key in keys}

    def copy(self, slot, src, dst, peer, landing=None):
        return pltpu.make_async_remote_copy(
            src_ref=src,
            dst_ref=dst,
            send_sem=self.send.at[slot],
            recv_sem=self.recv.at[slot if landing is None else landing],
            device_id=peer,
            device_id_type=MESH,
        )

    def start(self, slot, src, dst, peer, landing=None):
        copy = self.copy(slot, src, dst, peer, landing)
        copy.start()
        self.started.append(copy)

    def arrived(self, slot, dst, peer):
        self.copy(slot, dst, dst, peer).wait_recv()

    def finish(self):
        for copy in self.started:
            copy.wait_send()


def pixel_kernels(lift, conv_a):
    lifted = {
        (o, e): dot(lift, conv_a[3 * o + e])
        for o in range(3)
        for e in range(3)
    }

    def reach(pixel, cell):
        return [o for o in range(3) if (pixel + o - 1) // 2 == cell]

    out = {}
    for r in range(-1, 5):
        for c in range(-1, 5):
            parts = []
            for a in range(2):
                for b in range(2):
                    total = jnp.zeros_like(lifted[0, 0])
                    for o in reach(r, a):
                        for e in reach(c, b):
                            total = total + lifted[o, e]
                    parts.append(total)
            out[r, c] = jnp.concatenate(parts, axis=0)
    return out


def forward_kernel(
    tokens_hbm, shift, scale, gate, projt, fc1_own, fc2t, lift, conv_a_hbm, conv_b_hbm, target_hbm,
    slope_hbm, act_hbm, sums, fold, gboth, nrmt_hbm, kern_hbm, conv_bt_hbm,
    want_hbm,
    t_rows, t_cols, t_ends, want, target, fc1, gps, tokens, conv_a, conv_b, kern, conv_bt, normed, nrm, nrmt, gath, gin, wpart, wsib, wsum, wz_out, wz_in, wy_out, wy_in, wfull, xp,
    pre, act, part, part_in, psrc, main_in, edge_in, send, recv, local,
):
    y, z, core, device = place()
    a, b, turn = oriented(y, z, core)
    grp, tile = lax.axis_index("grp"), lax.axis_index("tile")
    other = 1 - core
    sibling = device(y, z, other)
    peers = (
        [sibling]
        + [device((y + d) % 4, z, k) for d in STEPS for k in range(2)]
        + [device(y, (z + d) % 4, k) for d in STEPS for k in range(2)]
        + [tile_peer(ds, dt) for ds, dt in AROUND]
    )
    announce(peers)
    loads = [
        pltpu.make_async_copy(src, dst, local.at[i])
        for i, (src, dst) in enumerate(
            (
                (tokens_hbm, tokens),
                (conv_a_hbm, conv_a),
                (conv_b_hbm, conv_b),
                (target_hbm, target),
            )
        )
    ]
    for load in loads:
        load.start()
    mail = Courier(send, recv)
    rows, half = gath.shape[1] // 2, gath.shape[2]
    here_rows, width = tokens.shape
    cols = fc2t.shape[0]
    last = cols // 16 * 16
    fc1[:last] = fc1_own[:last]
    tail = jnp.concatenate(
        [fc1_own[last:].astype(F32), jnp.zeros((rows - cols, 2 * half), F32)], axis=0
    )
    fc1[last:] = tail.astype(BF16)

    n_out = projt.shape[0]
    seq = lax.axis_index("seq")
    for i, g in enumerate((grp, 1 - grp)):
        start = (g * 16 + seq) * cols
        first = jnp.minimum(start // 128 * 128, width - 256)
        at = pl.ds(pl.multiple_of(first, 128), 256)
        high, low = split(gate[:, at] * projt[:, at].astype(F32))
        r = lax.broadcasted_iota(jnp.int32, (rows, 256), 0)
        k = lax.broadcasted_iota(jnp.int32, (rows, 256), 1)
        pick = jnp.where((k == r + (start - first)) & (r < cols), 1.0, 0.0).astype(BF16)
        value = dot(pick, high, NT) + dot(pick, low, NT)
        zero = jnp.zeros_like(value)
        gps[i] = jnp.concatenate(
            [jnp.where(grp == 0, value, zero), jnp.where(grp == 1, value, zero)], axis=1
        )
    await_peers(peers)

    def peer(da, db):
        return device(*turn((a + da) % 4, (b + db) % 4), core)

    def block(da, db):
        return block_of(*turn((a + da) % 4, (b + db) % 4))

    own = block(0, 0)
    mine = pl.ds(pl.multiple_of(core * rows, 16), rows)
    theirs = pl.ds(pl.multiple_of(other * rows, 16), rows)
    s_a = mail.slots((h, d) for h in range(2) for d in STEPS)
    r_a = {d: mail.slot(2) for d in STEPS}
    s_gate, s_own = mail.slot(), mail.slot()
    partner = device(y // 2 * 2 + 1 - grp, z, core)
    mail.start(s_gate, gps.at[1], gin, partner)
    src = fc1.at[:, pl.ds(pl.multiple_of(other * half, 128), half)]
    mail.start(s_own, src, gath.at[own, mine], sibling)
    for d in STEPS:
        for h in range(2):
            to = device((y + d) % 4, z, 0) if h == 0 else device(y, (z + d) % 4, 1)
            src = fc1.at[:, h * half : (h + 1) * half]
            mail.start(s_a[h, d], src, gath.at[own, mine], to, r_a[d] + core)
    gath[own, mine, :] = fc1[:, pl.ds(pl.multiple_of(core * half, 128), half)]

    loads[0].wait()

    def normalise(i):
        x = tokens[pl.ds(pl.multiple_of(i * 64, 64), 64), :].astype(F32)
        center = x - jnp.mean(x, axis=1, keepdims=True)
        spread = jnp.mean(center * center, axis=1, keepdims=True)
        value = center * lax.rsqrt(spread + 1e-06) * (1.0 + scale[...]) + shift[...]
        at = pl.ds(pl.multiple_of(core * here_rows + i * 64, 64), 64)
        normed[at, :] = value.astype(BF16)

    s_b = mail.slots((da, d) for da in range(4) for d in STEPS)

    def put_b(da):
        ref = gath.at[block(da, 0)]
        for d in STEPS:
            mail.start(s_b[da, d], ref, ref, peer(0, d))

    n_steps = here_rows // 64
    pl.loop(0, n_steps // 2)(normalise)
    mail.arrived(s_own, gath.at[own, theirs], sibling)
    put_b(0)
    pl.loop(n_steps // 2, n_steps)(normalise)
    blk_rows = pl.ds(pl.multiple_of(core * here_rows, 128), here_rows)
    s_n = mail.slot()
    mail.start(s_n, normed.at[blk_rows], normed.at[blk_rows], sibling)

    mail.arrived(s_gate, gin, partner)
    both = gps[0] + gin[...]
    gboth[...] = both
    high, low = split(both[:cols])
    wpart[...] = dot(fc2t[...], high, TN) + dot(fc2t[...], low, TN)
    wq = half // 4
    s_w = mail.slot()
    mail.start(s_w, wpart.at[pl.ds(pl.multiple_of(other * half, 16), half)], wsib, sibling)

    def window_of(i):
        first = 2 * cols * i // 128 * 128
        off = 2 * cols * i - first
        span = 256 if off + 2 * cols <= 256 else 384
        r = lax.broadcasted_iota(jnp.int32, (2 * rows, span), 0)
        k = lax.broadcasted_iota(jnp.int32, (2 * rows, span), 1)
        low_part = (k == r + off) & (r < cols)
        high_part = (k == r + (off + cols - rows)) & (r >= rows) & (r < rows + cols)
        pick = jnp.where(low_part | high_part, 1.0, 0.0).astype(BF16)
        return normed[:, first : first + span], pick

    def rechunk(i):
        value, pick = window_of(i)
        nrm[i] = dot(value, pick, NT).astype(BF16)

    def rechunk_turned(indices):
        for i in indices:
            value, pick = window_of(i)
            nrmt[i] = dot(pick, value, NT).astype(BF16)

    mail.arrived(s_w, wsib, sibling)
    wsum[...] = wpart[pl.ds(pl.multiple_of(core * half, 16), half), :] + wsib[...]
    wz_out[...] = wsum[...].astype(BF16)
    s_wz, s_wy, s_wa = mail.slots(STEPS), mail.slots(STEPS), mail.slots(STEPS)
    for d in STEPS:
        to = (z + d) % 4
        src = wz_out.at[pl.ds(pl.multiple_of(to * wq, 16), wq)]
        mail.start(s_wz[d], src, wz_in.at[d - 1], device(y, to, core))

    keep = [
        pltpu.make_async_copy(src, dst, local.at[4 + i])
        for i, (src, dst) in enumerate(
            (
                (nrmt, nrmt_hbm),
                (act, act_hbm),
                (pre, slope_hbm),
                (kern, kern_hbm),
                (conv_bt, conv_bt_hbm),
                (want, want_hbm),
            )
        )
    ]
    loads[1].wait()
    kernels = pixel_kernels(lift[...], conv_a)
    for i, value in enumerate(kernels.values()):
        kern[i] = value.astype(BF16)
    keep[3].start()

    def relay(d):
        at = block(-d, 0)
        frm = turn((a + 4 - d) % 4, b)
        for k in range(2):
            landed = gath.at[at, pl.ds(k * rows, rows)]
            mail.arrived(r_a[d] + k, landed, device(*frm, k))
        put_b((4 - d) % 4)

    def w_along_y():
        for d in STEPS:
            mail.arrived(s_wz[d], wz_in.at[d - 1], device(y, (z + 4 - d) % 4, core))
        total = wsum[pl.ds(pl.multiple_of(z * wq, 16), wq), :]
        for d in STEPS:
            total = total + wz_in[d - 1].astype(F32)
        for i in range(2):
            image = total[:, i * n_out : (i + 1) * n_out]
            wy_out[i] = jnp.concatenate([image[: wq // 2], image[wq // 2 :]], axis=1).astype(BF16)
        for d in STEPS:
            src = wy_out.at[(grp + d) % 2]
            mail.start(s_wy[d], src, wy_in.at[d - 1], device((y + d) % 4, z, core))

    def w_rows(z):
        return pl.ds(pl.multiple_of(z * (wq // 2), 16), wq // 2)

    def w_back():
        total = wy_out[grp].astype(F32)
        for d in STEPS:
            mail.arrived(s_wy[d], wy_in.at[d - 1], device((y + 4 - d) % 4, z, core))
            total = total + wy_in[d - 1].astype(F32)
        wfull[w_rows(z), :] = total.astype(BF16)
        for d in STEPS:
            ref = wfull.at[w_rows(z)]
            mail.start(s_wa[d], ref, ref, device(y, (z + d) % 4, core))

    relay(1)
    relay(3)
    w_along_y()
    mail.arrived(s_n, normed.at[pl.ds(pl.multiple_of(other * here_rows, 128), here_rows)], sibling)
    for i in range(gath.shape[0]):
        rechunk(i)
    relay(2)
    loads[3].wait()
    height, breadth = target.shape[0], target.shape[1]
    top_rows, end_rows = pl.ds(0, 2), pl.ds(height - 2, 2)
    lead, trail = pl.ds(0, LEAD), pl.ds(breadth - LEAD, LEAD)
    borders = {
        (1, 0): (target.at[end_rows], t_rows.at[0]),
        (-1, 0): (target.at[top_rows], t_rows.at[1]),
        (0, 1): (target.at[:, trail], t_cols.at[0]),
        (0, -1): (target.at[:, lead], t_cols.at[1]),
        (1, 1): (target.at[end_rows, trail], t_ends.at[0]),
        (1, -1): (target.at[end_rows, lead], t_ends.at[1]),
        (-1, 1): (target.at[top_rows, trail], t_ends.at[2]),
        (-1, -1): (target.at[top_rows, lead], t_ends.at[3]),
    }
    s_border = mail.slots(NEXT)
    for to in NEXT:
        mail.start(s_border[to], *borders[to], tile_peer(*to))

    def multiply(blocks, first=False):
        total = None
        for da, db in blocks:
            at = block(da, db)
            term = dot(nrm[at], gath[at])
            total = term if total is None else total + term
        pre[...] = total if first else pre[...] + total

    def take_b(da, d):
        mail.arrived(s_b[da, d], gath.at[block(da, -d)], peer(0, -d))

    multiply([(0, 0), (3, 0)], first=True)
    multiply([(1, 0), (2, 0)])
    for da in (0, 3, 1, 2):
        take_b(da, 1)
        take_b(da, 3)
        multiply([(da, 3), (da, 1)])
        take_b(da, 2)
        multiply([(da, 2)])
        if da == 0:
            rechunk_turned(range(0, 6))
            w_back()
        elif da == 3:
            rechunk_turned(range(6, 11))
            loads[2].wait()
            ch = conv_b.shape[2]
            for o in range(3):
                for e in range(3):
                    conv_bt[o, e * ch : (e + 1) * ch, :] = conv_b[8 - 3 * o - e].T
            keep[4].start()
            xp[...] = dot(tokens[...], projt[...], NT).reshape(xp.shape)
        elif da == 1:
            rechunk_turned(range(11, 16))
            keep[0].start()

    for d in STEPS:
        frm = (z + 4 - d) % 4
        mail.arrived(s_wa[d], wfull.at[w_rows(frm)], device(y, frm, core))
    for i in range(4):
        value = wfull[i * (wq // 2) : (i + 1) * (wq // 2), :]
        fold[i * wq : i * wq + wq // 2, :] = value[:, :n_out]
        fold[i * wq + wq // 2 : (i + 1) * wq, :] = value[:, n_out:]

    n_rows, n_cols = xp.shape[0], xp.shape[1]
    s_part = mail.slot()
    for k in (other, core):
        at = pl.ds(pl.multiple_of(k * here_rows, 128), here_rows)
        value = gelu_tanh(pre[at, :]).astype(BF16)
        act[at, :] = value
        part[k] = dot(value, fold[...]).reshape(part.shape[1:])
        if k is other:
            mail.start(s_part, part.at[other], part_in, sibling)
    own_cols = pl.ds(pl.multiple_of(tile * (n_cols // 4), 16), n_cols // 4)
    part[core, :, own_cols, :] = part[core, :, own_cols, :] + xp[:, own_cols, :]
    keep[1].start()
    mail.arrived(s_part, part_in, sibling)
    total = part[core] + part_in[...]

    edge = jnp.zeros((n_rows // 2, EDGE, 2 * n_out), F32)
    psrc[:, :EDGE, :] = edge
    psrc[:, EDGE + n_cols :, :] = edge
    psrc[:, EDGE : EDGE + n_cols, :] = jnp.concatenate(
        [total[: n_rows // 2], total[n_rows // 2 :]], axis=2
    )
    span = main_in.shape[2]

    def window(dt):
        return pl.ds(pl.multiple_of((tile + dt) % 4 * (n_cols // 4), 8), span)

    s_around = mail.slots(AROUND)
    for ds, dt in AROUND:
        if ds == 0:
            src, dst = psrc.at[:, window(dt)], main_in.at[dt]
        elif ds == -1:
            src, dst = psrc.at[pl.ds(0, 1), window(dt)], edge_in.at[1, dt]
        else:
            src, dst = psrc.at[pl.ds(n_rows // 2 - 1, 1), window(dt)], edge_in.at[0, dt]
        mail.start(s_around[ds, dt], src, dst, tile_peer(ds, dt))
    pre[...] = gelu_slope(pre[...])
    keep[2].start()

    for ds, dt in NEXT:
        mail.arrived(s_border[ds, dt], borders[ds, dt][1], tile_peer(-ds, -dt))
    body, first_cols = slice(LEAD, LEAD + breadth), slice(0, LEAD)
    last_cols = slice(LEAD + breadth, 2 * LEAD + breadth)
    inner, under = slice(2, 2 + height), slice(2 + height, 4 + height)

    def want_at(rows, at, value):
        value = value.astype(F32)
        want[rows, 0, at, :] = value[:, :, :128]
        want[rows, 1, at, :] = value[:, :, 128:]

    want_at(inner, body, target[...])
    want_at(slice(0, 2), body, t_rows[0])
    want_at(under, body, t_rows[1])
    for side, at in ((0, first_cols), (1, last_cols)):
        want_at(inner, at, t_cols[side])
        want_at(slice(0, 2), at, t_ends[side])
        want_at(under, at, t_ends[2 + side])
    keep[5].start()

    total = psrc[:, window(0), :]
    for dt in range(1, 4):
        mail.arrived(s_around[0, dt], main_in.at[dt], tile_peer(0, -dt))
        total = total + main_in[dt]
    sums[1 : 1 + n_rows // 2] = total[:, :, :n_out]
    sums[1 + n_rows // 2 : 1 + n_rows] = total[:, :, n_out:]
    for i, ds in ((0, 1), (1, -1)):
        total = jnp.zeros(edge_in.shape[3:], F32)
        for dt in range(4):
            mail.arrived(s_around[ds, dt], edge_in.at[i, dt], tile_peer(-ds, -dt))
            total = total + edge_in[i, dt, 0]
        outside = (seq == 0) if i == 0 else (seq == 15)
        total = total[:, n_out:] if i == 0 else total[:, :n_out]
        sums[(n_rows + 1) * i] = jnp.where(outside, 0.0, total)

    for copy in keep:
        copy.wait()
    mail.finish()


def forward(tokens, shift, scale, gate, projt, fc1, fc2t, lift, conv_a, conv_b, target):
    rows, width = tokens.shape
    hidden = fc1.shape[1]
    depth = (fc1.shape[0] + 15) // 16 * 16
    half = hidden // 2
    n_out = projt.shape[0]
    wide = (depth, 2 * n_out)
    n_blk = 16
    height, breadth, ch = target.shape
    token_rows, n_cols = 4 * rows // 512, 128
    span = n_cols // 4 + 2 * EDGE
    vmem, hbm = pl.BlockSpec(memory_space=VMEM), pl.BlockSpec(memory_space=pl.ANY)
    shape = jax.ShapeDtypeStruct
    return pl.pallas_call(
        forward_kernel,
        out_shape=(
            shape((2 * rows, half), F32),
            shape((2 * rows, half), BF16),
            shape((token_rows + 2, span, n_out), F32),
            shape((half, n_out), BF16),
            shape(wide, F32),
            shape((n_blk, 2 * depth, 2 * rows), BF16),
            shape((36, n_out, ch), BF16),
            shape((3, 3 * ch, ch), BF16),
            shape((height + 4, 2, breadth + 2 * LEAD, ch // 2), F32),
        ),
        in_specs=[hbm] + [vmem] * 7 + [hbm] * 3,
        out_specs=(hbm, hbm, vmem, vmem, vmem) + (hbm,) * 4,
        scratch_shapes=[
            VMEM((2, 2, breadth, ch), BF16),
            VMEM((2, height, LEAD, ch), BF16),
            VMEM((4, 2, LEAD, ch), BF16),
            VMEM((height + 4, 2, breadth + 2 * LEAD, ch // 2), F32),
            VMEM((height, breadth, ch), BF16),
            VMEM((depth, hidden), BF16),
            VMEM((2,) + wide, F32),
            VMEM((rows, width), BF16),
            VMEM((9, ch, ch), BF16),
            VMEM((9, ch, ch), BF16),
            VMEM((36, n_out, ch), BF16),
            VMEM((3, 3 * ch, ch), BF16),
            VMEM((2 * rows, width), BF16),
            VMEM((n_blk, 2 * rows, 2 * depth), BF16),
            VMEM((n_blk, 2 * depth, 2 * rows), BF16),
            VMEM((n_blk, 2 * depth, half), BF16),
            VMEM(wide, F32),
            VMEM((hidden, 2 * n_out), F32),
            VMEM((half, 2 * n_out), F32),
            VMEM((half, 2 * n_out), F32),
            VMEM((half, 2 * n_out), BF16),
            VMEM((3, half // 4, 2 * n_out), BF16),
            VMEM((2, half // 8, 2 * n_out), BF16),
            VMEM((3, half // 8, 2 * n_out), BF16),
            VMEM((half // 2, 2 * n_out), BF16),
            VMEM((token_rows, n_cols, n_out), F32),
            VMEM((2 * rows, half), F32),
            VMEM((2 * rows, half), BF16),
            VMEM((2, token_rows, n_cols, n_out), F32),
            VMEM((token_rows, n_cols, n_out), F32),
            VMEM((token_rows // 2, n_cols + 2 * EDGE, 2 * n_out), F32),
            VMEM((4, token_rows // 2, span, 2 * n_out), F32),
            VMEM((2, 4, 1, span, 2 * n_out), F32),
            pltpu.SemaphoreType.DMA((72,)),
            pltpu.SemaphoreType.DMA((72,)),
            pltpu.SemaphoreType.DMA((10,)),
        ],
        compiler_params=pltpu.CompilerParams(
            collective_id=1, has_side_effects=True, vmem_limit_bytes=60 * 2**20
        ),
    )(tokens, shift, scale, gate, projt, fc1, fc2t, lift, conv_a, conv_b, target)


def middle_kernel(
    sums, *refs,
):
    hbm, (latent, lg), refs = refs[:4], refs[4:6], refs[6:]
    kern, want, conv_b, conv_bt = refs[:4]
    patch, f_ref, a_ref, b_ref, acc, gf, send, recv, local = refs[4:]
    loads = [
        pltpu.make_async_copy(src, dst, local.at[i])
        for i, (src, dst) in enumerate(zip(hbm, refs))
    ]
    for load in loads:
        load.start()
    grp, seq, tile = lax.axis_index("grp"), lax.axis_index("seq"), lax.axis_index("tile")
    core = seq % 2

    def cores(k, dt):
        return (grp, seq - core + (core + k) % 2, (tile + dt) % 4)

    around = [(k, dt) for k in range(2) for dt in range(4) if (k, dt) != (0, 0)]
    announce([cores(k, dt) for k, dt in around])
    mail = Courier(send, recv)
    n_tok, span, width = sums.shape
    n_rows, here = n_tok - 2, span - 2 * EDGE
    pairs, ch = a_ref.shape[1], a_ref.shape[2] // 4

    rows = {r: sums[r] for r in range(n_tok)}
    height, breadth = f_ref.shape[0] - 8, 4 * here
    for r in range(n_tok):
        patch[0, r + 1] = pltpu.roll(rows[r], 1, 0).astype(BF16)
        patch[1, r + 1] = rows[r].astype(BF16)
        patch[2, r + 1] = pltpu.roll(rows[r], span - 1, 0).astype(BF16)
    for k in range(3):
        patch[k, 0] = jnp.zeros((span, width), BF16)
        patch[k, n_tok + 1] = jnp.zeros((span, width), BF16)

    loads[0].wait()

    def near(phase):
        return [(d, phase - 4 * d) for d in (-1, 0, 1) if -1 <= phase - 4 * d <= 4]

    for al in range(4):
        for ph in range(4):
            value = None
            for dr, r in near(al):
                for dc, c in near(ph):
                    lhs = patch[1 + dc, 1 + dr : 1 + dr + n_tok].reshape(n_tok * span, width)
                    term = dot(lhs, kern[6 * (r + 1) + c + 1])
                    value = term if value is None else value + term
            value = value.reshape(n_tok, span, ch)
            for tr in range(n_tok):
                at = pl.ds(ph // 2, span, stride=2)
                f_ref[4 * tr + al, ph % 2, 0, at, :] = value[tr, :, :128]
                f_ref[4 * tr + al, ph % 2, 1, at, :] = value[tr, :, 128:]

    first_pair = 2 * EDGE - PAIR_EDGE

    def inside(row, b):
        r = seq * height + row
        c = 2 * (tile * breadth // 2 + lax.broadcasted_iota(jnp.int32, (pairs, 1), 0) - PAIR_EDGE) + b
        return (r >= 0) & (r < 16 * height) & (c >= 0) & (c < 4 * breadth)

    def both(ref, at, rows):
        return jnp.concatenate([ref[*at, 0, rows, :], ref[*at, 1, rows, :]], axis=1)

    def spread(ref, at, v0, v1):
        ref[at, :, 0:ch] = pltpu.roll(v1, 1, 0).astype(BF16)
        ref[at, :, ch : 2 * ch] = v0.astype(BF16)
        ref[at, :, 2 * ch : 3 * ch] = v1.astype(BF16)
        ref[at, :, 3 * ch :] = pltpu.roll(v0, pairs - 1, 0).astype(BF16)

    @pl.loop(0, height + 6)
    def _(i):
        smooth = []
        for b in range(2):
            f = both(f_ref, (i + 1, b), slice(first_pair, first_pair + pairs))
            sigma = jax.nn.sigmoid(f)
            smooth.append(jnp.where(inside(i - 3, b), f * sigma, 0.0))
            slope = sigma * (1.0 + f * (1.0 - sigma))
            f_ref[i + 1, b, 0, first_pair : first_pair + pairs, :] = slope[:, :128]
            f_ref[i + 1, b, 1, first_pair : first_pair + pairs, :] = slope[:, 128:]
        spread(a_ref, i, *smooth)

    def conv(src, weights, out_rows, chunk):
        @pl.loop(0, out_rows // chunk)
        def _(i):
            for b in range(2):
                value = None
                for o in range(3):
                    lhs = src[pl.ds(i * chunk + o, chunk), :, b * ch : (b + 3) * ch]
                    term = dot(lhs.reshape(chunk * pairs, 3 * ch), weights[o])
                    value = term if value is None else value + term
                acc[b, pl.ds(i * chunk, chunk)] = value.reshape(chunk, pairs, ch)

    loads[2].wait()
    conv(a_ref, conv_b, height + 4, (height + 4) // 2)
    loads[1].wait()

    @pl.loop(0, height + 4)
    def _(i):
        grad = []
        for b in range(2):
            diff = acc[b, i] - both(want, (i,), pl.ds(LEAD - 2 * PAIR_EDGE + b, pairs, stride=2))
            grad.append(jnp.where(inside(i - 2, b), diff, 0.0))
        spread(b_ref, i, *grad)

    loads[3].wait()
    conv(b_ref, conv_bt, height + 2, (height + 2) // 2)

    @pl.loop(0, height + 2)
    def _(i):
        for b in range(2):
            value = acc[b, i] * both(f_ref, (i + 3, b), slice(first_pair, first_pair + pairs))
            value = jnp.where(inside(i - 1, b), value, 0.0)
            gf[i, b, 0], gf[i, b, 1] = value[:, :128], value[:, 128:]

    grad = None
    for r in range(-1, 5):
        for c in range(-1, 5):
            at = pl.ds(PAIR_EDGE + c // 2, here, stride=2)
            lhs = jnp.concatenate(
                [both(gf, (4 * tr + r + 1, c % 2), at).astype(BF16) for tr in range(n_rows)],
                axis=0,
            )
            term = dot(lhs, kern[6 * (r + 1) + c + 1], NT)
            grad = term if grad is None else grad + term
    grad = grad.reshape(n_rows, here, width)
    latent[...] = grad
    def part_of(k, dt):
        cols = pl.ds(pl.multiple_of((tile + dt) % 4 * here, 16), here)
        return lg.at[pl.ds((core + k) % 2 * n_rows, n_rows), cols]

    cols = pl.ds(pl.multiple_of(tile * here, 16), here)
    lg[pl.ds(core * n_rows, n_rows), cols, :] = grad.astype(BF16)
    await_peers(around)
    s_back = mail.slots(around)
    for k, dt in around:
        mail.start(s_back[k, dt], part_of(0, 0), part_of(0, 0), cores(k, dt))
    for k, dt in around:
        mail.arrived(s_back[k, dt], part_of(k, -dt), cores(k, -dt))
    mail.finish()


def middle(sums, kern, want, conv_b, conv_bt):
    n_tok, span, width = sums.shape
    n_rows, here = n_tok - 2, span - 2 * EDGE
    height, breadth, ch = want.shape[0] - 4, 4 * here, conv_bt.shape[2]
    pairs = breadth // 2 + 2 * PAIR_EDGE
    vmem, hbm = pl.BlockSpec(memory_space=VMEM), pl.BlockSpec(memory_space=pl.ANY)
    shape = jax.ShapeDtypeStruct
    loaded = (kern, want, conv_b, conv_bt)
    return pl.pallas_call(
        middle_kernel,
        out_shape=(
            shape((n_rows, here, width), F32),
            shape((2 * n_rows, 4 * here, width), BF16),
        ),
        in_specs=[vmem] + [hbm] * len(loaded),
        out_specs=(vmem,) * 2,
        scratch_shapes=[VMEM(x.shape, x.dtype) for x in loaded]
        + [
            VMEM((3, n_rows + 4, span, width), BF16),
            VMEM((height + 8, 2, 2, 2 * span, ch // 2), F32),
            VMEM((height + 6, pairs, 4 * ch), BF16),
            VMEM((height + 4, pairs, 4 * ch), BF16),
            VMEM((2, height + 4, pairs, ch), F32),
            VMEM((height + 2, 2, 2, pairs, ch // 2), F32),
            pltpu.SemaphoreType.DMA((16,)),
            pltpu.SemaphoreType.DMA((16,)),
            pltpu.SemaphoreType.DMA((len(loaded),)),
        ],
        compiler_params=pltpu.CompilerParams(
            collective_id=3, has_side_effects=True, vmem_limit_bytes=58 * 2**20
        ),
    )(sums, *loaded)


def backward_kernel(
    nrmt_hbm, slope_hbm, act_hbm, fold, lg, gboth, out, two,
    nrmt, slope, act, gpre, st, sz_in, sy_out, sy_in, sfull, b_out, b_in, a_out, a_in, fin, fin_in,
    send, recv, local,
):
    y, z, core, device = place()
    a, b, turn = oriented(y, z, core)
    grp = lax.axis_index("grp")
    other = 1 - core
    sibling = device(y, z, other)
    peers = (
        [sibling]
        + [device((y + d) % 4, z, core) for d in STEPS]
        + [device(y, (z + d) % 4, core) for d in STEPS]
    )
    announce(peers)
    loads = [
        pltpu.make_async_copy(src, dst, local.at[i])
        for i, (src, dst) in enumerate(
            ((act_hbm, act), (slope_hbm, slope), (nrmt_hbm, nrmt))
        )
    ]
    for load in loads:
        load.start()
    mail = Courier(send, recv)
    half = gpre.shape[1]
    rows = nrmt.shape[1] // 2

    def peer(da, db):
        return device(*turn((a + da) % 4, (b + db) % 4), core)

    def block(da, db):
        return block_of(*turn((a + da) % 4, (b + db) % 4))

    def term(da, db):
        return dot(nrmt[block(da, db)], gpre[...])

    s_b = mail.slots((da, d) for da in range(4) for d in STEPS)
    s_a = mail.slots(STEPS)

    def send_b(da):
        for d in (2, 1, 3):
            b_out[da, d - 1] = term(da, d).astype(BF16)
            mail.start(s_b[da, d], b_out.at[da, d - 1], b_in.at[da, d - 1], peer(0, d))

    def sum_b(da):
        total = term(da, 0)
        for d in STEPS:
            mail.arrived(s_b[da, d], b_in.at[da, d - 1], peer(0, -d))
            total = total + b_in[da, d - 1].astype(F32)
        return total

    def send_a(d):
        a_out[d - 1] = sum_b(d).astype(BF16)
        mail.start(s_a[d], a_out.at[d - 1], a_in.at[d - 1], peer(d, 0))

    loads[0].wait()
    st[...] = dot(lg[...], act[...], TN).astype(BF16)
    sq = st.shape[0] // 4
    s_sz, s_sy, s_sa = mail.slots(STEPS), mail.slots(STEPS), mail.slots(STEPS)
    await_peers(peers)
    for d in STEPS:
        to = (z + d) % 4
        src = st.at[pl.ds(pl.multiple_of(to * sq, 16), sq)]
        mail.start(s_sz[d], src, sz_in.at[d - 1], device(y, to, core))

    loads[1].wait()
    gpre[...] = (dot(lg[...], fold[...], NT) * slope[...]).astype(BF16)
    loads[2].wait()
    send_b(2)

    for d in STEPS:
        mail.arrived(s_sz[d], sz_in.at[d - 1], device(y, (z + 4 - d) % 4, core))
    s_at = pl.ds(pl.multiple_of(z * sq, 16), sq)
    total = st[s_at, :].astype(F32)
    for d in STEPS:
        total = total + sz_in[d - 1].astype(F32)
    sy_out[...] = total.astype(BF16)
    for d in STEPS:
        mail.start(s_sy[d], sy_out, sy_in.at[d - 1], device((y + d) % 4, z, core))

    send_b(1)
    for d in STEPS:
        mail.arrived(s_sy[d], sy_in.at[d - 1], device((y + 4 - d) % 4, z, core))
    sfull[core, grp, s_at] = (total + sy_in[1].astype(F32)).astype(BF16)
    sfull[core, 1 - grp, s_at] = (sy_in[0].astype(F32) + sy_in[2].astype(F32)).astype(BF16)
    for d in STEPS:
        ref = sfull.at[core, :, s_at]
        mail.start(s_sa[d], ref, ref, device(y, (z + d) % 4, core))
    send_b(3)
    send_b(0)

    send_a(2)
    for d in STEPS:
        frm = (z + 4 - d) % 4
        at = pl.ds(pl.multiple_of(frm * sq, 16), sq)
        mail.arrived(s_sa[d], sfull.at[core, :, at], device(y, frm, core))
    s_ss = mail.slot()
    mail.start(s_ss, sfull.at[core], sfull.at[core], sibling)
    send_a(1)
    send_a(3)

    mail.arrived(s_ss, sfull.at[other], sibling)
    g_high, g_low = split(gboth[...])
    for h in range(2):
        sums = sfull[h].reshape(-1, half)
        value = dot(g_high, sums) + dot(g_low, sums)
        two[:, h * half : (h + 1) * half] = value[: two.shape[0]]

    total = sum_b(0)
    for d in STEPS:
        mail.arrived(s_a[d], a_in.at[d - 1], peer(-d, 0))
        total = total + a_in[d - 1].astype(F32)
    fin[...] = total
    s_fin = mail.slot()
    theirs = pl.ds(pl.multiple_of(other * rows, 16), rows)
    mail.start(s_fin, fin.at[theirs], fin_in, sibling)
    here = out.shape[0]
    mine = fin[pl.ds(pl.multiple_of(core * rows, 16), rows), :]
    out[:, pl.ds(pl.multiple_of(core * half, 128), half)] = mine[:here]
    mail.arrived(s_fin, fin_in, sibling)
    out[:, pl.ds(pl.multiple_of(other * half, 128), half)] = fin_in[:here, :]
    mail.finish()


def backward(nrmt, slope, act, fold, lg, gboth, here):
    n_blk, depth, rows = nrmt.shape
    half = slope.shape[1]
    width = lg.shape[1]
    vmem, hbm = pl.BlockSpec(memory_space=VMEM), pl.BlockSpec(memory_space=pl.ANY)
    shape = jax.ShapeDtypeStruct
    return pl.pallas_call(
        backward_kernel,
        out_shape=(shape((here, 2 * half), F32), shape((here, 2 * half), F32)),
        in_specs=[hbm] * 3 + [vmem] * 3,
        out_specs=(vmem,) * 2,
        scratch_shapes=[
            VMEM(nrmt.shape, BF16),
            VMEM(slope.shape, F32),
            VMEM(act.shape, BF16),
            VMEM((rows, half), BF16),
            VMEM((width, half), BF16),
            VMEM((3, width // 4, half), BF16),
            VMEM((width // 4, half), BF16),
            VMEM((3, width // 4, half), BF16),
            VMEM((2, 2, width, half), BF16),
            VMEM((4, 3, depth, half), BF16),
            VMEM((4, 3, depth, half), BF16),
            VMEM((3, depth, half), BF16),
            VMEM((3, depth, half), BF16),
            VMEM((depth, half), F32),
            VMEM((depth // 2, half), F32),
            pltpu.SemaphoreType.DMA((32,)),
            pltpu.SemaphoreType.DMA((32,)),
            pltpu.SemaphoreType.DMA((3,)),
        ],
        compiler_params=pltpu.CompilerParams(
            collective_id=2, has_side_effects=True, vmem_limit_bytes=58 * 2**20
        ),
    )(nrmt, slope, act, fold, lg, gboth)


def leave_kernel(*refs):
    for src, dst in zip(refs[:3], refs[3:]):
        dst[...] = src[...]


def leave(*values):
    vmem = pl.BlockSpec(memory_space=VMEM)
    return pl.pallas_call(
        leave_kernel,
        out_shape=tuple(jax.ShapeDtypeStruct(v.shape, v.dtype) for v in values),
        in_specs=[vmem] * 3,
        out_specs=(vmem,) * 3,
    )(*values)


def shards(tokens, shift, scale, gate, fc1, fc2, proj, lift, conv_a, conv_b, target):
    width = tokens.shape[3]
    patch_width = proj.shape[1]

    cols_here = fc2.shape[1]
    ch = conv_a.shape[2]
    slope, act, sums, fold, gboth, nrmt, kern, conv_bt, want = forward(
        tokens[0].reshape(-1, width),
        shift,
        scale,
        gate,
        proj.T,
        fc1,
        fc2.T,
        lift,
        conv_a.reshape(9, ch, ch),
        conv_b.reshape(9, ch, ch),
        target[0],
    )
    latent_mine, latent_rows = middle(
        sums, kern, want, conv_b.reshape(3, 3 * ch, ch), conv_bt
    )
    latent_rows = latent_rows.reshape(-1, patch_width)
    grad_one, grad_two = backward(nrmt, slope, act, fold, latent_rows, gboth, cols_here)
    grad_one, grad_two, latent_mine = leave(grad_one, grad_two, latent_mine)
    return (grad_one, grad_two.T, latent_mine[None])


def solution(mesh):
    in_specs = (
        P("grp", "seq", None, None),
        P("grp", None),
        P("grp", None),
        P("grp", None),
        P(("grp", "seq"), "tile"),
        P("tile", ("grp", "seq")),
        P(),
        P(),
        P(),
        P(),
        P("grp", "seq", "tile", None),
    )
    out_specs = (
        P(("grp", "seq"), "tile"),
        P("tile", ("grp", "seq")),
        P("grp", "seq", "tile", None),
    )
    return jax.shard_map(shards, mesh=mesh, in_specs=in_specs, out_specs=out_specs, check_vma=False)
```

```python
import jax
import jax.numpy as jnp
from jax import lax
from jax.experimental import pallas as pl
from jax.experimental.pallas import tpu as pltpu
from jax.sharding import PartitionSpec as P

F32 = jnp.float32
BF16 = jnp.bfloat16
MESH = pl.DeviceIdType.MESH
VMEM = pltpu.VMEM
NT = (((1,), (1,)), ((), ()))
TN = (((0,), (0,)), ((), ()))
EDGE = 8
PAIR_EDGE = 4
LEAD = 16
NEXT = [(1, 0), (-1, 0), (0, 1), (0, -1), (1, 1), (1, -1), (-1, 1), (-1, -1)]
AROUND = [(0, 1), (0, 2), (0, 3)] + [(ds, dt) for ds in (-1, 1) for dt in range(4)]
STEPS = (1, 3, 2)


def gelu_tanh(value):
    return jax.nn.gelu(value, approximate=True)


def gelu_slope(x):
    k = 0.7978845608028654
    t = jnp.tanh(k * (x + 0.044715 * x * x * x))
    return 0.5 * (1.0 + t) + 0.5 * x * (1.0 - t * t) * (k + 3 * 0.044715 * k * x * x)


def split(value):
    high = value.astype(BF16)
    return high, (value - high.astype(F32)).astype(BF16)


def dot(lhs, rhs, dims=(((1,), (0,)), ((), ()))):
    return lax.dot_general(lhs, rhs, dims, preferred_element_type=F32)


def place():
    grp, seq, tile = lax.axis_index("grp"), lax.axis_index("seq"), lax.axis_index("tile")
    core = seq % 2
    y = (seq // 2) % 2 * 2 + grp
    z = seq // 4

    def device(y, z, core):
        return (y % 2, z * 4 + y // 2 * 2 + core, tile)

    return y, z, core, device


def oriented(y, z, core):
    a = y + core * (z - y)
    b = z + core * (y - z)

    def turn(a, b):
        return a + core * (b - a), b + core * (a - b)

    return a, b, turn


def block_of(y, z):
    return y % 2 * 8 + z * 2 + y // 2


def tile_peer(ds, dt):
    grp, seq, tile = lax.axis_index("grp"), lax.axis_index("seq"), lax.axis_index("tile")
    return (grp, (seq + ds) % 16, (tile + dt) % 4)


def announce(peers):
    for peer in peers:
        pl.semaphore_signal(
            pltpu.get_barrier_semaphore(), inc=1, device_id=peer, device_id_type=MESH
        )


def await_peers(peers):
    pl.semaphore_wait(pltpu.get_barrier_semaphore(), len(peers))


def greet(peers):
    announce(peers)
    await_peers(peers)


class Courier:
    def __init__(self, send, recv):
        self.send, self.recv, self.used, self.started = send, recv, 0, []

    def slot(self, count=1):
        self.used += count
        return self.used - count

    def slots(self, keys):
        return {key: self.slot() for key in keys}

    def copy(self, slot, src, dst, peer, landing=None):
        return pltpu.make_async_remote_copy(
            src_ref=src,
            dst_ref=dst,
            send_sem=self.send.at[slot],
            recv_sem=self.recv.at[slot if landing is None else landing],
            device_id=peer,
            device_id_type=MESH,
        )

    def start(self, slot, src, dst, peer, landing=None):
        copy = self.copy(slot, src, dst, peer, landing)
        copy.start()
        self.started.append(copy)

    def arrived(self, slot, dst, peer):
        self.copy(slot, dst, dst, peer).wait_recv()

    def finish(self):
        for copy in self.started:
            copy.wait_send()


def pixel_kernels(lift, conv_a):
    lifted = {
        (o, e): dot(lift, conv_a[3 * o + e])
        for o in range(3)
        for e in range(3)
    }

    def reach(pixel, cell):
        return [o for o in range(3) if (pixel + o - 1) // 2 == cell]

    out = {}
    for r in range(-1, 5):
        for c in range(-1, 5):
            parts = []
            for a in range(2):
                for b in range(2):
                    total = jnp.zeros_like(lifted[0, 0])
                    for o in reach(r, a):
                        for e in reach(c, b):
                            total = total + lifted[o, e]
                    parts.append(total)
            out[r, c] = jnp.concatenate(parts, axis=0)
    return out


def forward_kernel(
    tokens_hbm, shift, scale, gate, projt, fc1_own, fc2t, lift, conv_a_hbm, conv_b_hbm, target_hbm,
    slope_hbm, act_hbm, sums, fold, gboth, nrmt_hbm, kern_hbm, conv_bt_hbm,
    want_hbm,
    t_rows, t_cols, t_ends, want, target, fc1, gps, tokens, conv_a, conv_b, kern, conv_bt, normed, nrm, nrmt, gath, gin, wpart, wsib, wsum, wz_out, wz_in, wy_out, wy_in, wfull, xp,
    pre, act, part, part_in, psrc, main_in, edge_in, send, recv, local,
):
    y, z, core, device = place()
    a, b, turn = oriented(y, z, core)
    grp, tile = lax.axis_index("grp"), lax.axis_index("tile")
    other = 1 - core
    sibling = device(y, z, other)
    peers = (
        [sibling]
        + [device((y + d) % 4, z, k) for d in STEPS for k in range(2)]
        + [device(y, (z + d) % 4, k) for d in STEPS for k in range(2)]
        + [tile_peer(ds, dt) for ds, dt in AROUND]
    )
    announce(peers)
    loads = [
        pltpu.make_async_copy(src, dst, local.at[i])
        for i, (src, dst) in enumerate(
            (
                (tokens_hbm, tokens),
                (conv_a_hbm, conv_a),
                (conv_b_hbm, conv_b),
                (target_hbm, target),
            )
        )
    ]
    for load in loads:
        load.start()
    mail = Courier(send, recv)
    rows, half = gath.shape[1] // 2, gath.shape[2]
    here_rows, width = tokens.shape
    cols = fc2t.shape[0]
    last = cols // 16 * 16
    fc1[:last] = fc1_own[:last]
    tail = jnp.concatenate(
        [fc1_own[last:].astype(F32), jnp.zeros((rows - cols, 2 * half), F32)], axis=0
    )
    fc1[last:] = tail.astype(BF16)

    await_peers(peers)

    def peer(da, db):
        return device(*turn((a + da) % 4, (b + db) % 4), core)

    def block(da, db):
        return block_of(*turn((a + da) % 4, (b + db) % 4))

    own = block(0, 0)
    mine = pl.ds(pl.multiple_of(core * rows, 16), rows)
    theirs = pl.ds(pl.multiple_of(other * rows, 16), rows)
    s_a = mail.slots((h, d) for h in range(2) for d in STEPS)
    r_a = {d: mail.slot(2) for d in STEPS}
    s_gate, s_own = mail.slot(), mail.slot()
    src = fc1.at[:, pl.ds(pl.multiple_of(other * half, 128), half)]
    mail.start(s_own, src, gath.at[own, mine], sibling)
    for d in STEPS:
        for h in range(2):
            to = device((y + d) % 4, z, 0) if h == 0 else device(y, (z + d) % 4, 1)
            src = fc1.at[:, h * half : (h + 1) * half]
            mail.start(s_a[h, d], src, gath.at[own, mine], to, r_a[d] + core)
    gath[own, mine, :] = fc1[:, pl.ds(pl.multiple_of(core * half, 128), half)]

    n_out = projt.shape[0]
    seq = lax.axis_index("seq")
    for i, g in enumerate((grp, 1 - grp)):
        start = (g * 16 + seq) * cols
        first = jnp.minimum(start // 128 * 128, width - 256)
        at = pl.ds(pl.multiple_of(first, 128), 256)
        high, low = split(gate[:, at] * projt[:, at].astype(F32))
        r = lax.broadcasted_iota(jnp.int32, (rows, 256), 0)
        k = lax.broadcasted_iota(jnp.int32, (rows, 256), 1)
        pick = jnp.where((k == r + (start - first)) & (r < cols), 1.0, 0.0).astype(BF16)
        value = dot(pick, high, NT) + dot(pick, low, NT)
        zero = jnp.zeros_like(value)
        gps[i] = jnp.concatenate(
            [jnp.where(grp == 0, value, zero), jnp.where(grp == 1, value, zero)], axis=1
        )
    partner = device(y // 2 * 2 + 1 - grp, z, core)
    mail.start(s_gate, gps.at[1], gin, partner)

    loads[0].wait()

    def normalise(i):
        x = tokens[pl.ds(pl.multiple_of(i * 64, 64), 64), :].astype(F32)
        center = x - jnp.mean(x, axis=1, keepdims=True)
        spread = jnp.mean(center * center, axis=1, keepdims=True)
        value = center * lax.rsqrt(spread + 1e-06) * (1.0 + scale[...]) + shift[...]
        at = pl.ds(pl.multiple_of(core * here_rows + i * 64, 64), 64)
        normed[at, :] = value.astype(BF16)

    s_b = mail.slots((da, d) for da in range(4) for d in STEPS)

    def put_b(da):
        ref = gath.at[block(da, 0)]
        for d in STEPS:
            mail.start(s_b[da, d], ref, ref, peer(0, d))

    n_steps = here_rows // 64
    pl.loop(0, n_steps // 2)(normalise)
    mail.arrived(s_own, gath.at[own, theirs], sibling)
    put_b(0)
    pl.loop(n_steps // 2, n_steps)(normalise)
    blk_rows = pl.ds(pl.multiple_of(core * here_rows, 128), here_rows)
    s_n = mail.slot()
    mail.start(s_n, normed.at[blk_rows], normed.at[blk_rows], sibling)

    mail.arrived(s_gate, gin, partner)
    both = gps[0] + gin[...]
    gboth[...] = both
    high, low = split(both[:cols])
    wpart[...] = dot(fc2t[...], high, TN) + dot(fc2t[...], low, TN)
    wq = half // 4
    s_w = mail.slot()
    mail.start(s_w, wpart.at[pl.ds(pl.multiple_of(other * half, 16), half)], wsib, sibling)

    def window_of(i):
        first = 2 * cols * i // 128 * 128
        off = 2 * cols * i - first
        span = 256 if off + 2 * cols <= 256 else 384
        r = lax.broadcasted_iota(jnp.int32, (2 * rows, span), 0)
        k = lax.broadcasted_iota(jnp.int32, (2 * rows, span), 1)
        low_part = (k == r + off) & (r < cols)
        high_part = (k == r + (off + cols - rows)) & (r >= rows) & (r < rows + cols)
        pick = jnp.where(low_part | high_part, 1.0, 0.0).astype(BF16)
        return normed[:, first : first + span], pick

    def rechunk(i):
        value, pick = window_of(i)
        nrm[i] = dot(value, pick, NT).astype(BF16)

    def rechunk_turned(indices):
        for i in indices:
            value, pick = window_of(i)
            nrmt[i] = dot(pick, value, NT).astype(BF16)

    mail.arrived(s_w, wsib, sibling)
    wsum[...] = wpart[pl.ds(pl.multiple_of(core * half, 16), half), :] + wsib[...]
    wz_out[...] = wsum[...].astype(BF16)
    s_wz, s_wy, s_wa = mail.slots(STEPS), mail.slots(STEPS), mail.slots(STEPS)
    for d in STEPS:
        to = (z + d) % 4
        src = wz_out.at[pl.ds(pl.multiple_of(to * wq, 16), wq)]
        mail.start(s_wz[d], src, wz_in.at[d - 1], device(y, to, core))

    keep = [
        pltpu.make_async_copy(src, dst, local.at[4 + i])
        for i, (src, dst) in enumerate(
            (
                (nrmt, nrmt_hbm),
                (act, act_hbm),
                (pre, slope_hbm),
                (kern, kern_hbm),
                (conv_bt, conv_bt_hbm),
                (want, want_hbm),
            )
        )
    ]
    loads[1].wait()
    kernels = pixel_kernels(lift[...], conv_a)
    for i, value in enumerate(kernels.values()):
        kern[i] = value.astype(BF16)
    keep[3].start()

    def relay(d):
        at = block(-d, 0)
        frm = turn((a + 4 - d) % 4, b)
        for k in range(2):
            landed = gath.at[at, pl.ds(k * rows, rows)]
            mail.arrived(r_a[d] + k, landed, device(*frm, k))
        put_b((4 - d) % 4)

    def w_along_y():
        for d in STEPS:
            mail.arrived(s_wz[d], wz_in.at[d - 1], device(y, (z + 4 - d) % 4, core))
        total = wsum[pl.ds(pl.multiple_of(z * wq, 16), wq), :]
        for d in STEPS:
            total = total + wz_in[d - 1].astype(F32)
        for i in range(2):
            image = total[:, i * n_out : (i + 1) * n_out]
            wy_out[i] = jnp.concatenate([image[: wq // 2], image[wq // 2 :]], axis=1).astype(BF16)
        for d in STEPS:
            src = wy_out.at[(grp + d) % 2]
            mail.start(s_wy[d], src, wy_in.at[d - 1], device((y + d) % 4, z, core))

    def w_rows(z):
        return pl.ds(pl.multiple_of(z * (wq // 2), 16), wq // 2)

    def w_back():
        total = wy_out[grp].astype(F32)
        for d in STEPS:
            mail.arrived(s_wy[d], wy_in.at[d - 1], device((y + 4 - d) % 4, z, core))
            total = total + wy_in[d - 1].astype(F32)
        wfull[w_rows(z), :] = total.astype(BF16)
        for d in STEPS:
            ref = wfull.at[w_rows(z)]
            mail.start(s_wa[d], ref, ref, device(y, (z + d) % 4, core))

    relay(1)
    relay(3)
    w_along_y()
    mail.arrived(s_n, normed.at[pl.ds(pl.multiple_of(other * here_rows, 128), here_rows)], sibling)
    for i in range(gath.shape[0]):
        rechunk(i)
    relay(2)
    loads[3].wait()
    height, breadth = target.shape[0], target.shape[1]
    top_rows, end_rows = pl.ds(0, 2), pl.ds(height - 2, 2)
    lead, trail = pl.ds(0, LEAD), pl.ds(breadth - LEAD, LEAD)
    borders = {
        (1, 0): (target.at[end_rows], t_rows.at[0]),
        (-1, 0): (target.at[top_rows], t_rows.at[1]),
        (0, 1): (target.at[:, trail], t_cols.at[0]),
        (0, -1): (target.at[:, lead], t_cols.at[1]),
        (1, 1): (target.at[end_rows, trail], t_ends.at[0]),
        (1, -1): (target.at[end_rows, lead], t_ends.at[1]),
        (-1, 1): (target.at[top_rows, trail], t_ends.at[2]),
        (-1, -1): (target.at[top_rows, lead], t_ends.at[3]),
    }
    s_border = mail.slots(NEXT)
    for to in NEXT:
        mail.start(s_border[to], *borders[to], tile_peer(*to))

    def multiply(blocks, first=False):
        total = None
        for da, db in blocks:
            at = block(da, db)
            term = dot(nrm[at], gath[at])
            total = term if total is None else total + term
        pre[...] = total if first else pre[...] + total

    def take_b(da, d):
        mail.arrived(s_b[da, d], gath.at[block(da, -d)], peer(0, -d))

    multiply([(0, 0), (3, 0)], first=True)
    multiply([(1, 0), (2, 0)])
    for da in (0, 3, 1, 2):
        take_b(da, 1)
        take_b(da, 3)
        multiply([(da, 3), (da, 1)])
        take_b(da, 2)
        multiply([(da, 2)])
        if da == 0:
            rechunk_turned(range(0, 6))
            w_back()
        elif da == 3:
            rechunk_turned(range(6, 11))
            loads[2].wait()
            ch = conv_b.shape[2]
            for o in range(3):
                for e in range(3):
                    conv_bt[o, e * ch : (e + 1) * ch, :] = conv_b[8 - 3 * o - e].T
            keep[4].start()
            xp[...] = dot(tokens[...], projt[...], NT).reshape(xp.shape)
        elif da == 1:
            rechunk_turned(range(11, 16))
            keep[0].start()

    for d in STEPS:
        frm = (z + 4 - d) % 4
        mail.arrived(s_wa[d], wfull.at[w_rows(frm)], device(y, frm, core))
    for i in range(4):
        value = wfull[i * (wq // 2) : (i + 1) * (wq // 2), :]
        fold[i * wq : i * wq + wq // 2, :] = value[:, :n_out]
        fold[i * wq + wq // 2 : (i + 1) * wq, :] = value[:, n_out:]

    n_rows, n_cols = xp.shape[0], xp.shape[1]
    s_part = mail.slot()
    for k in (other, core):
        at = pl.ds(pl.multiple_of(k * here_rows, 128), here_rows)
        value = gelu_tanh(pre[at, :]).astype(BF16)
        act[at, :] = value
        part[k] = dot(value, fold[...]).reshape(part.shape[1:])
        if k is other:
            mail.start(s_part, part.at[other], part_in, sibling)
    own_cols = pl.ds(pl.multiple_of(tile * (n_cols // 4), 16), n_cols // 4)
    part[core, :, own_cols, :] = part[core, :, own_cols, :] + xp[:, own_cols, :]
    keep[1].start()
    mail.arrived(s_part, part_in, sibling)
    total = part[core] + part_in[...]

    edge = jnp.zeros((n_rows // 2, EDGE, 2 * n_out), F32)
    psrc[:, :EDGE, :] = edge
    psrc[:, EDGE + n_cols :, :] = edge
    psrc[:, EDGE : EDGE + n_cols, :] = jnp.concatenate(
        [total[: n_rows // 2], total[n_rows // 2 :]], axis=2
    )
    span = main_in.shape[2]

    def window(dt):
        return pl.ds(pl.multiple_of((tile + dt) % 4 * (n_cols // 4), 8), span)

    s_around = mail.slots(AROUND)
    for ds, dt in AROUND:
        if ds == 0:
            src, dst = psrc.at[:, window(dt)], main_in.at[dt]
        elif ds == -1:
            src, dst = psrc.at[pl.ds(0, 1), window(dt)], edge_in.at[1, dt]
        else:
            src, dst = psrc.at[pl.ds(n_rows // 2 - 1, 1), window(dt)], edge_in.at[0, dt]
        mail.start(s_around[ds, dt], src, dst, tile_peer(ds, dt))
    pre[...] = gelu_slope(pre[...])
    keep[2].start()

    for ds, dt in NEXT:
        mail.arrived(s_border[ds, dt], borders[ds, dt][1], tile_peer(-ds, -dt))
    body, first_cols = slice(LEAD, LEAD + breadth), slice(0, LEAD)
    last_cols = slice(LEAD + breadth, 2 * LEAD + breadth)
    inner, under = slice(2, 2 + height), slice(2 + height, 4 + height)

    def want_at(rows, at, value):
        value = value.astype(F32)
        want[rows, 0, at, :] = value[:, :, :128]
        want[rows, 1, at, :] = value[:, :, 128:]

    want_at(inner, body, target[...])
    want_at(slice(0, 2), body, t_rows[0])
    want_at(under, body, t_rows[1])
    for side, at in ((0, first_cols), (1, last_cols)):
        want_at(inner, at, t_cols[side])
        want_at(slice(0, 2), at, t_ends[side])
        want_at(under, at, t_ends[2 + side])
    keep[5].start()

    total = psrc[:, window(0), :]
    for dt in range(1, 4):
        mail.arrived(s_around[0, dt], main_in.at[dt], tile_peer(0, -dt))
        total = total + main_in[dt]
    sums[1 : 1 + n_rows // 2] = total[:, :, :n_out]
    sums[1 + n_rows // 2 : 1 + n_rows] = total[:, :, n_out:]
    for i, ds in ((0, 1), (1, -1)):
        total = jnp.zeros(edge_in.shape[3:], F32)
        for dt in range(4):
            mail.arrived(s_around[ds, dt], edge_in.at[i, dt], tile_peer(-ds, -dt))
            total = total + edge_in[i, dt, 0]
        outside = (seq == 0) if i == 0 else (seq == 15)
        total = total[:, n_out:] if i == 0 else total[:, :n_out]
        sums[(n_rows + 1) * i] = jnp.where(outside, 0.0, total)

    for copy in keep:
        copy.wait()
    mail.finish()


def forward(tokens, shift, scale, gate, projt, fc1, fc2t, lift, conv_a, conv_b, target):
    rows, width = tokens.shape
    hidden = fc1.shape[1]
    depth = (fc1.shape[0] + 15) // 16 * 16
    half = hidden // 2
    n_out = projt.shape[0]
    wide = (depth, 2 * n_out)
    n_blk = 16
    height, breadth, ch = target.shape
    token_rows, n_cols = 4 * rows // 512, 128
    span = n_cols // 4 + 2 * EDGE
    vmem, hbm = pl.BlockSpec(memory_space=VMEM), pl.BlockSpec(memory_space=pl.ANY)
    shape = jax.ShapeDtypeStruct
    return pl.pallas_call(
        forward_kernel,
        out_shape=(
            shape((2 * rows, half), F32),
            shape((2 * rows, half), BF16),
            shape((token_rows + 2, span, n_out), F32),
            shape((half, n_out), BF16),
            shape(wide, F32),
            shape((n_blk, 2 * depth, 2 * rows), BF16),
            shape((36, n_out, ch), BF16),
            shape((3, 3 * ch, ch), BF16),
            shape((height + 4, 2, breadth + 2 * LEAD, ch // 2), F32),
        ),
        in_specs=[hbm] + [vmem] * 7 + [hbm] * 3,
        out_specs=(hbm, hbm, vmem, vmem, vmem) + (hbm,) * 4,
        scratch_shapes=[
            VMEM((2, 2, breadth, ch), BF16),
            VMEM((2, height, LEAD, ch), BF16),
            VMEM((4, 2, LEAD, ch), BF16),
            VMEM((height + 4, 2, breadth + 2 * LEAD, ch // 2), F32),
            VMEM((height, breadth, ch), BF16),
            VMEM((depth, hidden), BF16),
            VMEM((2,) + wide, F32),
            VMEM((rows, width), BF16),
            VMEM((9, ch, ch), BF16),
            VMEM((9, ch, ch), BF16),
            VMEM((36, n_out, ch), BF16),
            VMEM((3, 3 * ch, ch), BF16),
            VMEM((2 * rows, width), BF16),
            VMEM((n_blk, 2 * rows, 2 * depth), BF16),
            VMEM((n_blk, 2 * depth, 2 * rows), BF16),
            VMEM((n_blk, 2 * depth, half), BF16),
            VMEM(wide, F32),
            VMEM((hidden, 2 * n_out), F32),
            VMEM((half, 2 * n_out), F32),
            VMEM((half, 2 * n_out), F32),
            VMEM((half, 2 * n_out), BF16),
            VMEM((3, half // 4, 2 * n_out), BF16),
            VMEM((2, half // 8, 2 * n_out), BF16),
            VMEM((3, half // 8, 2 * n_out), BF16),
            VMEM((half // 2, 2 * n_out), BF16),
            VMEM((token_rows, n_cols, n_out), F32),
            VMEM((2 * rows, half), F32),
            VMEM((2 * rows, half), BF16),
            VMEM((2, token_rows, n_cols, n_out), F32),
            VMEM((token_rows, n_cols, n_out), F32),
            VMEM((token_rows // 2, n_cols + 2 * EDGE, 2 * n_out), F32),
            VMEM((4, token_rows // 2, span, 2 * n_out), F32),
            VMEM((2, 4, 1, span, 2 * n_out), F32),
            pltpu.SemaphoreType.DMA((72,)),
            pltpu.SemaphoreType.DMA((72,)),
            pltpu.SemaphoreType.DMA((10,)),
        ],
        compiler_params=pltpu.CompilerParams(
            collective_id=1, has_side_effects=True, vmem_limit_bytes=60 * 2**20
        ),
    )(tokens, shift, scale, gate, projt, fc1, fc2t, lift, conv_a, conv_b, target)


def middle_kernel(
    sums, *refs,
):
    hbm, (latent, lg), refs = refs[:4], refs[4:6], refs[6:]
    kern, want, conv_b, conv_bt = refs[:4]
    patch, f_ref, a_ref, b_ref, acc, gf, send, recv, local = refs[4:]
    loads = [
        pltpu.make_async_copy(src, dst, local.at[i])
        for i, (src, dst) in enumerate(zip(hbm, refs))
    ]
    for load in loads:
        load.start()
    grp, seq, tile = lax.axis_index("grp"), lax.axis_index("seq"), lax.axis_index("tile")
    core = seq % 2

    def cores(k, dt):
        return (grp, seq - core + (core + k) % 2, (tile + dt) % 4)

    around = [(k, dt) for k in range(2) for dt in range(4) if (k, dt) != (0, 0)]
    announce([cores(k, dt) for k, dt in around])
    mail = Courier(send, recv)
    n_tok, span, width = sums.shape
    n_rows, here = n_tok - 2, span - 2 * EDGE
    pairs, ch = a_ref.shape[1], a_ref.shape[2] // 4

    rows = {r: sums[r] for r in range(n_tok)}
    height, breadth = f_ref.shape[0] - 8, 4 * here
    for r in range(n_tok):
        patch[0, r + 1] = pltpu.roll(rows[r], 1, 0).astype(BF16)
        patch[1, r + 1] = rows[r].astype(BF16)
        patch[2, r + 1] = pltpu.roll(rows[r], span - 1, 0).astype(BF16)
    for k in range(3):
        patch[k, 0] = jnp.zeros((span, width), BF16)
        patch[k, n_tok + 1] = jnp.zeros((span, width), BF16)

    loads[0].wait()

    def near(phase):
        return [(d, phase - 4 * d) for d in (-1, 0, 1) if -1 <= phase - 4 * d <= 4]

    for al in range(4):
        for ph in range(4):
            value = None
            for dr, r in near(al):
                for dc, c in near(ph):
                    lhs = patch[1 + dc, 1 + dr : 1 + dr + n_tok].reshape(n_tok * span, width)
                    term = dot(lhs, kern[6 * (r + 1) + c + 1])
                    value = term if value is None else value + term
            value = value.reshape(n_tok, span, ch)
            for tr in range(n_tok):
                at = pl.ds(ph // 2, span, stride=2)
                f_ref[4 * tr + al, ph % 2, 0, at, :] = value[tr, :, :128]
                f_ref[4 * tr + al, ph % 2, 1, at, :] = value[tr, :, 128:]

    first_pair = 2 * EDGE - PAIR_EDGE

    def inside(row, b):
        r = seq * height + row
        c = 2 * (tile * breadth // 2 + lax.broadcasted_iota(jnp.int32, (pairs, 1), 0) - PAIR_EDGE) + b
        return (r >= 0) & (r < 16 * height) & (c >= 0) & (c < 4 * breadth)

    def both(ref, at, rows):
        return jnp.concatenate([ref[*at, 0, rows, :], ref[*at, 1, rows, :]], axis=1)

    def spread(ref, at, v0, v1):
        ref[at, :, 0:ch] = pltpu.roll(v1, 1, 0).astype(BF16)
        ref[at, :, ch : 2 * ch] = v0.astype(BF16)
        ref[at, :, 2 * ch : 3 * ch] = v1.astype(BF16)
        ref[at, :, 3 * ch :] = pltpu.roll(v0, pairs - 1, 0).astype(BF16)

    @pl.loop(0, height + 6)
    def _(i):
        smooth = []
        for b in range(2):
            f = both(f_ref, (i + 1, b), slice(first_pair, first_pair + pairs))
            sigma = jax.nn.sigmoid(f)
            smooth.append(jnp.where(inside(i - 3, b), f * sigma, 0.0))
            slope = sigma * (1.0 + f * (1.0 - sigma))
            f_ref[i + 1, b, 0, first_pair : first_pair + pairs, :] = slope[:, :128]
            f_ref[i + 1, b, 1, first_pair : first_pair + pairs, :] = slope[:, 128:]
        spread(a_ref, i, *smooth)

    def conv(src, weights, out_rows, chunk):
        @pl.loop(0, out_rows // chunk)
        def _(i):
            for b in range(2):
                value = None
                for o in range(3):
                    lhs = src[pl.ds(i * chunk + o, chunk), :, b * ch : (b + 3) * ch]
                    term = dot(lhs.reshape(chunk * pairs, 3 * ch), weights[o])
                    value = term if value is None else value + term
                acc[b, pl.ds(i * chunk, chunk)] = value.reshape(chunk, pairs, ch)

    loads[2].wait()
    conv(a_ref, conv_b, height + 4, (height + 4) // 2)
    loads[1].wait()

    @pl.loop(0, height + 4)
    def _(i):
        grad = []
        for b in range(2):
            diff = acc[b, i] - both(want, (i,), pl.ds(LEAD - 2 * PAIR_EDGE + b, pairs, stride=2))
            grad.append(jnp.where(inside(i - 2, b), diff, 0.0))
        spread(b_ref, i, *grad)

    loads[3].wait()
    conv(b_ref, conv_bt, height + 2, (height + 2) // 2)

    @pl.loop(0, height + 2)
    def _(i):
        for b in range(2):
            value = acc[b, i] * both(f_ref, (i + 3, b), slice(first_pair, first_pair + pairs))
            value = jnp.where(inside(i - 1, b), value, 0.0)
            gf[i, b, 0], gf[i, b, 1] = value[:, :128], value[:, 128:]

    grad = None
    for r in range(-1, 5):
        for c in range(-1, 5):
            at = pl.ds(PAIR_EDGE + c // 2, here, stride=2)
            lhs = jnp.concatenate(
                [both(gf, (4 * tr + r + 1, c % 2), at).astype(BF16) for tr in range(n_rows)],
                axis=0,
            )
            term = dot(lhs, kern[6 * (r + 1) + c + 1], NT)
            grad = term if grad is None else grad + term
    grad = grad.reshape(n_rows, here, width)
    latent[...] = grad
    def part_of(k, dt):
        cols = pl.ds(pl.multiple_of((tile + dt) % 4 * here, 16), here)
        return lg.at[pl.ds((core + k) % 2 * n_rows, n_rows), cols]

    cols = pl.ds(pl.multiple_of(tile * here, 16), here)
    lg[pl.ds(core * n_rows, n_rows), cols, :] = grad.astype(BF16)
    await_peers(around)
    s_back = mail.slots(around)
    for k, dt in around:
        mail.start(s_back[k, dt], part_of(0, 0), part_of(0, 0), cores(k, dt))
    for k, dt in around:
        mail.arrived(s_back[k, dt], part_of(k, -dt), cores(k, -dt))
    mail.finish()


def middle(sums, kern, want, conv_b, conv_bt):
    n_tok, span, width = sums.shape
    n_rows, here = n_tok - 2, span - 2 * EDGE
    height, breadth, ch = want.shape[0] - 4, 4 * here, conv_bt.shape[2]
    pairs = breadth // 2 + 2 * PAIR_EDGE
    vmem, hbm = pl.BlockSpec(memory_space=VMEM), pl.BlockSpec(memory_space=pl.ANY)
    shape = jax.ShapeDtypeStruct
    loaded = (kern, want, conv_b, conv_bt)
    return pl.pallas_call(
        middle_kernel,
        out_shape=(
            shape((n_rows, here, width), F32),
            shape((2 * n_rows, 4 * here, width), BF16),
        ),
        in_specs=[vmem] + [hbm] * len(loaded),
        out_specs=(vmem,) * 2,
        scratch_shapes=[VMEM(x.shape, x.dtype) for x in loaded]
        + [
            VMEM((3, n_rows + 4, span, width), BF16),
            VMEM((height + 8, 2, 2, 2 * span, ch // 2), F32),
            VMEM((height + 6, pairs, 4 * ch), BF16),
            VMEM((height + 4, pairs, 4 * ch), BF16),
            VMEM((2, height + 4, pairs, ch), F32),
            VMEM((height + 2, 2, 2, pairs, ch // 2), F32),
            pltpu.SemaphoreType.DMA((16,)),
            pltpu.SemaphoreType.DMA((16,)),
            pltpu.SemaphoreType.DMA((len(loaded),)),
        ],
        compiler_params=pltpu.CompilerParams(
            collective_id=3, has_side_effects=True, vmem_limit_bytes=58 * 2**20
        ),
    )(sums, *loaded)


def backward_kernel(
    nrmt_hbm, slope_hbm, act_hbm, fold, lg, gboth, out, two,
    nrmt, slope, act, gpre, st, sz_in, sy_out, sy_in, sfull, b_out, b_in, a_out, a_in, fin, fin_in,
    send, recv, local,
):
    y, z, core, device = place()
    a, b, turn = oriented(y, z, core)
    grp = lax.axis_index("grp")
    other = 1 - core
    sibling = device(y, z, other)
    peers = (
        [sibling]
        + [device((y + d) % 4, z, core) for d in STEPS]
        + [device(y, (z + d) % 4, core) for d in STEPS]
    )
    announce(peers)
    loads = [
        pltpu.make_async_copy(src, dst, local.at[i])
        for i, (src, dst) in enumerate(
            ((act_hbm, act), (slope_hbm, slope), (nrmt_hbm, nrmt))
        )
    ]
    for load in loads:
        load.start()
    mail = Courier(send, recv)
    half = gpre.shape[1]
    rows = nrmt.shape[1] // 2

    def peer(da, db):
        return device(*turn((a + da) % 4, (b + db) % 4), core)

    def block(da, db):
        return block_of(*turn((a + da) % 4, (b + db) % 4))

    def term(da, db):
        return dot(nrmt[block(da, db)], gpre[...])

    s_b = mail.slots((da, d) for da in range(4) for d in STEPS)
    s_a = mail.slots(STEPS)

    def send_b(da):
        for d in (2, 1, 3):
            b_out[da, d - 1] = term(da, d).astype(BF16)
            mail.start(s_b[da, d], b_out.at[da, d - 1], b_in.at[da, d - 1], peer(0, d))

    def sum_b(da):
        total = term(da, 0)
        for d in STEPS:
            mail.arrived(s_b[da, d], b_in.at[da, d - 1], peer(0, -d))
            total = total + b_in[da, d - 1].astype(F32)
        return total

    def send_a(d):
        a_out[d - 1] = sum_b(d).astype(BF16)
        mail.start(s_a[d], a_out.at[d - 1], a_in.at[d - 1], peer(d, 0))

    loads[0].wait()
    st[...] = dot(lg[...], act[...], TN).astype(BF16)
    sq = st.shape[0] // 4
    s_sz, s_sy, s_sa = mail.slots(STEPS), mail.slots(STEPS), mail.slots(STEPS)
    await_peers(peers)
    for d in STEPS:
        to = (z + d) % 4
        src = st.at[pl.ds(pl.multiple_of(to * sq, 16), sq)]
        mail.start(s_sz[d], src, sz_in.at[d - 1], device(y, to, core))

    loads[1].wait()
    gpre[...] = (dot(lg[...], fold[...], NT) * slope[...]).astype(BF16)
    loads[2].wait()
    send_b(2)

    for d in STEPS:
        mail.arrived(s_sz[d], sz_in.at[d - 1], device(y, (z + 4 - d) % 4, core))
    s_at = pl.ds(pl.multiple_of(z * sq, 16), sq)
    total = st[s_at, :].astype(F32)
    for d in STEPS:
        total = total + sz_in[d - 1].astype(F32)
    sy_out[...] = total.astype(BF16)
    for d in STEPS:
        mail.start(s_sy[d], sy_out, sy_in.at[d - 1], device((y + d) % 4, z, core))

    send_b(1)
    for d in STEPS:
        mail.arrived(s_sy[d], sy_in.at[d - 1], device((y + 4 - d) % 4, z, core))
    sfull[core, grp, s_at] = (total + sy_in[1].astype(F32)).astype(BF16)
    sfull[core, 1 - grp, s_at] = (sy_in[0].astype(F32) + sy_in[2].astype(F32)).astype(BF16)
    for d in STEPS:
        ref = sfull.at[core, :, s_at]
        mail.start(s_sa[d], ref, ref, device(y, (z + d) % 4, core))
    send_b(3)
    send_b(0)

    send_a(2)
    for d in STEPS:
        frm = (z + 4 - d) % 4
        at = pl.ds(pl.multiple_of(frm * sq, 16), sq)
        mail.arrived(s_sa[d], sfull.at[core, :, at], device(y, frm, core))
    s_ss = mail.slot()
    mail.start(s_ss, sfull.at[core], sfull.at[core], sibling)
    send_a(1)
    send_a(3)

    mail.arrived(s_ss, sfull.at[other], sibling)
    g_high, g_low = split(gboth[...])
    for h in range(2):
        sums = sfull[h].reshape(-1, half)
        value = dot(g_high, sums) + dot(g_low, sums)
        two[:, h * half : (h + 1) * half] = value[: two.shape[0]]

    total = sum_b(0)
    for d in STEPS:
        mail.arrived(s_a[d], a_in.at[d - 1], peer(-d, 0))
        total = total + a_in[d - 1].astype(F32)
    fin[...] = total
    s_fin = mail.slot()
    theirs = pl.ds(pl.multiple_of(other * rows, 16), rows)
    mail.start(s_fin, fin.at[theirs], fin_in, sibling)
    here = out.shape[0]
    mine = fin[pl.ds(pl.multiple_of(core * rows, 16), rows), :]
    out[:, pl.ds(pl.multiple_of(core * half, 128), half)] = mine[:here]
    mail.arrived(s_fin, fin_in, sibling)
    out[:, pl.ds(pl.multiple_of(other * half, 128), half)] = fin_in[:here, :]
    mail.finish()


def backward(nrmt, slope, act, fold, lg, gboth, here):
    n_blk, depth, rows = nrmt.shape
    half = slope.shape[1]
    width = lg.shape[1]
    vmem, hbm = pl.BlockSpec(memory_space=VMEM), pl.BlockSpec(memory_space=pl.ANY)
    shape = jax.ShapeDtypeStruct
    return pl.pallas_call(
        backward_kernel,
        out_shape=(shape((here, 2 * half), F32), shape((here, 2 * half), F32)),
        in_specs=[hbm] * 3 + [vmem] * 3,
        out_specs=(vmem,) * 2,
        scratch_shapes=[
            VMEM(nrmt.shape, BF16),
            VMEM(slope.shape, F32),
            VMEM(act.shape, BF16),
            VMEM((rows, half), BF16),
            VMEM((width, half), BF16),
            VMEM((3, width // 4, half), BF16),
            VMEM((width // 4, half), BF16),
            VMEM((3, width // 4, half), BF16),
            VMEM((2, 2, width, half), BF16),
            VMEM((4, 3, depth, half), BF16),
            VMEM((4, 3, depth, half), BF16),
            VMEM((3, depth, half), BF16),
            VMEM((3, depth, half), BF16),
            VMEM((depth, half), F32),
            VMEM((depth // 2, half), F32),
            pltpu.SemaphoreType.DMA((32,)),
            pltpu.SemaphoreType.DMA((32,)),
            pltpu.SemaphoreType.DMA((3,)),
        ],
        compiler_params=pltpu.CompilerParams(
            collective_id=2, has_side_effects=True, vmem_limit_bytes=58 * 2**20
        ),
    )(nrmt, slope, act, fold, lg, gboth)


def leave_kernel(*refs):
    for src, dst in zip(refs[:3], refs[3:]):
        dst[...] = src[...]


def leave(*values):
    vmem = pl.BlockSpec(memory_space=VMEM)
    return pl.pallas_call(
        leave_kernel,
        out_shape=tuple(jax.ShapeDtypeStruct(v.shape, v.dtype) for v in values),
        in_specs=[vmem] * 3,
        out_specs=(vmem,) * 3,
    )(*values)


def shards(tokens, shift, scale, gate, fc1, fc2, proj, lift, conv_a, conv_b, target):
    width = tokens.shape[3]
    patch_width = proj.shape[1]

    cols_here = fc2.shape[1]
    ch = conv_a.shape[2]
    slope, act, sums, fold, gboth, nrmt, kern, conv_bt, want = forward(
        tokens[0].reshape(-1, width),
        shift,
        scale,
        gate,
        proj.T,
        fc1,
        fc2.T,
        lift,
        conv_a.reshape(9, ch, ch),
        conv_b.reshape(9, ch, ch),
        target[0],
    )
    latent_mine, latent_rows = middle(
        sums, kern, want, conv_b.reshape(3, 3 * ch, ch), conv_bt
    )
    latent_rows = latent_rows.reshape(-1, patch_width)
    grad_one, grad_two = backward(nrmt, slope, act, fold, latent_rows, gboth, cols_here)
    grad_one, grad_two, latent_mine = leave(grad_one, grad_two, latent_mine)
    return (grad_one, grad_two.T, latent_mine[None])


def solution(mesh):
    in_specs = (
        P("grp", "seq", None, None),
        P("grp", None),
        P("grp", None),
        P("grp", None),
        P(("grp", "seq"), "tile"),
        P("tile", ("grp", "seq")),
        P(),
        P(),
        P(),
        P(),
        P("grp", "seq", "tile", None),
    )
    out_specs = (
        P(("grp", "seq"), "tile"),
        P("tile", ("grp", "seq")),
        P("grp", "seq", "tile", None),
    )
    return jax.shard_map(shards, mesh=mesh, in_specs=in_specs, out_specs=out_specs, check_vma=False)
```
